32 devices in a mesh: fsdp: 8 (over z, y), tensor: 4 (over x, core).
Axes of the slice: x: 2, y: 2, z: 4, core: 2. Of those that a mesh axis runs over, the one named last changes fastest.
Arguments:
- block_input: float32 [1376, 8, 1024], P('tensor', 'fsdp'), may hold values from -30 to 30
- live_mask: int32 [1376, 8], P(None, 'fsdp'), may hold values from 0 to 1, as said below
- cotangent: float32 [1376, 8, 1024], P('tensor', 'fsdp'), may hold values from -6 to 6
- project_in: float32 [1024, 3, 1024], P('fsdp', None, 'tensor'), may hold values from -4 to 4
- project_out: float32 [1024, 1024], P('tensor', 'fsdp'), may hold values from -3 to 3
- expand: float32 [1024, 4096], P('fsdp', 'tensor'), may hold values from -0.1875 to 0.1875
- contract: float32 [4096, 1024], P('tensor', 'fsdp'), may hold values from -0.09375 to 0.09375
- vectors: float32 [10, 1024], P(None, 'fsdp'), may hold values from -2 to 2
- expand_bias: float32 [4096], P('fsdp'), may hold values from -1.8 to 1.8
- moment_project_in: float32 [1024, 3, 1024], P('fsdp', None, 'tensor'), may hold values from -112 to 112
- second_project_in: float32 [1024, 3, 1024], P('fsdp', None, 'tensor'), may hold values from 4.5 to 22.5
- moment_project_out: float32 [1024, 1024], P('tensor', 'fsdp'), may hold values from -6 to 6
- second_project_out: float32 [1024, 1024], P('tensor', 'fsdp'), may hold values from 0.02 to 0.1
- moment_expand: float32 [1024, 4096], P('fsdp', 'tensor'), may hold values from -40 to 40
- second_expand: float32 [1024, 4096], P('fsdp', 'tensor'), may hold values from 0.72 to 3.6
- moment_contract: float32 [4096, 1024], P('tensor', 'fsdp'), may hold values from -96 to 96
- second_contract: float32 [4096, 1024], P('tensor', 'fsdp'), may hold values from 3 to 15
- moment_vectors: float32 [10, 1024], P(None, 'fsdp'), may hold values from -128 to 128
- second_vectors: float32 [10, 1024], P(None, 'fsdp'), may hold values from 8 to 40
- moment_expand_bias: float32 [4096], P('fsdp'), may hold values from -40 to 40
- second_expand_bias: float32 [4096], P('fsdp'), may hold values from 0.72 to 3.6
Outputs:
- block_output: float32 [1376, 8, 1024], P('tensor', 'fsdp')
- input_grad: float32 [1376, 8, 1024], P('tensor', 'fsdp')
- grad_project_in: float32 [1024, 3, 1024], P('fsdp', None, 'tensor')
- grad_project_out: float32 [1024, 1024], P('tensor', 'fsdp')
- grad_expand: float32 [1024, 4096], P('fsdp', 'tensor')
- grad_contract: float32 [4096, 1024], P('tensor', 'fsdp')
- grad_vectors: float32 [10, 1024], P(None, 'fsdp')
- grad_expand_bias: float32 [4096], P('fsdp')
- new_project_in: float32 [1024, 3, 1024], P('fsdp', None, 'tensor')
- update_project_out: float32 [1024, 1024], P('tensor', 'fsdp')
- new_expand: float32 [1024, 4096], P('fsdp', 'tensor')
- new_contract: float32 [4096, 1024], P('tensor', 'fsdp')
- update_vectors: float32 [10, 1024], P(None, 'fsdp')
- update_expand_bias: float32 [4096], P('fsdp')
- new_moment_project_in: float32 [1024, 3, 1024], P('fsdp', None, 'tensor')
- new_second_project_in: float32 [1024, 3, 1024], P('fsdp', None, 'tensor')
- new_moment_project_out: float32 [1024, 1024], P('tensor', 'fsdp')
- new_second_project_out: float32 [1024, 1024], P('tensor', 'fsdp')
- new_moment_expand: float32 [1024, 4096], P('fsdp', 'tensor')
- new_second_expand: float32 [1024, 4096], P('fsdp', 'tensor')
- new_moment_contract: float32 [4096, 1024], P('tensor', 'fsdp')
- new_second_contract: float32 [4096, 1024], P('tensor', 'fsdp')
- new_moment_vectors: float32 [10, 1024], P(None, 'fsdp')
- new_second_vectors: float32 [10, 1024], P(None, 'fsdp')
- new_moment_expand_bias: float32 [4096], P('fsdp')
- new_second_expand_bias: float32 [4096], P('fsdp')
- shift_gradient: float32 [1024], P('fsdp')
The draws below stay inside these ranges and needn't reach their ends.
Inputs may be any that keep to these rules, and one draw needn't show every extreme that they name: `live_mask`: 1 marks a real token, 0 a pad token; in every image the pad tokens are its last 1 to 8 positions, and the first image has exactly 8.
All inputs are finite; a program needn't handle non-finite values.
Results may differ from the reference program's by a relative error of at most 0.023.
Values may be sent and summed in bfloat16 or wider, within the bound.
No kernel may reach another device: no remote copies, remote signals or barrier semaphores. Data moves between devices by JAX's collectives and lax.ppermute only.
A program may use at most 128 MiB of HBM per device.

```python
import math
import jax
import jax.numpy as jnp
from jax import lax

D = 1024
HEADS = 16
HEAD_DIM = 64
FF = 4096
SEQ = 1376
PAD_MOST = 8
STEP = 3
IMAGES = 8
N_TENSOR = 4


def draw_block_input(key, part):
    key = jax.random.fold_in(key, 11)
    key_base, key_rows, key_cols = jax.random.split(key, 3)
    row_scale = jnp.exp(jax.random.uniform(key_rows, (SEQ, IMAGES, 1), jnp.float32, math.log(0.3), math.log(3.0)))
    col_scale = jnp.exp(jax.random.uniform(key_cols, (1, 1, D), jnp.float32, math.log(0.5), math.log(2.0)))
    base = jnp.clip(jax.random.normal(key_base, (SEQ, IMAGES, D), jnp.float32), -5.0, 5.0)
    return jnp.clip(base * row_scale * col_scale, -30.0, 30.0)


def draw_project_in(key, part):
    key = jax.random.fold_in(key, 23)
    key_base = jax.random.fold_in(key, 0)
    base = jnp.clip(jax.random.normal(key_base, (D, 3, D), jnp.float32), -6.0, 6.0) / math.sqrt(D)
    return jnp.clip(base, -4.0, 4.0)


def draw_vectors(key, part):
    key = jax.random.fold_in(key, 37)
    offsets = jnp.array([1.0, 0.0, 0.0, 0.0, 0.0, 0.6, 1.0, 0.0, 0.0, 0.6], jnp.float32)[:, None]
    spreads = jnp.array([0.15, 0.3, 0.02, 0.02, 0.3, 0.2, 0.15, 0.3, 0.3, 0.2], jnp.float32)[:, None]
    noise = jax.random.normal(key, (10, D), jnp.float32)
    return jnp.clip(offsets + spreads * noise, -2.0, 2.0)


def draw_live_mask(key, part):
    key = jax.random.fold_in(key, 53)
    pads = jax.random.randint(key, (IMAGES,), 1, PAD_MOST + 1)
    pads = jnp.where(jnp.arange(IMAGES) == 0, PAD_MOST, pads)
    return (jnp.arange(SEQ)[:, None] < (SEQ - pads)[None, :]).astype(jnp.int32)


def levels(key, dims, shards, least, high):
    def one(position, parts):
        steps = jax.random.uniform(jax.random.fold_in(jax.random.fold_in(key, 6), position), (parts,), jnp.float32, least / len(shards), high / len(shards))
        return jnp.repeat(jnp.exp(steps), dims[position] // parts).reshape((-1,) + (1,) * (len(dims) - position - 1))

    level = one(*shards[0])
    for cut in shards[1:]:
        level = level * one(*cut)
    return level


def gaussian(key, shape, scale, bound, shards=(), held_as=jnp.bfloat16):
    loudness = levels(key, shape, shards, -0.22, 0.18) if shards else 1.0
    values = jax.random.normal(key, shape, jnp.float32) * scale * loudness
    return jnp.minimum(jnp.maximum(values, -bound), bound).astype(held_as)


def setup_inputs(seed: int = 0) -> dict:
    key_of = jax.random.split(jax.random.key(seed), 22)
    block_input = draw_block_input(jax.random.fold_in(key_of[21], 71), 0)
    live_mask = draw_live_mask(jax.random.fold_in(key_of[21], 71), 0)
    cotangent = gaussian(key_of[2], (SEQ, IMAGES, D), 1.0, 6.0, ((0, 4), (1, 8)), jnp.float32)
    project_in = draw_project_in(jax.random.fold_in(key_of[21], 71), 0)
    project_out = gaussian(key_of[4], (D, D), (max(1, D // 256)) ** -0.5, 3.0, ((0, 4), (1, 8)), jnp.float32)
    expand = gaussian(key_of[5], (D, FF), D ** -0.5, 0.1875, ((0, 8), (1, 4)), jnp.float32)
    contract = gaussian(key_of[6], (FF, D), FF ** -0.5, 0.09375, ((0, 4), (1, 8)), jnp.float32)
    vectors = draw_vectors(jax.random.fold_in(key_of[21], 71), 0)
    expand_bias = gaussian(key_of[8], (FF,), 0.3, 1.8, ((0, 8),), jnp.float32)
    moment_project_in = gaussian(key_of[9], (D, 3, D), 18.0, 112.0, ((0, 8), (2, 4)), jnp.float32)
    second_project_in = jnp.clip(jnp.exp(math.log(22.5) - 1.609438 * jax.random.uniform(key_of[10], (D, 3, D), jnp.float32) ** levels(key_of[10], (D, 3, D), ((0, 8), (2, 4)), -0.2, 0.2)), 4.5, 22.5)
    moment_project_out = gaussian(key_of[11], (D, D), 1.2, 6.0, ((0, 4), (1, 8)), jnp.float32)
    second_project_out = jnp.clip(jnp.exp(math.log(0.1) - 1.609438 * jax.random.uniform(key_of[12], (D, D), jnp.float32) ** levels(key_of[12], (D, D), ((0, 4), (1, 8)), -0.2, 0.2)), 0.02, 0.1)
    moment_expand = gaussian(key_of[13], (D, FF), 7.0, 40.0, ((0, 8), (1, 4)), jnp.float32)
    second_expand = jnp.clip(jnp.exp(math.log(3.6) - 1.6094378 * jax.random.uniform(key_of[14], (D, FF), jnp.float32) ** levels(key_of[14], (D, FF), ((0, 8), (1, 4)), -0.2, 0.2)), 0.72, 3.6)
    moment_contract = gaussian(key_of[15], (FF, D), 15.0, 96.0, ((0, 4), (1, 8)), jnp.float32)
    second_contract = jnp.clip(jnp.exp(math.log(15.0) - 1.609438 * jax.random.uniform(key_of[16], (FF, D), jnp.float32) ** levels(key_of[16], (FF, D), ((0, 4), (1, 8)), -0.2, 0.2)), 3.0, 15.0)
    moment_vectors = gaussian(key_of[17], (10, D), 20.0, 128.0, ((1, 8),), jnp.float32)
    second_vectors = jnp.clip(jnp.exp(math.log(40.0) - 1.609438 * jax.random.uniform(key_of[18], (10, D), jnp.float32) ** levels(key_of[18], (10, D), ((1, 8),), -0.2, 0.2)), 8.0, 40.0)
    moment_expand_bias = gaussian(key_of[19], (FF,), 7.0, 40.0, ((0, 8),), jnp.float32)
    second_expand_bias = jnp.clip(jnp.exp(math.log(3.6) - 1.6094378 * jax.random.uniform(key_of[20], (FF,), jnp.float32) ** levels(key_of[20], (FF,), ((0, 8),), -0.2, 0.2)), 0.72, 3.6)
    return dict(block_input=block_input, live_mask=live_mask, cotangent=cotangent, project_in=project_in, project_out=project_out, expand=expand, contract=contract, vectors=vectors, expand_bias=expand_bias, moment_project_in=moment_project_in, second_project_in=second_project_in, moment_project_out=moment_project_out, second_project_out=second_project_out, moment_expand=moment_expand, second_expand=second_expand, moment_contract=moment_contract, second_contract=second_contract, moment_vectors=moment_vectors, second_vectors=second_vectors, moment_expand_bias=moment_expand_bias, second_expand_bias=second_expand_bias)


NORM_EPS = 1e-06
BETA_FIRST = 0.9
BETA_SECOND = 0.999
LEARN_RATE = 0.004
WEIGHT_DECAY = 0.04
ADAM_EPS = 1e-08
MASKED_SCORE = -1e+30
ROOT_HALF = 0.7071067811865476
DENSITY_NORM = 0.3989422804014327

def norm_forward(values, norm_gain, norm_shift):
    center = lax.optimization_barrier(jnp.mean(values, axis=-1, keepdims=True))
    offset = values - center
    spread = lax.optimization_barrier(jnp.mean(offset * offset, axis=-1, keepdims=True))
    inverse = lax.rsqrt(spread + NORM_EPS)
    scaled = offset * inverse
    return (scaled, inverse, scaled * norm_gain + norm_shift)

def norm_backward(scaled, inverse, grad_normed, norm_gain):
    grad_scaled = grad_normed * norm_gain
    first_mean = lax.optimization_barrier(jnp.mean(grad_scaled, axis=-1, keepdims=True))
    second_mean = lax.optimization_barrier(jnp.mean(grad_scaled * scaled, axis=-1, keepdims=True))
    return inverse * (grad_scaled - first_mean - scaled * second_mean)

def gelu_parts(hidden):
    normal_cdf = 0.5 * (1.0 + lax.erf(hidden * ROOT_HALF))
    density = DENSITY_NORM * jnp.exp(-0.5 * hidden * hidden)
    return (hidden * normal_cdf, normal_cdf + hidden * density)

def head_scores(queries, key_rows, usable):
    scores = jnp.dot(queries, key_rows.T, preferred_element_type=jnp.float32) * HEAD_DIM ** (-0.5)
    return jnp.where(usable[None, :], scores, MASKED_SCORE)

def head_forward(inputs):
    queries, key_rows, value_rows, usable = inputs
    scores = head_scores(queries, key_rows, usable)
    highest = lax.optimization_barrier(jnp.max(scores, axis=-1, keepdims=True))
    summed = lax.optimization_barrier(jnp.sum(jnp.exp(scores - highest), axis=-1, keepdims=True))
    log_total = highest + jnp.log(summed)
    weights = jnp.exp(scores - log_total).astype(jnp.bfloat16)
    output = jnp.dot(weights, value_rows, preferred_element_type=jnp.float32)
    return (output.astype(jnp.bfloat16), log_total[:, 0])

def head_backward(inputs):
    queries, key_rows, value_rows, usable, log_total, grad_output = inputs
    scores = head_scores(queries, key_rows, usable)
    weights = jnp.exp(scores - log_total[:, None])
    grad_values = jnp.dot(weights.astype(jnp.bfloat16).T, grad_output, preferred_element_type=jnp.float32)
    grad_weights = jnp.dot(grad_output, value_rows.T, preferred_element_type=jnp.float32)
    row_inner = lax.optimization_barrier(jnp.sum(weights * grad_weights, axis=-1, keepdims=True))
    grad_scores = (weights * (grad_weights - row_inner)).astype(jnp.bfloat16)
    score_scale = HEAD_DIM ** (-0.5)
    grad_queries = jnp.dot(grad_scores, key_rows, preferred_element_type=jnp.float32) * score_scale
    grad_keys = jnp.dot(grad_scores.T, queries, preferred_element_type=jnp.float32) * score_scale
    return (grad_queries.astype(jnp.bfloat16), grad_keys.astype(jnp.bfloat16), grad_values.astype(jnp.bfloat16))

def to_heads(flat_rows):
    return flat_rows.reshape(SEQ, HEADS, HEAD_DIM).transpose(1, 0, 2)

def from_heads(stacked):
    return stacked.transpose(1, 0, 2).reshape(SEQ, HEADS * HEAD_DIM)

def grouped_forward(attended, copy_out):
    group_width = attended.shape[1] // N_TENSOR
    summed = jnp.zeros((attended.shape[0], copy_out.shape[1]), jnp.float32)
    for group_index in range(N_TENSOR):
        low_col = group_index * group_width
        partial_value = jnp.dot(attended[:, low_col:low_col + group_width], copy_out[low_col:low_col + group_width], preferred_element_type=jnp.float32)
        rounded = lax.optimization_barrier(partial_value.astype(jnp.bfloat16))
        summed = summed + rounded.astype(jnp.float32)
    return summed

def grouped_backward(grad_mixed, copy_in):
    group_width = grad_mixed.shape[2] // N_TENSOR
    summed = jnp.zeros((grad_mixed.shape[0], copy_in.shape[0]), jnp.float32)
    for group_index in range(N_TENSOR):
        low_col = group_index * group_width
        partial_value = jnp.einsum('sce,dce->sd', grad_mixed[:, :, low_col:low_col + group_width].astype(jnp.float32), copy_in[:, :, low_col:low_col + group_width].astype(jnp.float32))
        rounded = lax.optimization_barrier(partial_value.astype(jnp.bfloat16))
        summed = summed + rounded.astype(jnp.float32)
    return summed

def image_pass(copies, image_input, image_live, image_cot):
    copy_in, copy_out, copy_expand, copy_contract, rows_now, bias_now = copies
    usable = image_live > 0
    scaled_one, inverse_one, normed = norm_forward(image_input, rows_now[0], rows_now[1])
    normed_one = normed.astype(jnp.bfloat16)
    bias_rows = jnp.stack([rows_now[2], jnp.zeros_like(rows_now[2]), rows_now[3]])
    mixed = jnp.einsum('sd,dce->sce', normed_one.astype(jnp.float32), copy_in.astype(jnp.float32))
    mixed = (mixed + bias_rows[None]).astype(jnp.bfloat16)
    queries = to_heads(mixed[:, 0])
    key_rows = to_heads(mixed[:, 1])
    value_rows = to_heads(mixed[:, 2])
    key_usable = jnp.broadcast_to(usable, (HEADS, SEQ))
    outputs, log_totals = lax.map(head_forward, (queries, key_rows, value_rows, key_usable))
    attended = from_heads(outputs)
    attn_sum = grouped_forward(attended, copy_out) + rows_now[4]
    residual = image_input + rows_now[5] * attn_sum
    scaled_two, inverse_two, normed = norm_forward(residual, rows_now[6], rows_now[7])
    normed_two = normed.astype(jnp.bfloat16)
    hidden = jnp.dot(normed_two, copy_expand, preferred_element_type=jnp.float32) + bias_now
    activated, slope = gelu_parts(hidden)
    activated = activated.astype(jnp.bfloat16)
    branch = jnp.dot(activated, copy_contract, preferred_element_type=jnp.float32) + rows_now[8]
    block_output = residual + rows_now[9] * branch
    grad_top = image_cot * usable[:, None].astype(jnp.float32)
    grad_scale_two = lax.optimization_barrier(jnp.sum(grad_top * branch, axis=0))
    grad_down_bias = lax.optimization_barrier(jnp.sum(grad_top * rows_now[9], axis=0))
    grad_branch = (grad_top * rows_now[9]).astype(jnp.bfloat16)
    grad_contract = jnp.dot(activated.T, grad_branch, preferred_element_type=jnp.float32)
    grad_act = jnp.dot(grad_branch, copy_contract.T, preferred_element_type=jnp.float32)
    grad_hidden = (grad_act * slope).astype(jnp.bfloat16)
    grad_expand = jnp.dot(normed_two.T, grad_hidden, preferred_element_type=jnp.float32)
    grad_expand_bias = lax.optimization_barrier(jnp.sum(grad_hidden.astype(jnp.float32), axis=0))
    grad_normed_two = jnp.dot(grad_hidden, copy_expand.T, preferred_element_type=jnp.float32)
    grad_gain_two = lax.optimization_barrier(jnp.sum(grad_normed_two * scaled_two, axis=0))
    grad_shift_two = lax.optimization_barrier(jnp.sum(grad_normed_two, axis=0))
    grad_residual = grad_top + norm_backward(scaled_two, inverse_two, grad_normed_two, rows_now[6])
    grad_scale_one = lax.optimization_barrier(jnp.sum(grad_residual * attn_sum, axis=0))
    grad_out_bias = lax.optimization_barrier(jnp.sum(grad_residual * rows_now[5], axis=0))
    grad_attn = (grad_residual * rows_now[5]).astype(jnp.bfloat16)
    grad_project_out = jnp.dot(attended.T, grad_attn, preferred_element_type=jnp.float32)
    grad_attended = jnp.dot(grad_attn, copy_out.T, preferred_element_type=jnp.float32).astype(jnp.bfloat16)
    grad_heads = lax.map(head_backward, (queries, key_rows, value_rows, key_usable, log_totals, to_heads(grad_attended)))
    grad_mixed = jnp.stack([from_heads(grad_part) for grad_part in grad_heads], axis=1)
    grad_project_in = jnp.einsum('sd,sce->dce', normed_one.astype(jnp.float32), grad_mixed.astype(jnp.float32))
    bias_sums = lax.optimization_barrier(jnp.sum(grad_mixed.astype(jnp.float32), axis=0))
    grad_normed_one = grouped_backward(grad_mixed, copy_in)
    grad_gain_one = lax.optimization_barrier(jnp.sum(grad_normed_one * scaled_one, axis=0))
    grad_shift_one = lax.optimization_barrier(jnp.sum(grad_normed_one, axis=0))
    input_grad = grad_residual + norm_backward(scaled_one, inverse_one, grad_normed_one, rows_now[0])
    grad_rows = jnp.stack([grad_gain_one, grad_shift_one, bias_sums[0], bias_sums[2], grad_out_bias, grad_scale_one, grad_gain_two, grad_shift_two, grad_down_bias, grad_scale_two])
    grads = (grad_project_in, grad_project_out, grad_expand, grad_contract, grad_rows, grad_expand_bias)
    return (block_output, input_grad, grads)

def adam_step(master, gradient, first, second, decay):
    first_new = BETA_FIRST * first + (1.0 - BETA_FIRST) * gradient
    second_new = BETA_SECOND * second + (1.0 - BETA_SECOND) * gradient * gradient
    first_hat = first_new / (1.0 - BETA_FIRST ** STEP)
    second_hat = second_new / (1.0 - BETA_SECOND ** STEP)
    change = -LEARN_RATE * (first_hat / (jnp.sqrt(second_hat) + ADAM_EPS) + decay * master)
    return (change, first_new, second_new)

def reference(block_input, live_mask, cotangent, project_in, project_out, expand, contract, vectors, expand_bias, moment_project_in, second_project_in, moment_project_out, second_project_out, moment_expand, second_expand, moment_contract, second_contract, moment_vectors, second_vectors, moment_expand_bias, second_expand_bias):
    rows_now = lax.optimization_barrier(vectors.astype(jnp.bfloat16)).astype(jnp.float32)
    bias_now = lax.optimization_barrier(expand_bias.astype(jnp.bfloat16)).astype(jnp.float32)
    copies = (project_in.astype(jnp.bfloat16), project_out.astype(jnp.bfloat16), expand.astype(jnp.bfloat16), contract.astype(jnp.bfloat16), rows_now, bias_now)
    masters = (project_in, project_out, expand, contract, vectors, expand_bias)
    initial = tuple((jnp.zeros(master.shape, jnp.float32) for master in masters))
    by_image = (jnp.moveaxis(block_input, 1, 0), jnp.moveaxis(live_mask, 1, 0), jnp.moveaxis(cotangent, 1, 0))

    def per_image(running, inputs):
        image_input, image_live, image_cot = inputs
        image_output, image_grad, grads = image_pass(copies, image_input, image_live, image_cot)
        return (tuple((left + right for left, right in zip(running, grads))), (image_output, image_grad))
    totals, (outputs, input_grads) = lax.scan(per_image, initial, by_image)
    firsts = (moment_project_in, moment_project_out, moment_expand, moment_contract, moment_vectors, moment_expand_bias)
    seconds = (second_project_in, second_project_out, second_expand, second_contract, second_vectors, second_expand_bias)
    decays = (WEIGHT_DECAY, WEIGHT_DECAY, WEIGHT_DECAY, WEIGHT_DECAY, 0.0, 0.0)
    results = [adam_step(masters[index], totals[index], firsts[index], seconds[index], decays[index]) for index in range(6)]
    changes = tuple((result[0] for result in results))
    moments = []
    for result in results:
        moments.append(result[1])
        moments.append(result[2])
    return (jnp.moveaxis(outputs, 0, 1), jnp.moveaxis(input_grads, 0, 1), totals[0], totals[1], totals[2], totals[3], totals[4], totals[5], masters[0] + changes[0], changes[1], masters[2] + changes[2], masters[3] + changes[3], changes[4], changes[5], moments[0], moments[1], moments[2], moments[3], moments[4], moments[5], moments[6], moments[7], moments[8], moments[9], moments[10], moments[11], totals[4][7])
```

```python
import functools

import jax
import jax.numpy as jnp
from jax import lax
from jax.experimental import pallas as pl
from jax.experimental.pallas import tpu as pltpu
from jax.sharding import PartitionSpec as P

HEAD_DIM = 64
STEP = 3
NORM_EPS = 1e-06
BETA_FIRST = 0.9
BETA_SECOND = 0.999
LEARN_RATE = 0.004
WEIGHT_DECAY = 0.04
ADAM_EPS = 1e-08
MASKED_SCORE = -1e30
ROOT_HALF = 0.7071067811865476
DENSITY_NORM = 0.3989422804014327
SCORE_SCALE = HEAD_DIM ** (-0.5)
LANES = 128
TILE = 352
VMEM_LIMIT = 56 * 2**20
F32 = jnp.float32
BF16 = jnp.bfloat16


def dot_nn(left, right):
    return lax.dot_general(left, right, (((1,), (0,)), ((), ())), preferred_element_type=F32)


def dot_nt(left, right):
    return lax.dot_general(left, right, (((1,), (1,)), ((), ())), preferred_element_type=F32)


def dot_tn(left, right):
    return lax.dot_general(left, right, (((0,), (0,)), ((), ())), preferred_element_type=F32)


def tiles_of(total, tile):
    return [(low, min(tile, total - low)) for low in range(0, total, tile)]


def norm_forward(values):
    center = jnp.mean(values, axis=-1, keepdims=True)
    offset = values - center
    spread = jnp.mean(offset * offset, axis=-1, keepdims=True)
    inverse = lax.rsqrt(spread + NORM_EPS)
    return offset * inverse, inverse


def norm_backward(scaled, inverse, grad_normed, norm_gain):
    grad_scaled = grad_normed * norm_gain
    first_mean = jnp.mean(grad_scaled, axis=-1, keepdims=True)
    second_mean = jnp.mean(grad_scaled * scaled, axis=-1, keepdims=True)
    return inverse * (grad_scaled - first_mean - scaled * second_mean)


def gelu_parts(hidden):
    normal_cdf = 0.5 * (1.0 + lax.erf(hidden * ROOT_HALF))
    density = DENSITY_NORM * jnp.exp(-0.5 * hidden * hidden)
    return (hidden * normal_cdf, normal_cdf + hidden * density)


def project_kernel(x_ref, rows_ref, weight_ref, bias_ref, normed_ref, qkv_ref):
    for low, count in tiles_of(x_ref.shape[0], TILE):
        at = slice(low, low + count)
        scaled, _ = norm_forward(x_ref[at, :].astype(F32))
        normed = (scaled * rows_ref[0:1, :] + rows_ref[1:2, :]).astype(BF16)
        normed_ref[at, :] = normed
        qkv_ref[at, :] = (dot_nn(normed, weight_ref[...]) + bias_ref[...]).astype(BF16)


def project(x_full, rows, weight, bias):
    seq, features = x_full.shape
    width = weight.shape[1]
    block = seq // 2
    return pl.pallas_call(
        project_kernel,
        grid=(2,),
        in_specs=[
            pl.BlockSpec((block, features), lambda i: (i, 0)),
            pl.BlockSpec(rows.shape, lambda i: (0, 0)),
            pl.BlockSpec(weight.shape, lambda i: (0, 0)),
            pl.BlockSpec(bias.shape, lambda i: (0, 0)),
        ],
        out_specs=[
            pl.BlockSpec((block, features), lambda i: (i, 0)),
            pl.BlockSpec((block, width), lambda i: (i, 0)),
        ],
        out_shape=[
            jax.ShapeDtypeStruct((seq, features), BF16),
            jax.ShapeDtypeStruct((seq, width), BF16),
        ],
        compiler_params=pltpu.CompilerParams(vmem_limit_bytes=VMEM_LIMIT),
        cost_estimate=pl.CostEstimate(
            flops=2 * seq * features * width,
            bytes_accessed=2 * (2 * seq * features + features * width + seq * width),
            transcendentals=0,
        ),
        name="project",
    )(x_full, rows, weight, bias)


def attend_kernel(live_ref, qkv_ref, attended_ref, query_ref, key_ref, value_ref):
    seq = qkv_ref.shape[0]
    lane = lax.broadcasted_iota(jnp.int32, (seq, LANES), 1)
    bias = jnp.where(live_ref[...] > 0, 0.0, MASKED_SCORE).astype(F32)
    key_rows = qkv_ref[:, LANES : 2 * LANES].astype(F32)
    value_rows = qkv_ref[:, 2 * LANES : 3 * LANES].astype(F32)
    for head in range(2):
        own = (lane // HEAD_DIM) == head
        spare = HEAD_DIM * (1 - head)
        extra = jnp.where(lane == spare, bias, 0.0)
        key_ref[head] = jnp.where(own, key_rows, extra).astype(BF16)
        extra = jnp.where(lane == spare, 1.0, 0.0)
        value_ref[head] = jnp.where(own, value_rows, extra).astype(BF16)
    for low, count in tiles_of(seq, TILE):
        at = slice(low, low + count)
        lane = lax.broadcasted_iota(jnp.int32, (count, LANES), 1)
        queries = qkv_ref[at, 0:LANES].astype(F32) * SCORE_SCALE
        both = None
        for head in range(2):
            own = (lane // HEAD_DIM) == head
            spare = HEAD_DIM * (1 - head)
            extra = jnp.where(lane == spare, 1.0, 0.0)
            mine = jnp.where(own, queries, extra).astype(BF16)
            scores = dot_nt(mine, key_ref[head])
            highest = jnp.max(scores, axis=-1, keepdims=True)
            weights = jnp.exp(scores - highest).astype(BF16)
            output = dot_nn(weights, value_ref[head])
            summed = output[:, spare : spare + 1]
            output = output / summed
            both = output if head == 0 else jnp.where(own, output, both)
            rest = -(highest + jnp.log(summed))
            extra = jnp.where(lane == spare + 3, 1.0, 0.0)
            for place in range(3):
                part = rest.astype(BF16).astype(F32)
                extra = jnp.where(lane == spare + place, part, extra)
                rest = rest - part
            query_ref[at, LANES * head : LANES * (head + 1)] = jnp.where(
                own, queries, extra
            ).astype(BF16)
        attended_ref[at, :] = both.astype(BF16)


def attend(live, qkv):
    seq = qkv.shape[0]
    pairs = qkv.shape[1] // (3 * LANES)
    return pl.pallas_call(
        attend_kernel,
        grid=(pairs,),
        in_specs=[
            pl.BlockSpec((seq, 1), lambda p: (0, 0)),
            pl.BlockSpec((seq, 3 * LANES), lambda p: (0, p)),
        ],
        out_specs=[
            pl.BlockSpec((seq, LANES), lambda p: (0, p)),
            pl.BlockSpec((seq, 2 * LANES), lambda p: (0, p)),
        ],
        out_shape=[
            jax.ShapeDtypeStruct((seq, pairs * LANES), BF16),
            jax.ShapeDtypeStruct((seq, pairs * 2 * LANES), BF16),
        ],
        scratch_shapes=[pltpu.VMEM((2, seq, LANES), BF16), pltpu.VMEM((2, seq, LANES), BF16)],
        compiler_params=pltpu.CompilerParams(vmem_limit_bytes=VMEM_LIMIT),
        cost_estimate=pl.CostEstimate(
            flops=pairs * 32 * seq * seq * HEAD_DIM,
            bytes_accessed=seq * pairs * 768 * 2,
            transcendentals=pairs * 2 * seq * seq,
        ),
        name="attend",
    )(live, qkv)


def attend_back_kernel(
    live_ref, qkv_ref, query_ref, attended_ref, grad_ref, out_ref, sums_ref, held_ref, query_sum_ref
):
    seq = qkv_ref.shape[0]
    lane = lax.broadcasted_iota(jnp.int32, (seq, LANES), 1)
    grad = grad_ref[...].astype(F32)
    product = grad * attended_ref[...].astype(F32)
    for head in range(2):
        own = (lane // HEAD_DIM) == head
        spare = HEAD_DIM * (1 - head)
        inner = -jnp.sum(jnp.where(own, product, 0.0), axis=-1, keepdims=True)
        first = inner.astype(BF16).astype(F32)
        extra = jnp.where(lane == spare, first, jnp.where(lane == spare + 1, inner - first, 0.0))
        held_ref[head] = jnp.where(own, grad, extra).astype(BF16)
    value_sum = jnp.zeros((1, LANES), F32)
    for index, (low, count) in enumerate(tiles_of(seq, TILE)):
        at = slice(low, low + count)
        lane = lax.broadcasted_iota(jnp.int32, (count, LANES), 1)
        bias = jnp.where(live_ref[at, :] > 0, 0.0, MASKED_SCORE).astype(F32)
        key_rows = qkv_ref[at, LANES : 2 * LANES].astype(F32)
        value_rows = qkv_ref[at, 2 * LANES : 3 * LANES].astype(F32)
        grad_keys = grad_values = None
        for head in range(2):
            own = (lane // HEAD_DIM) == head
            spare = HEAD_DIM * (1 - head)
            ones = jnp.where((lane >= spare) & (lane < spare + 3), 1.0, 0.0)
            extra = jnp.where(lane == spare + 3, bias, ones)
            keys = jnp.where(own, key_rows, extra).astype(BF16)
            values = jnp.where(own, value_rows, ones).astype(BF16)
            queries = query_ref[:, LANES * head : LANES * (head + 1)]
            above = held_ref[head]
            weights = jnp.exp(dot_nt(keys, queries))
            grad_scores = (weights * dot_nt(values, above)).astype(BF16)
            value_part = dot_nn(weights.astype(BF16), above)
            key_part = dot_nn(grad_scores, queries)
            query_part = dot_tn(keys, grad_scores)[HEAD_DIM * head : HEAD_DIM * (head + 1)]
            rows = slice(HEAD_DIM * head, HEAD_DIM * (head + 1))
            if index == 0:
                query_sum_ref[rows] = query_part
            else:
                query_sum_ref[rows] += query_part
            grad_keys = key_part if head == 0 else jnp.where(own, key_part, grad_keys)
            grad_values = value_part if head == 0 else jnp.where(own, value_part, grad_values)
        grad_values = grad_values.astype(BF16)
        out_ref[at, LANES : 2 * LANES] = grad_keys.astype(BF16)
        out_ref[at, 2 * LANES : 3 * LANES] = grad_values
        value_sum += jnp.sum(grad_values.astype(F32), axis=0, keepdims=True)
    grad_queries = (query_sum_ref[...].T * SCORE_SCALE).astype(BF16)
    out_ref[:, 0:LANES] = grad_queries
    sums_ref[0:1, :] = jnp.sum(grad_queries.astype(F32), axis=0, keepdims=True)
    sums_ref[1:2, :] = value_sum


def attend_back(live, qkv, queries, attended, grad):
    seq = qkv.shape[0]
    pairs = qkv.shape[1] // (3 * LANES)
    return pl.pallas_call(
        attend_back_kernel,
        grid=(pairs,),
        in_specs=[
            pl.BlockSpec((seq, 1), lambda p: (0, 0)),
            pl.BlockSpec((seq, 3 * LANES), lambda p: (0, p)),
            pl.BlockSpec((seq, 2 * LANES), lambda p: (0, p)),
            pl.BlockSpec((seq, LANES), lambda p: (0, p)),
            pl.BlockSpec((seq, LANES), lambda p: (0, p)),
        ],
        out_specs=[
            pl.BlockSpec((seq, 3 * LANES), lambda p: (0, p)),
            pl.BlockSpec((8, LANES), lambda p: (0, p)),
        ],
        out_shape=[
            jax.ShapeDtypeStruct((seq, pairs * 3 * LANES), BF16),
            jax.ShapeDtypeStruct((8, pairs * LANES), F32),
        ],
        scratch_shapes=[pltpu.VMEM((2, seq, LANES), BF16), pltpu.VMEM((LANES, seq), F32)],
        compiler_params=pltpu.CompilerParams(vmem_limit_bytes=VMEM_LIMIT),
        cost_estimate=pl.CostEstimate(
            flops=pairs * 80 * seq * seq * HEAD_DIM,
            bytes_accessed=seq * pairs * 1280 * 2,
            transcendentals=pairs * 2 * seq * seq,
        ),
        name="attend_back",
    )(live, qkv, queries, attended, grad)


def middle_kernel(
    x_ref,
    att_a,
    att_b,
    att_c,
    att_d,
    out_a,
    out_b,
    out_c,
    out_d,
    rows_ref,
    expand_ref,
    contract_ref,
    bias_ref,
    top_ref,
    attn_ref,
    normed_ref,
    act_ref,
    hidden_ref,
    grad_ref,
    branch_ref,
    back_ref,
    sums_ref,
):
    @pl.when(pl.program_id(0) == 0)
    def _():
        sums_ref[...] = jnp.zeros_like(sums_ref)

    pieces = ((att_a, out_a), (att_b, out_b), (att_c, out_c), (att_d, out_d))
    for low, count in tiles_of(x_ref.shape[0], TILE):
        at = slice(low, low + count)
        attn_sum = rows_ref[4:5, :]
        for att_ref, out_ref in pieces:
            attn_sum = attn_sum + dot_nt(att_ref[at, :], out_ref[...])
        attn_ref[at, :] = attn_sum
        residual = x_ref[at, :].astype(F32) + rows_ref[5:6, :] * attn_sum
        scaled, _ = norm_forward(residual)
        normed = (scaled * rows_ref[6:7, :] + rows_ref[7:8, :]).astype(BF16)
        normed_ref[at, :] = normed
        activated, slope = gelu_parts(dot_nn(normed, expand_ref[...]) + bias_ref[...])
        activated = activated.astype(BF16)
        act_ref[at, :] = activated
        grad_branch = (top_ref[at, :].astype(F32) * rows_ref[9:10, :]).astype(BF16)
        grad_ref[at, :] = grad_branch
        grad_hidden = (dot_nn(grad_branch, contract_ref[...]) * slope).astype(BF16)
        hidden_ref[at, :] = grad_hidden
        branch_ref[at, :] = dot_nt(activated, contract_ref[...]).astype(BF16)
        back = dot_nt(grad_hidden, expand_ref[...])
        back_ref[at, :] = back.astype(BF16)
        sums_ref[0:1, :] += jnp.sum(grad_hidden.astype(F32), axis=0, keepdims=True)
        sums_ref[1:2, :] += jnp.sum(back * scaled, axis=0, keepdims=True)
        sums_ref[2:3, :] += jnp.sum(back, axis=0, keepdims=True)


def middle(x_full, att, out, rows, expand, contract, bias, top):
    seq, features = x_full.shape
    hidden = expand.shape[1]
    width = att[0].shape[1]
    block = seq // 2
    part = lambda n: pl.BlockSpec((block, n), lambda i: (i, 0))
    whole = lambda a: pl.BlockSpec(a.shape, lambda i: (0, 0))
    return pl.pallas_call(
        middle_kernel,
        grid=(2,),
        in_specs=[part(features)]
        + [part(width)] * 4
        + [whole(o) for o in out]
        + [whole(rows), whole(expand), whole(contract), whole(bias), part(features)],
        out_specs=[
            part(features),
            part(features),
            part(hidden),
            part(hidden),
            part(features),
            part(features),
            part(features),
            pl.BlockSpec((8, features), lambda i: (0, 0)),
        ],
        out_shape=[
            jax.ShapeDtypeStruct((seq, features), F32),
            jax.ShapeDtypeStruct((seq, features), BF16),
            jax.ShapeDtypeStruct((seq, hidden), BF16),
            jax.ShapeDtypeStruct((seq, hidden), BF16),
            jax.ShapeDtypeStruct((seq, features), BF16),
            jax.ShapeDtypeStruct((seq, features), BF16),
            jax.ShapeDtypeStruct((seq, features), BF16),
            jax.ShapeDtypeStruct((8, features), F32),
        ],
        compiler_params=pltpu.CompilerParams(vmem_limit_bytes=VMEM_LIMIT),
        cost_estimate=pl.CostEstimate(
            flops=2 * seq * features * (features + 4 * hidden),
            bytes_accessed=seq * (9 * features + 4 * hidden + 4 * width) + 4 * features * hidden,
            transcendentals=2 * seq * hidden,
        ),
        name="middle",
    )(x_full, *att, *out, rows, expand, contract, bias, top)


def adam_step(master, gradient, first, second, decay):
    first_new = BETA_FIRST * first + (1.0 - BETA_FIRST) * gradient
    second_new = BETA_SECOND * second + (1.0 - BETA_SECOND) * gradient * gradient
    first_hat = first_new / (1.0 - BETA_FIRST**STEP)
    second_hat = second_new / (1.0 - BETA_SECOND**STEP)
    change = -LEARN_RATE * (first_hat / (jnp.sqrt(second_hat) + ADAM_EPS) + decay * master)
    return (change, first_new, second_new)


def tensor_swap(array, bit):
    return lax.ppermute(array, "tensor", [(rank, rank ^ bit) for rank in range(4)])


def gather_positions(block, rank):
    beside = tensor_swap(block, 1)
    across = tensor_swap(block, 2)
    corner = tensor_swap(across, 1)
    rows = block.shape[0]
    whole = jnp.zeros((4 * rows, block.shape[1]), block.dtype)
    for bit, piece in enumerate((block, beside, across, corner)):
        whole = lax.dynamic_update_slice_in_dim(whole, piece, (rank ^ bit) * rows, 0)
    return whole


def add_beside(partial, core, rows):
    blocks = partial.reshape(2, 2, rows, partial.shape[1])
    give = lax.dynamic_index_in_dim(blocks, 1 - core, 1, keepdims=False)
    keep = lax.dynamic_index_in_dim(blocks, core, 1, keepdims=False)
    return (keep.astype(F32) + tensor_swap(give, 1).astype(F32)).astype(BF16)


def scatter_positions(partial, core, half, rows):
    chip = add_beside(partial, core, rows)
    give = lax.dynamic_index_in_dim(chip, 1 - half, 0, keepdims=False)
    keep = lax.dynamic_index_in_dim(chip, half, 0, keepdims=False)
    return keep.astype(F32) + tensor_swap(give, 2).astype(F32)


def body(
    block_input,
    live_mask,
    cotangent,
    project_in,
    project_out,
    expand,
    contract,
    vectors,
    expand_bias,
    moment_project_in,
    second_project_in,
    moment_project_out,
    second_project_out,
    moment_expand,
    second_expand,
    moment_contract,
    second_contract,
    moment_vectors,
    second_vectors,
    moment_expand_bias,
    second_expand_bias,
):
    rows, _, features = block_input.shape
    shard, _, head_width = project_in.shape
    hidden_width = expand.shape[1]
    pairs = head_width // LANES
    groups = features // shard
    rank = lax.axis_index("tensor")
    core, half = rank % 2, rank // 2
    masters = (project_in, project_out, expand, contract, vectors, expand_bias)

    in_shard = (
        project_in.astype(BF16).reshape(shard, 3, pairs, LANES).transpose(0, 2, 1, 3)
    ).reshape(shard, 3 * head_width)
    out_shard = project_out.astype(BF16).T
    bias_shard = expand_bias.astype(BF16).reshape(-1, shard)
    small_rows = vectors.shape[0] + bias_shard.shape[0]
    small_shard = jnp.concatenate(
        [vectors.astype(BF16), bias_shard, jnp.zeros((LANES - small_rows, shard), BF16)]
    ).T
    first_copy = lax.all_gather(
        jnp.concatenate([in_shard, out_shard, small_shard], axis=1), "fsdp", axis=0, tiled=True
    )
    full_in = first_copy[:, : 3 * head_width]
    full_out = first_copy[:, 3 * head_width : 4 * head_width]
    small = first_copy[:, 4 * head_width :].T
    rows_now = jnp.concatenate([small[: vectors.shape[0]].astype(F32), jnp.zeros((6, features), F32)])
    bias_now = small[vectors.shape[0] : small_rows].astype(F32)
    bias_now = bias_now.reshape(-1, groups, shard).transpose(1, 0, 2).reshape(-1)
    second_copy = lax.all_gather(
        jnp.concatenate([expand.astype(BF16), contract.astype(BF16).T], axis=1),
        "fsdp",
        axis=0,
        tiled=True,
    )
    full_expand = second_copy[:, :hidden_width]
    full_contract = second_copy[:, hidden_width:]

    x_own = block_input[:, 0]
    live_own = lax.dynamic_slice_in_dim(live_mask, rank * rows, rows, 0) > 0
    top_own = cotangent[:, 0] * live_own.astype(F32)
    x_full = gather_positions(x_own.astype(BF16), rank)
    top_full = gather_positions(top_own.astype(BF16), rank)

    query_bias = lax.dynamic_slice_in_dim(rows_now[2], rank * head_width, head_width)
    value_bias = lax.dynamic_slice_in_dim(rows_now[3], rank * head_width, head_width)
    mixed_bias = jnp.stack([query_bias, jnp.zeros_like(query_bias), value_bias])
    mixed_bias = mixed_bias.reshape(3, pairs, LANES).transpose(1, 0, 2).reshape(1, -1)
    normed_one, qkv = project(x_full, rows_now, full_in, mixed_bias)
    attended, queries = attend(live_mask, qkv)

    out_across = tensor_swap(full_out, 2)
    out_all = (full_out, tensor_swap(full_out, 1), out_across, tensor_swap(out_across, 1))
    across = tensor_swap(attended, 2)
    att_all = (attended, tensor_swap(attended, 1), across, tensor_swap(across, 1))
    bias_here = lax.dynamic_slice_in_dim(bias_now, rank * hidden_width, hidden_width)
    attn_full, normed_two, activated, grad_hidden, grad_branch, branch_part, back_part, sums = middle(
        x_full, att_all, out_all, rows_now, full_expand, full_contract, bias_here[None], top_full
    )

    chip_sum = add_beside(back_part, core, rows)
    other_sum = tensor_swap(chip_sum, 2)
    back_sum = chip_sum.astype(F32) + other_sum.astype(F32)

    def block_of(full, index):
        return lax.dynamic_slice_in_dim(full, index * rows, rows, 0)

    def residual_back(x_block, attn_block, top_block, grad_block):
        scaled, inverse = norm_forward(x_block + rows_now[5] * attn_block)
        return top_block + norm_backward(scaled, inverse, grad_block, rows_now[6])

    attn_own = block_of(attn_full, rank)
    pick = lambda array, index: lax.dynamic_index_in_dim(array, index, 0, keepdims=False)
    grad_residual = residual_back(x_own, attn_own, top_own, pick(back_sum, half))
    partner = rank ^ 2
    grad_partner = residual_back(
        block_of(x_full, partner).astype(F32),
        block_of(attn_full, partner),
        block_of(top_full, partner).astype(F32),
        pick(back_sum, 1 - half),
    )
    attn_mine = (grad_residual * rows_now[5]).astype(BF16)
    attn_partner = (grad_partner * rows_now[5]).astype(BF16)
    low = jnp.where(half == 0, attn_mine, attn_partner)
    high = jnp.where(half == 0, attn_partner, attn_mine)
    mine = jnp.stack([low, high])
    other = tensor_swap(mine, 1)
    grad_attn = jnp.where(
        core == 0, jnp.stack([mine, other], axis=1), jnp.stack([other, mine], axis=1)
    ).reshape(4 * rows, features)

    grad_attended = dot_nn(grad_attn, full_out).astype(BF16)
    grad_mixed, head_sums = attend_back(live_mask, qkv, queries, attended, grad_attended)

    branch = scatter_positions(branch_part, core, half, rows) + rows_now[8]
    residual = x_own + rows_now[5] * attn_own
    block_output = residual + rows_now[9] * branch

    grad_expand = dot_tn(normed_two, grad_hidden).astype(BF16)
    grad_contract = dot_tn(grad_branch, activated).astype(BF16)
    grad_out = dot_tn(grad_attn, attended).astype(BF16)
    grad_in = dot_tn(normed_one, grad_mixed).astype(BF16)
    second_sum = lax.psum_scatter(
        jnp.concatenate([grad_expand, grad_contract], axis=1),
        "fsdp",
        scatter_dimension=0,
        tiled=True,
    ).astype(F32)

    normed_part = dot_nt(grad_mixed, full_in).astype(BF16)
    grad_normed_one = scatter_positions(normed_part, core, half, rows)
    scaled_one, inverse_one = norm_forward(x_own)
    input_grad = grad_residual + norm_backward(
        scaled_one, inverse_one, grad_normed_one, rows_now[0]
    )

    place = lambda values, start, total: lax.dynamic_update_slice_in_dim(
        jnp.zeros((total,), F32), values, start, 0
    )
    grad_rows = jnp.stack(
        [
            jnp.sum(grad_normed_one * scaled_one, axis=0),
            jnp.sum(grad_normed_one, axis=0),
            place(head_sums[0], rank * head_width, features),
            place(head_sums[1], rank * head_width, features),
            jnp.sum(grad_residual * rows_now[5], axis=0),
            jnp.sum(grad_residual * attn_own, axis=0),
            sums[1],
            sums[2],
            jnp.sum(top_own * rows_now[9], axis=0),
            jnp.sum(top_own * branch, axis=0),
        ]
    )
    grad_bias = place(sums[0], rank * hidden_width, expand_bias.shape[0] * groups)
    grad_bias = grad_bias.reshape(groups, -1, shard).transpose(1, 0, 2).reshape(-1, features)
    grad_small = jnp.concatenate([grad_rows, grad_bias])
    grad_small = grad_small + tensor_swap(grad_small, 2)
    grad_small = grad_small + tensor_swap(grad_small, 1)
    small_lanes = jnp.concatenate(
        [grad_small, jnp.zeros((LANES - small_rows, features), F32)]
    ).T.astype(BF16)
    first_sum = lax.psum_scatter(
        jnp.concatenate([grad_in, grad_out, small_lanes], axis=1),
        "fsdp",
        scatter_dimension=0,
        tiled=True,
    ).astype(F32)

    sum_in = first_sum[:, : 3 * head_width].reshape(shard, pairs, 3, LANES).transpose(0, 2, 1, 3)
    sum_out = first_sum[:, 3 * head_width : 4 * head_width].T
    sum_small = first_sum[:, 4 * head_width :].T
    shard_rows = sum_small[: vectors.shape[0]]
    totals = (
        sum_in.reshape(project_in.shape),
        sum_out,
        second_sum[:, :hidden_width],
        second_sum[:, hidden_width:].T,
        shard_rows,
        sum_small[vectors.shape[0] : small_rows].reshape(-1),
    )
    firsts = (
        moment_project_in,
        moment_project_out,
        moment_expand,
        moment_contract,
        moment_vectors,
        moment_expand_bias,
    )
    seconds = (
        second_project_in,
        second_project_out,
        second_expand,
        second_contract,
        second_vectors,
        second_expand_bias,
    )
    decays = (WEIGHT_DECAY, WEIGHT_DECAY, WEIGHT_DECAY, WEIGHT_DECAY, 0.0, 0.0)
    results = [adam_step(*each) for each in zip(masters, totals, firsts, seconds, decays)]
    changes = tuple((result[0] for result in results))
    moments = []
    for result in results:
        moments.append(result[1])
        moments.append(result[2])
    return (
        block_output[:, None],
        input_grad[:, None],
        *totals,
        masters[0] + changes[0],
        changes[1],
        masters[2] + changes[2],
        masters[3] + changes[3],
        changes[4],
        changes[5],
        *moments,
        shard_rows[7],
    )


def solution(mesh):
    tokens = P("tensor", "fsdp", None)
    into = P("fsdp", None, "tensor")
    wide = P("fsdp", "tensor")
    tall = P("tensor", "fsdp")
    row = P(None, "fsdp")
    line = P("fsdp")
    params = (into, tall, wide, tall, row, line)
    moments = (into, into, tall, tall, wide, wide, tall, tall, row, row, line, line)
    return jax.shard_map(
        body,
        mesh=mesh,
        in_specs=(tokens, row, tokens) + params + moments,
        out_specs=(tokens, tokens) + params + params + moments + (line,),
        check_vma=False,
    )
```

```python
import functools

import jax
import jax.numpy as jnp
from jax import lax
from jax.experimental import pallas as pl
from jax.experimental.pallas import tpu as pltpu
from jax.sharding import PartitionSpec as P

HEAD_DIM = 64
STEP = 3
NORM_EPS = 1e-06
BETA_FIRST = 0.9
BETA_SECOND = 0.999
LEARN_RATE = 0.004
WEIGHT_DECAY = 0.04
ADAM_EPS = 1e-08
MASKED_SCORE = -1e30
ROOT_HALF = 0.7071067811865476
DENSITY_NORM = 0.3989422804014327
SCORE_SCALE = HEAD_DIM ** (-0.5)
LANES = 128
TILE = 352
CHUNK = 256
LONG = 4
VMEM_LIMIT = 56 * 2**20
F32 = jnp.float32
BF16 = jnp.bfloat16


def dot_nn(left, right):
    return lax.dot_general(left, right, (((1,), (0,)), ((), ())), preferred_element_type=F32)


def dot_nt(left, right):
    return lax.dot_general(left, right, (((1,), (1,)), ((), ())), preferred_element_type=F32)


def dot_tn(left, right):
    return lax.dot_general(left, right, (((0,), (0,)), ((), ())), preferred_element_type=F32)


def tiles_of(total, tile):
    return [(low, min(tile, total - low)) for low in range(0, total, tile)]


def norm_forward(values):
    center = jnp.mean(values, axis=-1, keepdims=True)
    offset = values - center
    spread = jnp.mean(offset * offset, axis=-1, keepdims=True)
    inverse = lax.rsqrt(spread + NORM_EPS)
    return offset * inverse, inverse


def norm_backward(scaled, inverse, grad_normed, norm_gain):
    grad_scaled = grad_normed * norm_gain
    first_mean = jnp.mean(grad_scaled, axis=-1, keepdims=True)
    second_mean = jnp.mean(grad_scaled * scaled, axis=-1, keepdims=True)
    return inverse * (grad_scaled - first_mean - scaled * second_mean)


def gelu_parts(hidden):
    normal_cdf = 0.5 * (1.0 + lax.erf(hidden * ROOT_HALF))
    density = DENSITY_NORM * jnp.exp(-0.5 * hidden * hidden)
    return (hidden * normal_cdf, normal_cdf + hidden * density)


def call(kernel, ids, args, in_specs, outs, out_specs, name, cost=(0, 0, 0), grid=(1,), scratch=(), aliases=None, after=()):
    count = 1 + len(args)
    waits = len(after)

    def run(*refs):
        kernel(*refs[:count], *refs[count + waits :])

    several = isinstance(outs, (list, tuple))
    return pl.pallas_call(
        run,
        grid_spec=pltpu.PrefetchScalarGridSpec(
            num_scalar_prefetch=1,
            grid=grid,
            in_specs=list(in_specs) + [pl.BlockSpec(memory_space=pl.ANY)] * waits,
            out_specs=out_specs,
            scratch_shapes=scratch,
        ),
        out_shape=outs,
        input_output_aliases=aliases or {},
        compiler_params=pltpu.CompilerParams(vmem_limit_bytes=VMEM_LIMIT),
        cost_estimate=pl.CostEstimate(flops=cost[0], bytes_accessed=cost[1], transcendentals=cost[2]),
        name=name,
    )(ids, *args, *after)


def whole(array):
    zeros = (0,) * len(array.shape)
    return pl.BlockSpec(array.shape, lambda *i: zeros)


def plain(kernel, ids, args, outs, name, **more):
    return call(kernel, ids, args, [whole(a) for a in args], outs, [whole(o) for o in outs], name, **more)


def shape_of(shape, dtype):
    return jax.ShapeDtypeStruct(shape, dtype)


ANYWHERE = pl.BlockSpec(memory_space=pl.ANY)


def low_bit(ids_ref):
    return lax.rem(ids_ref[0], 2)


def pack_kernel(ids_ref, in_ref, out_ref, expand_ref, contract_ref, small_ref, first, second, third):
    for pair, packed in enumerate((first, second)):
        for part in range(3):
            packed[:, part * LANES : (part + 1) * LANES] = in_ref[
                part, :, pair * LANES : (pair + 1) * LANES
            ].astype(BF16)
    first[:, 3 * LANES :] = small_ref[...].T.astype(BF16)
    second[:, 3 * LANES :] = out_ref[...].T.astype(BF16)
    hidden = expand_ref.shape[1]
    third[:, :hidden] = expand_ref[...].astype(BF16)
    third[:, hidden:] = contract_ref[...].T.astype(BF16)


def pack(ids, project_in, project_out, expand, contract, small):
    _, shard, head_width = project_in.shape
    widths = (4 * LANES, 3 * LANES + head_width, 2 * expand.shape[1])
    args = (project_in, project_out, expand, contract, small)
    outs = [shape_of((shard, width), BF16) for width in widths]
    return plain(pack_kernel, ids, args, outs, "pack")


def place_rows(ids_ref, near_ref, far_ref, write):
    count, shard = near_ref.shape[0], near_ref.shape[1]
    mine = ids_ref[0]
    for step in range(count):
        for low, ref in enumerate((near_ref, far_ref)):
            owner = lax.bitwise_xor(mine, 2 * step + low)
            write(pl.ds(pl.multiple_of(owner * shard, shard), shard), ref[step])


def flatten_kernel(ids_ref, normed_ref, flat_ref):
    flat_ref[...] = normed_ref[...].T


def flatten(ids, normed, after=()):
    seq, features = normed.shape
    return plain(flatten_kernel, ids, (normed,), [shape_of((features, seq), BF16)], "flatten", after=after)[0]


def unpack_kernel(ids_ref, near_ref, far_ref, out_ref):
    def write(at, values):
        out_ref[at, :] = values[:, 3 * LANES :]

    place_rows(ids_ref, near_ref, far_ref, write)


def unpack(ids, near, far, after=()):
    count, shard, width = near.shape
    outs = [shape_of((2 * count * shard, width - 3 * LANES), BF16)]
    return plain(unpack_kernel, ids, (near, far), outs, "unpack", after=after)[0]


def attend_kernel(pair, ids_ref, live_ref, near_ref, far_ref, normed_ref, *refs):
    if pair == 0:
        x_ref = normed_ref
        rows_ref, normed_ref, scaled_ref, held_ref = refs[0], refs[1], refs[2], refs[-1]
        weight_ref, qkv_ref, attended_ref, query_ref, key_ref, value_ref = refs[3:-1]
    else:
        rows_ref, weight_ref, qkv_ref, attended_ref, query_ref, key_ref, value_ref = refs
    seq = normed_ref.shape[0]
    width = 3 * LANES

    def write(at, values):
        weight_ref[at, :] = values[:, :width]
        if pair == 0:
            held_ref[at, :] = values[:, width:].astype(F32)

    place_rows(ids_ref, near_ref, far_ref, write)
    if pair == 0:
        rows_ref[...] = held_ref[...].T[0 : rows_ref.shape[0]]
    start = pl.multiple_of(ids_ref[1] * (2 * LANES) + pair * LANES, LANES)
    bias_row = jnp.concatenate(
        [rows_ref[2:3, pl.ds(start, LANES)], jnp.zeros((1, LANES), F32), rows_ref[3:4, pl.ds(start, LANES)]],
        axis=1,
    )
    for low, count in tiles_of(seq, TILE):
        at = slice(low, low + count)
        if pair == 0:
            scaled, _ = norm_forward(x_ref[at, :].astype(F32))
            scaled_ref[at, :] = scaled.astype(BF16)
            normed_ref[at, :] = (scaled * rows_ref[0:1, :] + rows_ref[1:2, :]).astype(BF16)
        mixed = dot_nn(normed_ref[at, :], weight_ref[...]) + bias_row
        qkv_ref[at, :] = mixed.astype(BF16)
    lane = lax.broadcasted_iota(jnp.int32, (seq, LANES), 1)
    bias = jnp.where(live_ref[...] > 0, 0.0, MASKED_SCORE).astype(F32)
    key_rows = qkv_ref[:, LANES : 2 * LANES].astype(F32)
    value_rows = qkv_ref[:, 2 * LANES : 3 * LANES].astype(F32)
    for head in range(2):
        own = (lane // HEAD_DIM) == head
        spare = HEAD_DIM * (1 - head)
        extra = jnp.where(lane == spare, bias, 0.0)
        key_ref[head] = jnp.where(own, key_rows, extra).astype(BF16)
        extra = jnp.where(lane == spare, 1.0, 0.0)
        value_ref[head] = jnp.where(own, value_rows, extra).astype(BF16)
    for low, count in tiles_of(seq, TILE):
        at = slice(low, low + count)
        lane = lax.broadcasted_iota(jnp.int32, (count, LANES), 1)
        queries = qkv_ref[at, 0:LANES].astype(F32) * SCORE_SCALE
        both = None
        for head in range(2):
            own = (lane // HEAD_DIM) == head
            spare = HEAD_DIM * (1 - head)
            extra = jnp.where(lane == spare, 1.0, 0.0)
            mine = jnp.where(own, queries, extra).astype(BF16)
            scores = dot_nt(mine, key_ref[head])
            highest = jnp.max(scores, axis=-1, keepdims=True)
            weights = jnp.exp(scores - highest).astype(BF16)
            output = dot_nn(weights, value_ref[head])
            summed = output[:, spare : spare + 1]
            output = output / summed
            both = output if head == 0 else jnp.where(own, output, both)
            rest = -(highest + jnp.log(summed))
            extra = jnp.where(lane == spare + 3, 1.0, 0.0)
            for place in range(3):
                part = rest.astype(BF16).astype(F32)
                extra = jnp.where(lane == spare + place, part, extra)
                rest = rest - part
            query_ref[at, LANES * head : LANES * (head + 1)] = jnp.where(
                own, queries, extra
            ).astype(BF16)
        attended_ref[at, :] = both.astype(BF16)


def attend(pair, ids, live, near, far, normed, rows=None, after=()):
    seq, features = normed.shape
    outs = [
        shape_of((features, 3 * LANES), BF16),
        shape_of((seq, 3 * LANES), BF16),
        shape_of((seq, LANES), BF16),
        shape_of((seq, 2 * LANES), BF16),
    ]
    scratch = [pltpu.VMEM((2, seq, LANES), BF16), pltpu.VMEM((2, seq, LANES), BF16)]
    args = (live, near, far, normed)
    if pair == 0:
        outs = [shape_of((16, features), F32)] + [shape_of((seq, features), BF16)] * 2 + outs
        scratch.append(pltpu.VMEM((features, LANES), F32))
    else:
        args += (rows,)
    return plain(
        functools.partial(attend_kernel, pair),
        ids,
        args,
        outs,
        f"attend_{pair}",
        cost=(LONG * 160 * seq * seq * HEAD_DIM, 0, 0),
        scratch=scratch,
        after=after,
    )


def attend_back_kernel(
    ids_ref,
    live_ref,
    qkv_ref,
    query_ref,
    attended_ref,
    mine_a,
    other_a,
    mine_b,
    other_b,
    out_ref,
    mixed_ref,
    sums_ref,
    grad_ref,
    held_ref,
    query_sum_ref,
):
    seq = qkv_ref.shape[0]
    rows = mine_a.shape[0]
    core = ids_ref[2]
    for index, ref in enumerate((mine_a, other_a, mine_b, other_b)):
        block = 2 * (index // 2) + lax.bitwise_xor(core, index % 2)
        grad_ref[pl.ds(pl.multiple_of(block * rows, 8), rows), :] = dot_nn(ref[...], out_ref[...])
    lane = lax.broadcasted_iota(jnp.int32, (seq, LANES), 1)
    grad = grad_ref[...].astype(BF16).astype(F32)
    product = grad * attended_ref[...].astype(F32)
    for head in range(2):
        own = (lane // HEAD_DIM) == head
        spare = HEAD_DIM * (1 - head)
        inner = -jnp.sum(jnp.where(own, product, 0.0), axis=-1, keepdims=True)
        first = inner.astype(BF16).astype(F32)
        extra = jnp.where(lane == spare, first, jnp.where(lane == spare + 1, inner - first, 0.0))
        held_ref[head] = jnp.where(own, grad, extra).astype(BF16)
    value_sum = jnp.zeros((1, LANES), F32)
    for index, (low, count) in enumerate(tiles_of(seq, TILE)):
        at = slice(low, low + count)
        lane = lax.broadcasted_iota(jnp.int32, (count, LANES), 1)
        bias = jnp.where(live_ref[at, :] > 0, 0.0, MASKED_SCORE).astype(F32)
        key_rows = qkv_ref[at, LANES : 2 * LANES].astype(F32)
        value_rows = qkv_ref[at, 2 * LANES : 3 * LANES].astype(F32)
        grad_keys = grad_values = None
        for head in range(2):
            own = (lane // HEAD_DIM) == head
            spare = HEAD_DIM * (1 - head)
            ones = jnp.where((lane >= spare) & (lane < spare + 3), 1.0, 0.0)
            extra = jnp.where(lane == spare + 3, bias, ones)
            keys = jnp.where(own, key_rows, extra).astype(BF16)
            values = jnp.where(own, value_rows, ones).astype(BF16)
            queries = query_ref[:, LANES * head : LANES * (head + 1)]
            above = held_ref[head]
            weights = jnp.exp(dot_nt(keys, queries))
            grad_scores = (weights * dot_nt(values, above)).astype(BF16)
            value_part = dot_nn(weights.astype(BF16), above)
            key_part = dot_nn(grad_scores, queries)
            part = slice(HEAD_DIM * head, HEAD_DIM * (head + 1))
            query_part = dot_tn(keys, grad_scores)[part]
            if index == 0:
                query_sum_ref[part] = query_part
            else:
                query_sum_ref[part] += query_part
            grad_keys = key_part if head == 0 else jnp.where(own, key_part, grad_keys)
            grad_values = value_part if head == 0 else jnp.where(own, value_part, grad_values)
        grad_values = grad_values.astype(BF16)
        mixed_ref[at, LANES : 2 * LANES] = grad_keys.astype(BF16)
        mixed_ref[at, 2 * LANES : 3 * LANES] = grad_values
        value_sum += jnp.sum(grad_values.astype(F32), axis=0, keepdims=True)
    grad_queries = (query_sum_ref[...].T * SCORE_SCALE).astype(BF16)
    mixed_ref[:, 0:LANES] = grad_queries
    sums_ref[0:1, :] = jnp.sum(grad_queries.astype(F32), axis=0, keepdims=True)
    sums_ref[1:2, :] = value_sum


def attend_back(pair, ids, live, qkv, queries, attended, grads, out_own, after=()):
    seq = qkv.shape[0]
    features = out_own.shape[0]
    outs = [shape_of((seq, 3 * LANES), BF16), shape_of((8, LANES), F32)]
    args = (live, qkv, queries, attended, *grads)
    return call(
        attend_back_kernel,
        ids,
        (*args, out_own),
        [whole(a) for a in args] + [pl.BlockSpec((features, LANES), lambda i, _: (0, pair))],
        outs,
        [whole(o) for o in outs],
        f"attend_back_{pair}",
        cost=(LONG * 80 * seq * seq * HEAD_DIM, 0, 0),
        scratch=[
            pltpu.VMEM((seq, LANES), F32),
            pltpu.VMEM((2, seq, LANES), BF16),
            pltpu.VMEM((LANES, seq), F32),
        ],
        after=after,
    )


def middle_kernel(ids_ref, x_ref, *refs):
    att_refs, out_refs = refs[:8], refs[8:12]
    rows_ref, expand_ref, contract_ref, bias_ref, top_ref = refs[12:17]
    outs = refs[-14:-4]
    normed_ref, act_ref, hidden_ref, grad_ref = outs[:4]
    branch_refs, attn_ref, back_refs, sums_ref = outs[4:6], outs[6], outs[7:9], outs[9]
    held_ref, normed_held, act_held, hidden_held = refs[-4:]
    step = pl.program_id(0)

    @pl.when(step == 0)
    def _():
        sums_ref[...] = jnp.zeros_like(sums_ref)

    attn_sum = rows_ref[4:5, :]
    for device, out_ref in enumerate(out_refs):
        held_ref[:, :LANES] = att_refs[2 * device][0]
        held_ref[:, LANES:] = att_refs[2 * device + 1][0]
        attn_sum = attn_sum + dot_nt(held_ref[...], out_ref[...])

    @pl.when(step == 1)
    def _():
        attn_ref[...] = attn_sum

    residual = x_ref[0].astype(F32) + rows_ref[5:6, :] * attn_sum
    scaled, _ = norm_forward(residual)
    normed_held[...] = (scaled * rows_ref[6:7, :] + rows_ref[7:8, :]).astype(BF16)
    normed_ref[0] = normed_held[...]
    grad_ref[0] = (top_ref[0].astype(F32) * rows_ref[9:10, :]).astype(BF16)
    for low in range(0, act_held.shape[1], CHUNK):
        at = slice(low, low + CHUNK)
        activated, slope = gelu_parts(dot_nn(normed_held[...], expand_ref[:, at]) + bias_ref[:, at])
        act_held[:, at] = activated.astype(BF16)
        grad_hidden = (dot_nn(grad_ref[0], contract_ref[:, at]) * slope).astype(BF16)
        hidden_held[:, at] = grad_hidden
        sums_ref[0:1, at] += jnp.sum(grad_hidden.astype(F32), axis=0, keepdims=True)
    act_ref[0] = act_held[...]
    hidden_ref[0] = hidden_held[...]
    back = dot_nt(hidden_held[...], expand_ref[...])
    sums_ref[1:2, :] += jnp.sum(back * scaled, axis=0, keepdims=True)
    sums_ref[2:3, :] += jnp.sum(back, axis=0, keepdims=True)
    branch = dot_nt(act_held[...], contract_ref[...]).astype(BF16)
    for index in range(2):

        @pl.when(step == index)
        def _():
            back_refs[index][...] = back.astype(BF16)
            branch_refs[index][0] = branch


def middle(half, ids, x_full, att, out_all, rows, weights, bias, top_full, before=(), after=()):
    _, count, features = x_full.shape
    hidden = weights.shape[1] // 2
    block = lambda i, ids_ref: 2 * half + lax.bitwise_xor(ids_ref[2], 1 - i)
    part = lambda n: pl.BlockSpec((1, count, n), lambda i, ids_ref: (block(i, ids_ref), 0, 0))
    held = lambda n: pl.BlockSpec((1, count, n), lambda i, _: (half, 0, 0))
    column = lambda c: pl.BlockSpec((features, hidden), lambda i, _: (0, c))
    full = lambda n: shape_of((4, count, n), BF16)
    outs = [full(features), full(hidden), full(hidden), full(features)]
    specs = [part(features), part(hidden), part(hidden), part(features)]
    outs += [shape_of((2, count, features), BF16)] * 2
    specs += [held(features)] * 2
    rest = [
        shape_of((count, features), F32),
        shape_of((count, features), BF16),
        shape_of((count, features), BF16),
        shape_of((8, features), F32),
    ]
    args = (x_full, *att, *out_all, rows, weights, weights, bias, top_full)
    seq = 2 * count
    results = call(
        middle_kernel,
        ids,
        (*args, *before),
        [part(features)]
        + [part(LANES)] * len(att)
        + [whole(o) for o in out_all]
        + [whole(rows), column(0), column(1), whole(bias), part(features)]
        + [ANYWHERE] * len(before),
        outs + rest,
        specs + [whole(o) for o in rest],
        f"middle_{half}",
        (2 * seq * features * (features + 4 * hidden), seq * 24 * features + 6 * features * hidden, 2 * seq * hidden),
        grid=(2,),
        scratch=[pltpu.VMEM((count, 2 * LANES), BF16)] + [pltpu.VMEM((count, features), BF16)] * 3,
        aliases={1 + len(args) + index: index for index in range(len(before))},
        after=after,
    )
    return results[:6], results[6:]


def pair_sum_kernel(ids_ref, keep_ref, arrived_ref, sum_ref):
    sum_ref[...] = (keep_ref[...].astype(F32) + arrived_ref[...].astype(F32)).astype(BF16)


def pair_sum(ids, keep, arrived, name, after=()):
    outs = [shape_of(keep.shape, BF16)]
    return plain(pair_sum_kernel, ids, (keep, arrived), outs, name, after=after)[0]


def split_sum_kernel(ids_ref, keep_ref, arrived_ref, give_ref, stay_ref):
    half = ids_ref[3]
    total = keep_ref[...].astype(F32) + arrived_ref[...].astype(F32)
    give_ref[...] = jnp.where(half == 0, total[1], total[0]).astype(BF16)
    stay_ref[...] = jnp.where(half == 0, total[0], total[1]).astype(BF16)


def split_sum(ids, keep, arrived, name, after=()):
    outs = [shape_of(keep.shape[1:], BF16)] * 2
    return plain(split_sum_kernel, ids, (keep, arrived), outs, name, after=after)


def residual_kernel(ids_ref, chip_ref, arrived_ref, x_ref, attn_ref, top_ref, rows_ref, grad_ref):
    total = chip_ref[...].astype(F32) + arrived_ref[...].astype(F32)
    scaled, inverse = norm_forward(x_ref[0].astype(F32) + rows_ref[5:6, :] * attn_ref[...])
    grad = top_ref[0].astype(F32) + norm_backward(scaled, inverse, total, rows_ref[6:7, :])
    grad_ref[...] = (grad * rows_ref[5:6, :]).astype(BF16)


def residual_back(half, ids, chip, arrived, x_full, attn, top_full, rows, after=()):
    count, features = chip.shape
    part = pl.BlockSpec((1, count, features), lambda i, ids_ref: (2 * half + ids_ref[2], 0, 0))
    out = shape_of((count, features), BF16)
    return call(
        residual_kernel,
        ids,
        (chip, arrived, x_full, attn, top_full, rows),
        [whole(chip), whole(arrived), part, whole(attn), part, whole(rows)],
        [out],
        [whole(out)],
        f"residual_back_{half}",
        after=after,
    )[0]


def own_kernel(
    ids_ref,
    x_ref,
    top_ref,
    attn_a,
    attn_b,
    chip_a,
    chip_b,
    arrived_a,
    arrived_b,
    stay_ref,
    branch_ref,
    rows_ref,
    output_ref,
    grad_ref,
    sums_ref,
):
    first = ids_ref[3] == 0
    choose = lambda a, b: jnp.where(first, a[...].astype(F32), b[...].astype(F32))
    attn_sum = choose(attn_a, attn_b)
    total = choose(chip_a, chip_b) + choose(arrived_a, arrived_b)
    residual = x_ref[...] + rows_ref[5:6, :] * attn_sum
    branch = stay_ref[...].astype(F32) + branch_ref[...].astype(F32) + rows_ref[8:9, :]
    output_ref[:, 0, :] = residual + rows_ref[9:10, :] * branch
    scaled, inverse = norm_forward(residual)
    top = top_ref[...]
    grad = top + norm_backward(scaled, inverse, total, rows_ref[6:7, :])
    grad_ref[...] = grad
    for row, values in enumerate((grad * rows_ref[5:6, :], grad * attn_sum, top * rows_ref[9:10, :], top * branch)):
        sums_ref[row : row + 1, :] = jnp.sum(values, axis=0, keepdims=True)


def own_block(ids, x_own, top_own, attn, chips, arrived, stay, branch, rows, after=()):
    rows_count, features = x_own.shape
    outs = [
        shape_of((rows_count, 1, features), F32),
        shape_of(x_own.shape, F32),
        shape_of((8, features), F32),
    ]
    args = (x_own, top_own, *attn, *chips, *arrived, stay, branch, rows)
    return plain(own_kernel, ids, args, outs, "own_block", after=after)


def matrices_kernel(ids_ref, left_a, left_b, right_a, right_b, out_ref, flat_ref):
    step = pl.program_id(0)
    per = pl.num_programs(0) // 2

    @pl.when(step == 0)
    def _():
        flat_ref[...] = left_a[...].T

    @pl.when(step == per)
    def _():
        flat_ref[...] = left_b[...].T

    right = jnp.where(step < per, right_a[...], right_b[...])
    out_ref[...] = dot_nn(flat_ref[...], right).astype(BF16)


def matrices(ids, normed, hidden, grad, activated, after=()):
    seq, features = normed.shape
    width = hidden.shape[1]
    block = 512
    per = width // block
    out = shape_of((features, 2 * width), BF16)
    return call(
        matrices_kernel,
        ids,
        (normed, grad, hidden, activated),
        [
            whole(normed),
            whole(grad),
            pl.BlockSpec((seq, block), lambda i, _: (0, jnp.minimum(i, per - 1))),
            pl.BlockSpec((seq, block), lambda i, _: (0, jnp.maximum(i - per, 0))),
        ],
        [out],
        [pl.BlockSpec((features, block), lambda i, _: (0, i))],
        "matrices",
        grid=(2 * per,),
        scratch=[pltpu.VMEM((features, seq), BF16)],
        after=after,
    )[0]


def store_shards(ids_ref, index, values, give_ref, keep_ref):
    @pl.when(low_bit(ids_ref) == index % 2)
    def _():
        keep_ref[index // 2] = values

    @pl.when(low_bit(ids_ref) != index % 2)
    def _():
        give_ref[index // 2] = values


def out_grad_kernel(ids_ref, att_a, att_b, mine_a, other_a, mine_b, other_b, give_ref, keep_ref):
    core = ids_ref[2]
    total = [None, None]
    for index, ref in enumerate((mine_a, other_a, mine_b, other_b)):
        block = 2 * (index // 2) + lax.bitwise_xor(core, index % 2)
        for pair, att_ref in enumerate((att_a, att_b)):
            part = dot_tn(att_ref[block], ref[...])
            total[pair] = part if index == 0 else total[pair] + part
    count, _, shard = give_ref.shape
    for place in range(2 * count):
        values = jnp.concatenate([t[:, place * shard : (place + 1) * shard] for t in total]).astype(BF16)
        store_shards(ids_ref, place, values, give_ref, keep_ref)


def out_grad(ids, attended, grads, places, after=()):
    count, features = grads[0].shape
    outs = [shape_of((places // 2, 2 * LANES, features // places), BF16)] * 2
    args = [a.reshape(4, count, LANES) for a in attended] + list(grads)
    return plain(out_grad_kernel, ids, args, outs, "out_grad", after=after)


def in_grad_kernel(ids_ref, flat_ref, mixed_ref, give_ref, keep_ref):
    shard = give_ref.shape[1]
    values = dot_nn(flat_ref[...], mixed_ref[...]).astype(BF16)
    for place in range(values.shape[0] // shard):
        store_shards(ids_ref, place, values[place * shard : (place + 1) * shard], give_ref, keep_ref)


def in_grad(pair, ids, flat, mixed, places, after=()):
    features, seq = flat.shape
    width = mixed.shape[1]
    outs = [shape_of((places // 2, features // places, width), BF16)] * 2
    return plain(in_grad_kernel, ids, (flat, mixed), outs, f"in_grad_{pair}", after=after)


def low_sum_kernel(ids_ref, keep_ref, arrived_ref, *out_refs):
    high = lax.div(ids_ref[0], 2)
    for step, out_ref in enumerate(out_refs):
        at = lax.bitwise_xor(high, step)
        out_ref[...] = (keep_ref[at].astype(F32) + arrived_ref[at].astype(F32)).astype(BF16)


def low_sum(ids, keep, arrived, name, after=()):
    outs = [shape_of(keep.shape[1:], BF16)] * keep.shape[0]
    return plain(low_sum_kernel, ids, (keep, arrived), outs, name, after=after)


def input_back_kernel(ids_ref, scaled_ref, mixed_a, mixed_b, weight_a, weight_b, give_ref, keep_ref, sums_ref):
    step = pl.program_id(0)

    @pl.when(step == 0)
    def _():
        sums_ref[...] = jnp.zeros_like(sums_ref)

    total = dot_nt(mixed_a[0], weight_a[...]) + dot_nt(mixed_b[0], weight_b[...])
    sums_ref[0:1, :] += jnp.sum(total * scaled_ref[0].astype(F32), axis=0, keepdims=True)
    sums_ref[1:2, :] += jnp.sum(total, axis=0, keepdims=True)

    @pl.when(step < 2)
    def _():
        give_ref[0] = total.astype(BF16)

    @pl.when(step >= 2)
    def _():
        keep_ref[0] = total.astype(BF16)


def input_back(ids, scaled, mixed, weights, after=()):
    _, count, features = scaled.shape
    width = mixed[0].shape[2]
    def part(n):
        return pl.BlockSpec(
            (1, count, n),
            lambda i, ids_ref: (2 * lax.rem(i, 2) + lax.bitwise_xor(ids_ref[2], 1 - lax.div(i, 2)), 0, 0),
        )
    outs = [shape_of((2, count, features), BF16)] * 2 + [shape_of((8, features), F32)]
    return call(
        input_back_kernel,
        ids,
        (scaled, *mixed, *weights),
        [part(features), part(width), part(width)] + [whole(w) for w in weights],
        outs,
        [
            pl.BlockSpec((1, count, features), lambda i, _: (jnp.minimum(i, 1), 0, 0)),
            pl.BlockSpec((1, count, features), lambda i, _: (jnp.maximum(i - 2, 0), 0, 0)),
            whole(outs[2]),
        ],
        "input_back",
        grid=(4,),
        after=after,
    )


def input_kernel(ids_ref, stay_ref, arrived_ref, x_ref, grad_ref, rows_ref, out_ref):
    total = stay_ref[...].astype(F32) + arrived_ref[...].astype(F32)
    scaled, inverse = norm_forward(x_ref[...])
    out_ref[:, 0, :] = grad_ref[...] + norm_backward(scaled, inverse, total, rows_ref[0:1, :])


def input_grad_of(ids, stay, arrived, x_own, grad_residual, rows, after=()):
    outs = [shape_of((x_own.shape[0], 1, x_own.shape[1]), F32)]
    args = (stay, arrived, x_own, grad_residual, rows)
    return plain(input_kernel, ids, args, outs, "input_grad", after=after)[0]


def adam_step(master, gradient, first, second, decay):
    first_new = BETA_FIRST * first + (1.0 - BETA_FIRST) * gradient
    second_new = BETA_SECOND * second + (1.0 - BETA_SECOND) * gradient * gradient
    first_hat = first_new / (1.0 - BETA_FIRST**STEP)
    second_hat = second_new / (1.0 - BETA_SECOND**STEP)
    change = -LEARN_RATE * (first_hat / (jnp.sqrt(second_hat) + ADAM_EPS) + decay * master)
    return (change, first_new, second_new)


def adam_kernel(gradients, decay, keep_change, ids_ref, *refs):
    count = len(refs) - 7
    parts, (master, first, second), outs = refs[:count], refs[count:-4], refs[-4:]
    for at, gradient in gradients(parts):
        change, first_new, second_new = adam_step(master[at], gradient, first[at], second[at], decay)
        outs[0][at] = gradient
        outs[1][at] = change if keep_change else master[at] + change
        outs[2][at] = first_new
        outs[3][at] = second_new


def adam(gradients, decay, keep_change, ids, parts, master, first, second, name, after=()):
    outs = [shape_of(master.shape, F32)] * 4
    return plain(
        functools.partial(adam_kernel, gradients, decay, keep_change),
        ids,
        (*parts, master, first, second),
        outs,
        name,
        after=after,
    )


def sum_refs(refs):
    total = refs[0][...].astype(F32)
    for ref in refs[1:]:
        total = total + ref[...].astype(F32)
    return total


def high_sum_kernel(ids_ref, *refs):
    refs[-1][...] = sum_refs(refs[:-1])


def high_sum(ids, parts, name, after=()):
    out = shape_of(parts[0].shape, F32)
    return plain(high_sum_kernel, ids, parts, [out], name, after=after)[0]


def in_gradients(parts):
    totals = (parts[0][...], sum_refs(parts[1:]))
    for pair, total in enumerate(totals):
        columns = slice(pair * LANES, (pair + 1) * LANES)
        for part in range(3):
            yield (part, slice(None), columns), total[:, part * LANES : (part + 1) * LANES]


def out_gradients(parts):
    yield (slice(None), slice(None)), sum_refs(parts)


def expand_gradients(parts):
    yield (slice(None), slice(None)), parts[0][:, : parts[0].shape[1] // 2].astype(F32)


def contract_gradients(parts):
    yield (slice(None), slice(None)), parts[0][:, parts[0].shape[1] // 2 :].astype(F32).T


def tensor_swap(array, bit):
    return lax.ppermute(array, "tensor", [(rank, rank ^ bit) for rank in range(4)])


def fsdp_swap(array, bit):
    size = lax.axis_size("fsdp")
    return lax.ppermute(array, "fsdp", [(rank, rank ^ bit) for rank in range(size)])


def behind(array, *others):
    return lax.optimization_barrier((array,) + others)[0]


def around(array):
    across = tensor_swap(array, 2)
    return (array, tensor_swap(array, 1), across, tensor_swap(across, 1))


def gather_positions(block, rank):
    full = jnp.zeros((4,) + block.shape, block.dtype)
    for bit, piece in enumerate(around(block)):
        full = lax.dynamic_update_slice_in_dim(full, piece[None], rank ^ bit, 0)
    return full


def gather_shards(piece):
    count = lax.axis_size("fsdp") // 2
    near = jnp.stack([piece] + [fsdp_swap(piece, 2 * step) for step in range(1, count)])
    return near, fsdp_swap(near, 1)


def body(
    block_input,
    live_mask,
    cotangent,
    project_in,
    project_out,
    expand,
    contract,
    vectors,
    expand_bias,
    moment_project_in,
    second_project_in,
    moment_project_out,
    second_project_out,
    moment_expand,
    second_expand,
    moment_contract,
    second_contract,
    moment_vectors,
    second_vectors,
    moment_expand_bias,
    second_expand_bias,
):
    rows, _, features = block_input.shape
    shard, _, head_width = project_in.shape
    hidden_width = expand.shape[1]
    seq = 4 * rows
    places = lax.axis_size("fsdp")
    rank = lax.axis_index("tensor")
    place = lax.axis_index("fsdp")
    ids = jnp.stack([place, rank, rank % 2, rank // 2]).astype(jnp.int32)
    parts_first = lambda array: array.transpose(1, 0, 2)

    bias_shard = expand_bias.reshape(-1, shard)
    vector_rows = vectors.shape[0]
    small_rows = vector_rows + bias_shard.shape[0]
    small_shard = jnp.concatenate(
        [vectors, bias_shard, jnp.zeros((LANES - small_rows, shard), F32)]
    )
    packed = pack(ids, parts_first(project_in), project_out, expand, contract, small_shard)
    first_shards = gather_shards(packed[0])
    second_shards = gather_shards(behind(packed[1], first_shards[0]))
    weights = lax.all_gather(
        behind(packed[2], second_shards[0]), "fsdp", axis=0, tiled=True
    )

    x_own = block_input[:, 0]
    live_own = lax.dynamic_slice_in_dim(live_mask, rank * rows, rows, 0) > 0
    top_own = cotangent[:, 0] * live_own.astype(F32)
    x_full = gather_positions(x_own.astype(BF16), rank)
    top_full = gather_positions(behind(top_own.astype(BF16), x_full), rank)

    rows_now, normed_one, scaled_one, *heads = attend(
        0, ids, live_mask, *first_shards, x_full.reshape(seq, features)
    )
    heads = [heads]
    out_own = unpack(ids, *second_shards, after=(heads[0][2],))
    heads.append(attend(1, ids, live_mask, *second_shards, normed_one, rows_now, (out_own,)))
    normed_flat = flatten(ids, normed_one, (heads[1][2],))
    held = (normed_flat,)
    out_all = around(out_own)
    att_sets = [around(each[2]) for each in heads]
    att_all = [
        att_sets[pair][device].reshape(4, rows, LANES) for device in range(4) for pair in range(2)
    ]
    bias_now = rows_now[vector_rows:small_rows]
    bias_now = bias_now.reshape(-1, places, shard).transpose(1, 0, 2).reshape(1, -1)
    bias_here = lax.dynamic_slice_in_dim(bias_now, rank * hidden_width, hidden_width, 1)

    kept = ()
    sums, attn, chips, arrived = [], [], [], []
    grads = []
    for half in range(2):
        kept, (attn_part, back_give, back_keep, sums_part) = middle(
            half, ids, x_full, att_all, out_all, rows_now, weights, bias_here, top_full, kept, held
        )
        arrived_part = tensor_swap(back_give, 1)
        if half == 1:
            grads.append(
                residual_back(
                    0, ids, chips[0], arrived[0], x_full, attn[0], top_full, rows_now, (back_give,)
                )
            )
            grads.append(tensor_swap(grads[0], 1))
        chip = pair_sum(ids, back_keep, arrived_part, f"back_sum_{half}", grads[:1])
        held = (chip,)
        chips.append(chip)
        arrived.append(tensor_swap(chip, 2))
        attn.append(attn_part)
        sums.append(sums_part)
    normed_two, activated, grad_hidden, grad_branch = [
        array.reshape(seq, array.shape[2]) for array in kept[:4]
    ]
    branch_give, branch_keep = kept[4:]
    sums = sums[0] + sums[1]
    grad_second = matrices(ids, normed_two, grad_hidden, grad_branch, activated, held)
    grads.append(
        residual_back(
            1, ids, chips[1], arrived[1], x_full, attn[1], top_full, rows_now, (grad_second,)
        )
    )
    grads.append(tensor_swap(grads[2], 1))
    second_sum = lax.psum_scatter(
        behind(grad_second, grads[2]), "fsdp", scatter_dimension=0, tiled=True
    )

    branch_arrived = tensor_swap(behind(branch_give, chips[1]), 1)
    give, branch_stay = split_sum(ids, branch_keep, branch_arrived, "branch_sum", (grads[2],))
    branch_arrived = tensor_swap(give, 2)

    out_give, out_keep = out_grad(ids, [each[2] for each in heads], grads, places)
    out_arrived = fsdp_swap(out_give, 1)
    mixed, head_sums = [], []
    sends = lambda low: [low[0]] + [fsdp_swap(low[step], 2 * step) for step in range(1, places // 2)]
    wait = (out_give, give)
    for pair in range(2):
        weight, qkv, attended, queries = heads[pair]
        mixed_pair, pair_sums = attend_back(
            pair, ids, live_mask, qkv, queries, attended, grads, out_own, wait
        )
        mixed.append(mixed_pair)
        head_sums.append(pair_sums)
        if pair == 1:
            in_low = low_sum(ids, *in_parts, "in_low_0", (mixed_pair,))
            in_sums = sends(in_low)
            wait = (in_low[0],)
        else:
            wait = ()
        in_give, in_keep = in_grad(pair, ids, normed_flat, mixed_pair, places, wait)
        in_parts = (in_keep, fsdp_swap(in_give, 1))
        if pair == 0:
            out_low = low_sum(ids, out_keep, out_arrived, "out_low", (in_give,))
            wait = (in_give, out_low[0], branch_arrived)
    input_give, input_keep, input_sums = input_back(
        ids,
        scaled_one.reshape(4, rows, features),
        [each.reshape(4, rows, each.shape[1]) for each in mixed],
        [each[0] for each in heads],
        (in_give,),
    )
    out_sums = sends(out_low)
    give, stay = split_sum(ids, input_keep, tensor_swap(input_give, 1), "input_sum")
    input_arrived = tensor_swap(give, 2)
    block_output, grad_residual, own_sums = own_block(
        ids, x_own, top_own, attn, chips, arrived, branch_stay, branch_arrived, rows_now, (input_give,)
    )
    sum_first = high_sum(ids, in_sums, "in_sum_0", (own_sums,))
    in_sums = [sum_first] + sends(low_sum(ids, *in_parts, "in_low_1", (sum_first,)))
    input_grad = input_grad_of(ids, stay, input_arrived, x_own, grad_residual, rows_now)

    lay = lambda values, start, total: lax.dynamic_update_slice_in_dim(
        jnp.zeros((total,), F32), values, start, 0
    )
    head_sums = jnp.concatenate(head_sums, axis=1)
    grad_rows = jnp.stack(
        [
            input_sums[0],
            input_sums[1],
            lay(head_sums[0], rank * head_width, features),
            lay(head_sums[1], rank * head_width, features),
            own_sums[0],
            own_sums[1],
            sums[1],
            sums[2],
            own_sums[2],
            own_sums[3],
        ]
    )
    grad_bias = lay(sums[0], rank * hidden_width, expand_bias.shape[0] * places)
    grad_bias = grad_bias.reshape(places, -1, shard).transpose(1, 0, 2).reshape(-1, features)
    small = jnp.concatenate([grad_rows, grad_bias])
    small = sum([tensor_swap(small, bit) for bit in (1, 2, 3)], small)
    small = small + fsdp_swap(small, 1)
    small = sum([fsdp_swap(small, 2 * step) for step in range(1, places // 2)], small)
    small = lax.dynamic_slice_in_dim(small, place * shard, shard, 1)
    grad_vectors = small[:vector_rows]
    grad_bias = small[vector_rows:small_rows].reshape(-1)

    new_in = adam(
        in_gradients,
        WEIGHT_DECAY,
        False,
        ids,
        in_sums,
        parts_first(project_in),
        parts_first(moment_project_in),
        parts_first(second_project_in),
        "adam_in",
    )
    new_in = [parts_first(array) for array in new_in]
    new_out = adam(
        out_gradients,
        WEIGHT_DECAY,
        True,
        ids,
        out_sums,
        project_out,
        moment_project_out,
        second_project_out,
        "adam_out",
    )
    second = (second_sum,)
    new_expand = adam(
        expand_gradients, WEIGHT_DECAY, False, ids, second, expand, moment_expand, second_expand, "adam_expand"
    )
    new_contract = adam(
        contract_gradients,
        WEIGHT_DECAY,
        False,
        ids,
        second,
        contract,
        moment_contract,
        second_contract,
        "adam_contract",
    )
    change, first, second = adam_step(vectors, grad_vectors, moment_vectors, second_vectors, 0.0)
    new_vectors = (grad_vectors, change, first, second)
    change, first, second = adam_step(
        expand_bias, grad_bias, moment_expand_bias, second_expand_bias, 0.0
    )
    new_bias = (grad_bias, change, first, second)
    updated = (new_in, new_out, new_expand, new_contract, new_vectors, new_bias)
    return (
        block_output,
        input_grad,
        *[each[0] for each in updated],
        *[each[1] for each in updated],
        *[array for each in updated for array in each[2:]],
        grad_vectors[7],
    )


def solution(mesh):
    tokens = P("tensor", "fsdp", None)
    into = P("fsdp", None, "tensor")
    wide = P("fsdp", "tensor")
    tall = P("tensor", "fsdp")
    row = P(None, "fsdp")
    line = P("fsdp")
    params = (into, tall, wide, tall, row, line)
    moments = (into, into, tall, tall, wide, wide, tall, tall, row, row, line, line)
    return jax.shard_map(
        body,
        mesh=mesh,
        in_specs=(tokens, row, tokens) + params + moments,
        out_specs=(tokens, tokens) + params + params + moments + (line,),
        check_vma=False,
    )
```

```python
import functools

import jax
import jax.numpy as jnp
from jax import lax
from jax.experimental import pallas as pl
from jax.experimental.pallas import tpu as pltpu
from jax.sharding import PartitionSpec as P

HEAD_DIM = 64
STEP = 3
NORM_EPS = 1e-06
BETA_FIRST = 0.9
BETA_SECOND = 0.999
LEARN_RATE = 0.004
WEIGHT_DECAY = 0.04
ADAM_EPS = 1e-08
MASKED_SCORE = -1e30
ROOT_HALF = 0.7071067811865476
DENSITY_NORM = 0.3989422804014327
SCORE_SCALE = HEAD_DIM ** (-0.5)
LANES = 128
TILE = 352
CHUNK = 256
LONG = 4
SMALL = 16
LARGE = 32
ALL = 56
TOKENS = {}
F32 = jnp.float32
BF16 = jnp.bfloat16


def dot_nn(left, right):
    return lax.dot_general(left, right, (((1,), (0,)), ((), ())), preferred_element_type=F32)


def dot_nt(left, right):
    return lax.dot_general(left, right, (((1,), (1,)), ((), ())), preferred_element_type=F32)


def dot_tn(left, right):
    return lax.dot_general(left, right, (((0,), (0,)), ((), ())), preferred_element_type=F32)


def tiles_of(total, tile):
    return [(low, min(tile, total - low)) for low in range(0, total, tile)]


def norm_forward(values):
    center = jnp.mean(values, axis=-1, keepdims=True)
    offset = values - center
    spread = jnp.mean(offset * offset, axis=-1, keepdims=True)
    inverse = lax.rsqrt(spread + NORM_EPS)
    return offset * inverse, inverse


def norm_backward(scaled, inverse, grad_normed, norm_gain):
    grad_scaled = grad_normed * norm_gain
    first_mean = jnp.mean(grad_scaled, axis=-1, keepdims=True)
    second_mean = jnp.mean(grad_scaled * scaled, axis=-1, keepdims=True)
    return inverse * (grad_scaled - first_mean - scaled * second_mean)


def gelu_parts(hidden):
    normal_cdf = 0.5 * (1.0 + lax.erf(hidden * ROOT_HALF))
    density = DENSITY_NORM * jnp.exp(-0.5 * hidden * hidden)
    return (hidden * normal_cdf, normal_cdf + hidden * density)


def call(kernel, ids, args, in_specs, outs, out_specs, name, cost=(0, 0, 0), grid=(1,), scratch=(), aliases=None, after=(), vmem=SMALL):
    count = 1 + len(args)
    waits = len(after)
    token = shape_of((8, LANES), F32)

    def run(*refs):
        place = count + waits + len(outs)
        refs[place][...] = jnp.zeros_like(refs[place])
        kernel(*refs[:count], *refs[count + waits : place], *refs[place + 1 :])

    *results, done = pl.pallas_call(
        run,
        grid_spec=pltpu.PrefetchScalarGridSpec(
            num_scalar_prefetch=1,
            grid=grid,
            in_specs=list(in_specs) + [pl.BlockSpec(memory_space=pl.ANY)] * waits,
            out_specs=list(out_specs) + [whole(token)],
            scratch_shapes=scratch,
        ),
        out_shape=list(outs) + [token],
        input_output_aliases=aliases or {},
        compiler_params=pltpu.CompilerParams(vmem_limit_bytes=vmem * 2**20),
        cost_estimate=pl.CostEstimate(flops=cost[0], bytes_accessed=cost[1], transcendentals=cost[2]),
        name=name,
    )(ids, *args, *after)
    TOKENS[name] = done
    return results


def done(*names):
    return tuple(TOKENS[name] for name in names)


def whole(array):
    zeros = (0,) * len(array.shape)
    return pl.BlockSpec(array.shape, lambda *i: zeros)


def plain(kernel, ids, args, outs, name, **more):
    return call(kernel, ids, args, [whole(a) for a in args], outs, [whole(o) for o in outs], name, **more)


def shape_of(shape, dtype):
    return jax.ShapeDtypeStruct(shape, dtype)


ANYWHERE = pl.BlockSpec(memory_space=pl.ANY)


def low_bit(ids_ref):
    return lax.rem(ids_ref[0], 2)


def pack_kernel(ids_ref, in_ref, out_ref, expand_ref, contract_ref, small_ref, first, second, third):
    for pair, packed in enumerate((first, second)):
        for part in range(3):
            packed[:, part * LANES : (part + 1) * LANES] = in_ref[
                part, :, pair * LANES : (pair + 1) * LANES
            ].astype(BF16)
    first[:, 3 * LANES :] = small_ref[...].T.astype(BF16)
    second[:, 3 * LANES :] = out_ref[...].T.astype(BF16)
    hidden = expand_ref.shape[1]
    third[:, :hidden] = expand_ref[...].astype(BF16)
    third[:, hidden:] = contract_ref[...].T.astype(BF16)


def pack(ids, project_in, project_out, expand, contract, small):
    _, shard, head_width = project_in.shape
    widths = (4 * LANES, 3 * LANES + head_width, 2 * expand.shape[1])
    args = (project_in, project_out, expand, contract, small)
    outs = [shape_of((shard, width), BF16) for width in widths]
    return plain(pack_kernel, ids, args, outs, "pack", vmem=ALL)


def place_rows(ids_ref, near_ref, far_ref, write):
    count, shard = near_ref.shape[0], near_ref.shape[1]
    mine = ids_ref[0]
    for step in range(count):
        for low, ref in enumerate((near_ref, far_ref)):
            owner = lax.bitwise_xor(mine, 2 * step + low)
            write(pl.ds(pl.multiple_of(owner * shard, shard), shard), ref[step])


def flatten_kernel(ids_ref, normed_ref, flat_ref):
    flat_ref[...] = normed_ref[...].T


def flatten(ids, normed, after=()):
    seq, features = normed.shape
    return plain(flatten_kernel, ids, (normed,), [shape_of((features, seq), BF16)], "flatten", after=after)[0]


def unpack_kernel(ids_ref, near_ref, far_ref, out_ref):
    def write(at, values):
        out_ref[at, :] = values[:, 3 * LANES :]

    place_rows(ids_ref, near_ref, far_ref, write)


def unpack(ids, near, far, after=()):
    count, shard, width = near.shape
    outs = [shape_of((2 * count * shard, width - 3 * LANES), BF16)]
    return plain(unpack_kernel, ids, (near, far), outs, "unpack", after=after)[0]


def attend_kernel(pair, ids_ref, live_ref, near_ref, far_ref, normed_ref, *refs):
    if pair == 0:
        x_ref = normed_ref
        rows_ref, normed_ref, scaled_ref, held_ref = refs[0], refs[1], refs[2], refs[-1]
        weight_ref, qkv_ref, attended_ref, query_ref, key_ref, value_ref = refs[3:-1]
    else:
        rows_ref, weight_ref, qkv_ref, attended_ref, query_ref, key_ref, value_ref = refs
    seq = normed_ref.shape[0]
    width = 3 * LANES

    def write(at, values):
        weight_ref[at, :] = values[:, :width]
        if pair == 0:
            held_ref[at, :] = values[:, width:].astype(F32)

    place_rows(ids_ref, near_ref, far_ref, write)
    if pair == 0:
        rows_ref[...] = held_ref[...].T[0 : rows_ref.shape[0]]
    start = pl.multiple_of(ids_ref[1] * (2 * LANES) + pair * LANES, LANES)
    bias_row = jnp.concatenate(
        [rows_ref[2:3, pl.ds(start, LANES)], jnp.zeros((1, LANES), F32), rows_ref[3:4, pl.ds(start, LANES)]],
        axis=1,
    )
    for low, count in tiles_of(seq, TILE):
        at = slice(low, low + count)
        if pair == 0:
            scaled, _ = norm_forward(x_ref[at, :].astype(F32))
            scaled_ref[at, :] = scaled.astype(BF16)
            normed_ref[at, :] = (scaled * rows_ref[0:1, :] + rows_ref[1:2, :]).astype(BF16)
        mixed = dot_nn(normed_ref[at, :], weight_ref[...]) + bias_row
        qkv_ref[at, :] = mixed.astype(BF16)
    lane = lax.broadcasted_iota(jnp.int32, (seq, LANES), 1)
    bias = jnp.where(live_ref[...] > 0, 0.0, MASKED_SCORE).astype(F32)
    key_rows = qkv_ref[:, LANES : 2 * LANES].astype(F32)
    value_rows = qkv_ref[:, 2 * LANES : 3 * LANES].astype(F32)
    for head in range(2):
        own = (lane // HEAD_DIM) == head
        spare = HEAD_DIM * (1 - head)
        extra = jnp.where(lane == spare, bias, 0.0)
        key_ref[head] = jnp.where(own, key_rows, extra).astype(BF16)
        extra = jnp.where(lane == spare, 1.0, 0.0)
        value_ref[head] = jnp.where(own, value_rows, extra).astype(BF16)
    for low, count in tiles_of(seq, TILE):
        at = slice(low, low + count)
        lane = lax.broadcasted_iota(jnp.int32, (count, LANES), 1)
        queries = qkv_ref[at, 0:LANES].astype(F32) * SCORE_SCALE
        both = None
        for head in range(2):
            own = (lane // HEAD_DIM) == head
            spare = HEAD_DIM * (1 - head)
            extra = jnp.where(lane == spare, 1.0, 0.0)
            mine = jnp.where(own, queries, extra).astype(BF16)
            scores = dot_nt(mine, key_ref[head])
            highest = jnp.max(scores, axis=-1, keepdims=True)
            weights = jnp.exp(scores - highest).astype(BF16)
            output = dot_nn(weights, value_ref[head])
            summed = output[:, spare : spare + 1]
            output = output / summed
            both = output if head == 0 else jnp.where(own, output, both)
            rest = -(highest + jnp.log(summed))
            extra = jnp.where(lane == spare + 3, 1.0, 0.0)
            for place in range(3):
                part = rest.astype(BF16).astype(F32)
                extra = jnp.where(lane == spare + place, part, extra)
                rest = rest - part
            query_ref[at, LANES * head : LANES * (head + 1)] = jnp.where(
                own, queries, extra
            ).astype(BF16)
        attended_ref[at, :] = both.astype(BF16)


def attend(pair, ids, live, near, far, normed, rows=None, after=()):
    seq, features = normed.shape
    outs = [
        shape_of((features, 3 * LANES), BF16),
        shape_of((seq, 3 * LANES), BF16),
        shape_of((seq, LANES), BF16),
        shape_of((seq, 2 * LANES), BF16),
    ]
    scratch = [pltpu.VMEM((2, seq, LANES), BF16), pltpu.VMEM((2, seq, LANES), BF16)]
    args = (live, near, far, normed)
    if pair == 0:
        outs = [shape_of((16, features), F32)] + [shape_of((seq, features), BF16)] * 2 + outs
        scratch.append(pltpu.VMEM((features, LANES), F32))
    else:
        args += (rows,)
    return plain(
        functools.partial(attend_kernel, pair),
        ids,
        args,
        outs,
        f"attend_{pair}",
        cost=(LONG * 160 * seq * seq * HEAD_DIM, 0, 0),
        vmem=LARGE,
        scratch=scratch,
        after=after,
    )


def attend_back_kernel(
    ids_ref,
    live_ref,
    qkv_ref,
    query_ref,
    attended_ref,
    mine_a,
    other_a,
    mine_b,
    other_b,
    out_ref,
    mixed_ref,
    sums_ref,
    grad_ref,
    held_ref,
    query_sum_ref,
):
    seq = qkv_ref.shape[0]
    rows = mine_a.shape[0]
    core = ids_ref[2]
    for index, ref in enumerate((mine_a, other_a, mine_b, other_b)):
        block = 2 * (index // 2) + lax.bitwise_xor(core, index % 2)
        grad_ref[pl.ds(pl.multiple_of(block * rows, 8), rows), :] = dot_nn(ref[...], out_ref[...])
    lane = lax.broadcasted_iota(jnp.int32, (seq, LANES), 1)
    grad = grad_ref[...].astype(BF16).astype(F32)
    product = grad * attended_ref[...].astype(F32)
    for head in range(2):
        own = (lane // HEAD_DIM) == head
        spare = HEAD_DIM * (1 - head)
        inner = -jnp.sum(jnp.where(own, product, 0.0), axis=-1, keepdims=True)
        first = inner.astype(BF16).astype(F32)
        extra = jnp.where(lane == spare, first, jnp.where(lane == spare + 1, inner - first, 0.0))
        held_ref[head] = jnp.where(own, grad, extra).astype(BF16)
    value_sum = jnp.zeros((1, LANES), F32)
    for index, (low, count) in enumerate(tiles_of(seq, TILE)):
        at = slice(low, low + count)
        lane = lax.broadcasted_iota(jnp.int32, (count, LANES), 1)
        bias = jnp.where(live_ref[at, :] > 0, 0.0, MASKED_SCORE).astype(F32)
        key_rows = qkv_ref[at, LANES : 2 * LANES].astype(F32)
        value_rows = qkv_ref[at, 2 * LANES : 3 * LANES].astype(F32)
        grad_keys = grad_values = None
        for head in range(2):
            own = (lane // HEAD_DIM) == head
            spare = HEAD_DIM * (1 - head)
            ones = jnp.where((lane >= spare) & (lane < spare + 3), 1.0, 0.0)
            extra = jnp.where(lane == spare + 3, bias, ones)
            keys = jnp.where(own, key_rows, extra).astype(BF16)
            values = jnp.where(own, value_rows, ones).astype(BF16)
            queries = query_ref[:, LANES * head : LANES * (head + 1)]
            above = held_ref[head]
            weights = jnp.exp(dot_nt(keys, queries))
            grad_scores = (weights * dot_nt(values, above)).astype(BF16)
            value_part = dot_nn(weights.astype(BF16), above)
            key_part = dot_nn(grad_scores, queries)
            part = slice(HEAD_DIM * head, HEAD_DIM * (head + 1))
            query_part = dot_tn(keys, grad_scores)[part]
            if index == 0:
                query_sum_ref[part] = query_part
            else:
                query_sum_ref[part] += query_part
            grad_keys = key_part if head == 0 else jnp.where(own, key_part, grad_keys)
            grad_values = value_part if head == 0 else jnp.where(own, value_part, grad_values)
        grad_values = grad_values.astype(BF16)
        mixed_ref[at, LANES : 2 * LANES] = grad_keys.astype(BF16)
        mixed_ref[at, 2 * LANES : 3 * LANES] = grad_values
        value_sum += jnp.sum(grad_values.astype(F32), axis=0, keepdims=True)
    grad_queries = (query_sum_ref[...].T * SCORE_SCALE).astype(BF16)
    mixed_ref[:, 0:LANES] = grad_queries
    sums_ref[0:1, :] = jnp.sum(grad_queries.astype(F32), axis=0, keepdims=True)
    sums_ref[1:2, :] = value_sum


def attend_back(pair, ids, live, qkv, queries, attended, grads, out_own, after=()):
    seq = qkv.shape[0]
    features = out_own.shape[0]
    outs = [shape_of((seq, 3 * LANES), BF16), shape_of((8, LANES), F32)]
    args = (live, qkv, queries, attended, *grads)
    return call(
        attend_back_kernel,
        ids,
        (*args, out_own),
        [whole(a) for a in args] + [pl.BlockSpec((features, LANES), lambda i, _: (0, pair))],
        outs,
        [whole(o) for o in outs],
        f"attend_back_{pair}",
        cost=(LONG * 80 * seq * seq * HEAD_DIM, 0, 0),
        vmem=LARGE,
        scratch=[
            pltpu.VMEM((seq, LANES), F32),
            pltpu.VMEM((2, seq, LANES), BF16),
            pltpu.VMEM((LANES, seq), F32),
        ],
        after=after,
    )


def middle_kernel(ids_ref, x_ref, *refs):
    att_refs, out_refs = refs[:8], refs[8:12]
    rows_ref, expand_ref, contract_ref, bias_ref, top_ref = refs[12:17]
    outs = refs[-14:-4]
    normed_ref, act_ref, hidden_ref, grad_ref = outs[:4]
    branch_refs, attn_ref, back_refs, sums_ref = outs[4:6], outs[6], outs[7:9], outs[9]
    held_ref, normed_held, act_held, hidden_held = refs[-4:]
    step = pl.program_id(0)

    @pl.when(step == 0)
    def _():
        sums_ref[...] = jnp.zeros_like(sums_ref)

    attn_sum = rows_ref[4:5, :]
    for device, out_ref in enumerate(out_refs):
        held_ref[:, :LANES] = att_refs[2 * device][0]
        held_ref[:, LANES:] = att_refs[2 * device + 1][0]
        attn_sum = attn_sum + dot_nt(held_ref[...], out_ref[...])

    @pl.when(step == 1)
    def _():
        attn_ref[...] = attn_sum.astype(BF16)

    residual = x_ref[0].astype(F32) + rows_ref[5:6, :] * attn_sum
    scaled, _ = norm_forward(residual)
    normed_held[...] = (scaled * rows_ref[6:7, :] + rows_ref[7:8, :]).astype(BF16)
    normed_ref[0] = normed_held[...]
    grad_ref[0] = (top_ref[0].astype(F32) * rows_ref[9:10, :]).astype(BF16)
    for low in range(0, act_held.shape[1], CHUNK):
        at = slice(low, low + CHUNK)
        activated, slope = gelu_parts(dot_nn(normed_held[...], expand_ref[:, at]) + bias_ref[:, at])
        act_held[:, at] = activated.astype(BF16)
        grad_hidden = (dot_nn(grad_ref[0], contract_ref[:, at]) * slope).astype(BF16)
        hidden_held[:, at] = grad_hidden
        sums_ref[0:1, at] += jnp.sum(grad_hidden.astype(F32), axis=0, keepdims=True)
    act_ref[0] = act_held[...]
    hidden_ref[0] = hidden_held[...]
    back = dot_nt(hidden_held[...], expand_ref[...])
    sums_ref[1:2, :] += jnp.sum(back * scaled, axis=0, keepdims=True)
    sums_ref[2:3, :] += jnp.sum(back, axis=0, keepdims=True)
    branch = dot_nt(act_held[...], contract_ref[...]).astype(BF16)
    for index in range(2):

        @pl.when(step == index)
        def _():
            back_refs[index][...] = back.astype(BF16)
            branch_refs[index][0] = branch


def middle(half, ids, x_full, att, out_all, rows, weights, bias, top_full, before=(), after=()):
    _, count, features = x_full.shape
    hidden = weights.shape[1] // 2
    block = lambda i, ids_ref: 2 * half + lax.bitwise_xor(ids_ref[2], 1 - i)
    part = lambda n: pl.BlockSpec((1, count, n), lambda i, ids_ref: (block(i, ids_ref), 0, 0))
    held = lambda n: pl.BlockSpec((1, count, n), lambda i, _: (half, 0, 0))
    column = lambda c: pl.BlockSpec((features, hidden), lambda i, _: (0, c))
    full = lambda n: shape_of((4, count, n), BF16)
    outs = [full(features), full(hidden), full(hidden), full(features)]
    specs = [part(features), part(hidden), part(hidden), part(features)]
    outs += [shape_of((2, count, features), BF16)] * 2
    specs += [held(features)] * 2
    rest = [
        shape_of((count, features), BF16),
        shape_of((count, features), BF16),
        shape_of((count, features), BF16),
        shape_of((8, features), F32),
    ]
    args = (x_full, *att, *out_all, rows, weights, weights, bias, top_full)
    seq = 2 * count
    results = call(
        middle_kernel,
        ids,
        (*args, *before),
        [part(features)]
        + [part(LANES)] * len(att)
        + [whole(o) for o in out_all]
        + [whole(rows), column(0), column(1), whole(bias), part(features)]
        + [ANYWHERE] * len(before),
        outs + rest,
        specs + [whole(o) for o in rest],
        f"middle_{half}",
        (2 * seq * features * (features + 4 * hidden), seq * 24 * features + 6 * features * hidden, 2 * seq * hidden),
        grid=(2,),
        scratch=[pltpu.VMEM((count, 2 * LANES), BF16)] + [pltpu.VMEM((count, features), BF16)] * 3,
        aliases={1 + len(args) + index: index for index in range(len(before))},
        after=after,
        vmem=ALL,
    )
    return results[:6], results[6:]


def pair_sum_kernel(ids_ref, keep_ref, arrived_ref, sum_ref):
    sum_ref[...] = (keep_ref[...].astype(F32) + arrived_ref[...].astype(F32)).astype(BF16)


def pair_sum(ids, keep, arrived, name, after=()):
    outs = [shape_of(keep.shape, BF16)]
    return plain(pair_sum_kernel, ids, (keep, arrived), outs, name, after=after)[0]


def split_sum_kernel(ids_ref, keep_ref, arrived_ref, give_ref, stay_ref):
    half = ids_ref[3]
    total = keep_ref[...].astype(F32) + arrived_ref[...].astype(F32)
    give_ref[...] = jnp.where(half == 0, total[1], total[0]).astype(BF16)
    stay_ref[...] = jnp.where(half == 0, total[0], total[1]).astype(BF16)


def split_sum(ids, keep, arrived, name, after=()):
    outs = [shape_of(keep.shape[1:], BF16)] * 2
    return plain(split_sum_kernel, ids, (keep, arrived), outs, name, after=after)


def residual_kernel(ids_ref, chip_ref, arrived_ref, x_ref, attn_ref, top_ref, rows_ref, grad_ref, residual_ref):
    total = chip_ref[...].astype(F32) + arrived_ref[...].astype(F32)
    attn_sum = attn_ref[...].astype(F32)
    scaled, inverse = norm_forward(x_ref[0].astype(F32) + rows_ref[5:6, :] * attn_sum)
    grad = top_ref[0].astype(F32) + norm_backward(scaled, inverse, total, rows_ref[6:7, :])
    residual_ref[...] = grad.astype(BF16)
    grad_ref[...] = (grad * rows_ref[5:6, :]).astype(BF16)


def residual_back(half, ids, chip, arrived, x_full, attn, top_full, rows, after=()):
    count, features = chip.shape
    part = pl.BlockSpec((1, count, features), lambda i, ids_ref: (2 * half + ids_ref[2], 0, 0))
    outs = [shape_of((count, features), BF16)] * 2
    return call(
        residual_kernel,
        ids,
        (chip, arrived, x_full, attn, top_full, rows),
        [whole(chip), whole(arrived), part, whole(attn), part, whole(rows)],
        outs,
        [whole(out) for out in outs],
        f"residual_back_{half}",
        after=after,
        vmem=ALL,
    )


def own_kernel(
    ids_ref, x_ref, top_ref, attn_a, attn_b, grad_a, grad_b, stay_ref, branch_ref, rows_ref, output_ref, sums_ref
):
    first = ids_ref[3] == 0
    choose = lambda a, b: jnp.where(first, a[...].astype(F32), b[...].astype(F32))
    attn_sum = choose(attn_a, attn_b)
    grad = choose(grad_a, grad_b)
    branch = stay_ref[...].astype(F32) + branch_ref[...].astype(F32) + rows_ref[8:9, :]
    output_ref[:, 0, :] = x_ref[0].astype(F32) + rows_ref[5:6, :] * attn_sum + rows_ref[9:10, :] * branch
    top = top_ref[0].astype(F32)
    for row, values in enumerate((grad * rows_ref[5:6, :], grad * attn_sum, top * rows_ref[9:10, :], top * branch)):
        sums_ref[row : row + 1, :] = jnp.sum(values, axis=0, keepdims=True)


def own_block(ids, x_full, top_full, attn, grads, stay, branch, rows, after=()):
    _, count, features = x_full.shape
    part = pl.BlockSpec((1, count, features), lambda i, ids_ref: (ids_ref[1], 0, 0))
    outs = [shape_of((count, 1, features), F32), shape_of((8, features), F32)]
    rest = (*attn, *grads, stay, branch, rows)
    return call(
        own_kernel,
        ids,
        (x_full, top_full, *rest),
        [part, part] + [whole(a) for a in rest],
        outs,
        [whole(o) for o in outs],
        "own_block",
        after=after,
        vmem=24,
    )


def matrices_kernel(ids_ref, left_a, left_b, right_a, right_b, out_ref, flat_ref):
    step = pl.program_id(0)
    per = pl.num_programs(0) // 2

    @pl.when(step == 0)
    def _():
        flat_ref[...] = left_a[...].T

    @pl.when(step == per)
    def _():
        flat_ref[...] = left_b[...].T

    right = jnp.where(step < per, right_a[...], right_b[...])
    out_ref[...] = dot_nn(flat_ref[...], right).astype(BF16)


def matrices(ids, normed, hidden, grad, activated, after=()):
    seq, features = normed.shape
    width = hidden.shape[1]
    block = 512
    per = width // block
    out = shape_of((features, 2 * width), BF16)
    return call(
        matrices_kernel,
        ids,
        (normed, grad, hidden, activated),
        [
            whole(normed),
            whole(grad),
            pl.BlockSpec((seq, block), lambda i, _: (0, jnp.minimum(i, per - 1))),
            pl.BlockSpec((seq, block), lambda i, _: (0, jnp.maximum(i - per, 0))),
        ],
        [out],
        [pl.BlockSpec((features, block), lambda i, _: (0, i))],
        "matrices",
        grid=(2 * per,),
        scratch=[pltpu.VMEM((features, seq), BF16)],
        after=after,
        vmem=ALL,
    )[0]


def store_shards(ids_ref, index, values, give_ref, keep_ref):
    @pl.when(low_bit(ids_ref) == index % 2)
    def _():
        keep_ref[index // 2] = values

    @pl.when(low_bit(ids_ref) != index % 2)
    def _():
        give_ref[index // 2] = values


def out_grad_kernel(ids_ref, att_a, att_b, mine_a, other_a, mine_b, other_b, give_ref, keep_ref):
    core = ids_ref[2]
    total = [None, None]
    for index, ref in enumerate((mine_a, other_a, mine_b, other_b)):
        block = 2 * (index // 2) + lax.bitwise_xor(core, index % 2)
        for pair, att_ref in enumerate((att_a, att_b)):
            part = dot_tn(att_ref[block], ref[...])
            total[pair] = part if index == 0 else total[pair] + part
    count, _, shard = give_ref.shape
    for place in range(2 * count):
        values = jnp.concatenate([t[:, place * shard : (place + 1) * shard] for t in total]).astype(BF16)
        store_shards(ids_ref, place, values, give_ref, keep_ref)


def out_grad(ids, attended, grads, places, after=()):
    count, features = grads[0].shape
    outs = [shape_of((places // 2, 2 * LANES, features // places), BF16)] * 2
    args = [a.reshape(4, count, LANES) for a in attended] + list(grads)
    return plain(out_grad_kernel, ids, args, outs, "out_grad", after=after)


def in_grad_kernel(ids_ref, flat_ref, mixed_ref, *refs):
    give_ref, keep_ref = refs[-2:]
    count, held, width = give_ref.shape
    values = dot_nn(flat_ref[...], mixed_ref[...]).astype(BF16)
    shard = values.shape[0] // (2 * count)
    for place in range(2 * count):
        at = slice(place * shard, (place + 1) * shard)
        part = values[at]
        if held > shard:
            below = refs[0][:, at].astype(BF16)
            below = jnp.concatenate([below, jnp.zeros((held - shard, width - shard), BF16)], axis=1)
            part = jnp.concatenate([part, below])
        store_shards(ids_ref, place, part, give_ref, keep_ref)


def in_grad(pair, ids, flat, mixed, places, after=(), small=None):
    features = flat.shape[0]
    held = features // places + (0 if small is None else small.shape[0])
    outs = [shape_of((places // 2, held, mixed.shape[1]), BF16)] * 2
    args = (flat, mixed) if small is None else (flat, mixed, small)
    return plain(in_grad_kernel, ids, args, outs, f"in_grad_{pair}", after=after)


def low_sum_kernel(ids_ref, keep_ref, arrived_ref, *out_refs):
    high = lax.div(ids_ref[0], 2)
    for step, out_ref in enumerate(out_refs):
        at = lax.bitwise_xor(high, step)
        out_ref[...] = (keep_ref[at].astype(F32) + arrived_ref[at].astype(F32)).astype(BF16)


def low_sum(ids, keep, arrived, name, after=()):
    outs = [shape_of(keep.shape[1:], BF16)] * keep.shape[0]
    return plain(low_sum_kernel, ids, (keep, arrived), outs, name, after=after)


def input_back_kernel(ids_ref, scaled_ref, mixed_a, mixed_b, weight_a, weight_b, give_ref, keep_ref, sums_ref):
    step = pl.program_id(0)

    @pl.when(step == 0)
    def _():
        sums_ref[...] = jnp.zeros_like(sums_ref)

    total = dot_nt(mixed_a[0], weight_a[...]) + dot_nt(mixed_b[0], weight_b[...])
    sums_ref[0:1, :] += jnp.sum(total * scaled_ref[0].astype(F32), axis=0, keepdims=True)
    sums_ref[1:2, :] += jnp.sum(total, axis=0, keepdims=True)

    @pl.when(step < 2)
    def _():
        give_ref[0] = total.astype(BF16)

    @pl.when(step >= 2)
    def _():
        keep_ref[0] = total.astype(BF16)


def input_back(ids, scaled, mixed, weights, after=()):
    _, count, features = scaled.shape
    width = mixed[0].shape[2]
    def part(n):
        return pl.BlockSpec(
            (1, count, n),
            lambda i, ids_ref: (2 * lax.rem(i, 2) + lax.bitwise_xor(ids_ref[2], 1 - lax.div(i, 2)), 0, 0),
        )
    outs = [shape_of((2, count, features), BF16)] * 2 + [shape_of((8, features), F32)]
    return call(
        input_back_kernel,
        ids,
        (scaled, *mixed, *weights),
        [part(features), part(width), part(width)] + [whole(w) for w in weights],
        outs,
        [
            pl.BlockSpec((1, count, features), lambda i, _: (jnp.minimum(i, 1), 0, 0)),
            pl.BlockSpec((1, count, features), lambda i, _: (jnp.maximum(i - 2, 0), 0, 0)),
            whole(outs[2]),
        ],
        "input_back",
        grid=(4,),
        after=after,
    )


def input_kernel(ids_ref, stay_ref, arrived_ref, x_ref, grad_a, grad_b, rows_ref, out_ref):
    total = stay_ref[...].astype(F32) + arrived_ref[...].astype(F32)
    scaled, inverse = norm_forward(x_ref[0].astype(F32))
    grad = jnp.where(ids_ref[3] == 0, grad_a[...].astype(F32), grad_b[...].astype(F32))
    out_ref[:, 0, :] = grad + norm_backward(scaled, inverse, total, rows_ref[0:1, :])


def input_grad_of(ids, stay, arrived, x_full, grads, rows, after=()):
    _, count, features = x_full.shape
    part = pl.BlockSpec((1, count, features), lambda i, ids_ref: (ids_ref[1], 0, 0))
    outs = [shape_of((count, 1, features), F32)]
    return call(
        input_kernel,
        ids,
        (stay, arrived, x_full, *grads, rows),
        [whole(stay), whole(arrived), part, whole(grads[0]), whole(grads[1]), whole(rows)],
        outs,
        [whole(o) for o in outs],
        "input_grad",
        after=after,
        vmem=ALL,
    )[0]


def adam_step(master, gradient, first, second, decay):
    first_new = BETA_FIRST * first + (1.0 - BETA_FIRST) * gradient
    second_new = BETA_SECOND * second + (1.0 - BETA_SECOND) * gradient * gradient
    first_hat = first_new / (1.0 - BETA_FIRST**STEP)
    second_hat = second_new / (1.0 - BETA_SECOND**STEP)
    change = -LEARN_RATE * (first_hat / (jnp.sqrt(second_hat) + ADAM_EPS) + decay * master)
    return (change, first_new, second_new)


def adam_kernel(gradients, decay, keep_change, ids_ref, *refs):
    count = len(refs) - 7
    parts, (master, first, second), outs = refs[:count], refs[count:-4], refs[-4:]
    for at, gradient in gradients(parts):
        change, first_new, second_new = adam_step(master[at], gradient, first[at], second[at], decay)
        outs[0][at] = gradient
        outs[1][at] = change if keep_change else master[at] + change
        outs[2][at] = first_new
        outs[3][at] = second_new


def adam(gradients, decay, keep_change, ids, parts, master, first, second, name, after=()):
    outs = [shape_of(master.shape, F32)] * 4
    return plain(
        functools.partial(adam_kernel, gradients, decay, keep_change),
        ids,
        (*parts, master, first, second),
        outs,
        name,
        after=after,
        vmem=ALL,
    )


def sum_refs(refs):
    total = refs[0][...].astype(F32)
    for ref in refs[1:]:
        total = total + ref[...].astype(F32)
    return total


def high_sum_kernel(ids_ref, *refs):
    refs[-1][...] = sum_refs(refs[:-1])


def high_sum(ids, parts, name, after=()):
    out = shape_of(parts[0].shape, F32)
    return plain(high_sum_kernel, ids, parts, [out], name, after=after)[0]


def in_gradients(parts):
    totals = (parts[0][...], sum_refs(parts[1:]))
    for pair, total in enumerate(totals):
        columns = slice(pair * LANES, (pair + 1) * LANES)
        for part in range(3):
            values = total[: parts[0].shape[0], part * LANES : (part + 1) * LANES]
            yield (part, slice(None), columns), values


def out_gradients(parts):
    yield (slice(None), slice(None)), sum_refs(parts)


def expand_gradients(parts):
    yield (slice(None), slice(None)), parts[0][:, : parts[0].shape[1] // 2].astype(F32)


def contract_gradients(parts):
    yield (slice(None), slice(None)), parts[0][:, parts[0].shape[1] // 2 :].astype(F32).T


def tensor_swap(array, bit):
    return lax.ppermute(array, "tensor", [(rank, rank ^ bit) for rank in range(4)])


def fsdp_swap(array, bit):
    size = lax.axis_size("fsdp")
    return lax.ppermute(array, "fsdp", [(rank, rank ^ bit) for rank in range(size)])


def behind(array, *others):
    return lax.optimization_barrier((array,) + others)[0]


def around(array):
    across = tensor_swap(array, 2)
    return (array, tensor_swap(array, 1), across, tensor_swap(across, 1))


def gather_positions(block, rank):
    full = jnp.zeros((4,) + block.shape, block.dtype)
    for bit, piece in enumerate(around(block)):
        full = lax.dynamic_update_slice_in_dim(full, piece[None], rank ^ bit, 0)
    return full


def gather_shards(piece):
    count = lax.axis_size("fsdp") // 2
    near = jnp.stack([piece] + [fsdp_swap(piece, 2 * step) for step in range(1, count)])
    return near, fsdp_swap(near, 1)


def body(
    block_input,
    live_mask,
    cotangent,
    project_in,
    project_out,
    expand,
    contract,
    vectors,
    expand_bias,
    moment_project_in,
    second_project_in,
    moment_project_out,
    second_project_out,
    moment_expand,
    second_expand,
    moment_contract,
    second_contract,
    moment_vectors,
    second_vectors,
    moment_expand_bias,
    second_expand_bias,
):
    rows, _, features = block_input.shape
    shard, _, head_width = project_in.shape
    hidden_width = expand.shape[1]
    seq = 4 * rows
    places = lax.axis_size("fsdp")
    rank = lax.axis_index("tensor")
    place = lax.axis_index("fsdp")
    ids = jnp.stack([place, rank, rank % 2, rank // 2]).astype(jnp.int32)
    parts_first = lambda array: array.transpose(1, 0, 2)

    bias_shard = expand_bias.reshape(-1, shard)
    vector_rows = vectors.shape[0]
    small_rows = vector_rows + bias_shard.shape[0]
    small_shard = jnp.concatenate(
        [vectors, bias_shard, jnp.zeros((LANES - small_rows, shard), F32)]
    )
    packed = pack(ids, parts_first(project_in), project_out, expand, contract, small_shard)
    first_shards = gather_shards(packed[0])
    second_shards = gather_shards(behind(packed[1], first_shards[0]))
    weights = lax.all_gather(
        behind(packed[2], first_shards[0]), "fsdp", axis=0, tiled=True
    )

    x_own = block_input[:, 0]
    live_own = lax.dynamic_slice_in_dim(live_mask, rank * rows, rows, 0) > 0
    top_own = cotangent[:, 0] * live_own.astype(F32)
    x_full = gather_positions(x_own.astype(BF16), rank)
    top_full = gather_positions(behind(top_own.astype(BF16), x_full), rank)

    rows_now, normed_one, scaled_one, *heads = attend(
        0, ids, live_mask, *first_shards, x_full.reshape(seq, features)
    )
    heads = [heads]
    out_own = unpack(ids, *second_shards, after=done("attend_0"))
    heads.append(attend(1, ids, live_mask, *second_shards, normed_one, rows_now, done("unpack")))
    normed_flat = flatten(ids, normed_one, done("attend_1"))
    held = done("flatten")
    out_all = around(out_own)
    att_sets = [around(each[2]) for each in heads]
    att_all = [
        att_sets[pair][device].reshape(4, rows, LANES) for device in range(4) for pair in range(2)
    ]
    bias_now = rows_now[vector_rows:small_rows]
    bias_now = bias_now.reshape(-1, places, shard).transpose(1, 0, 2).reshape(1, -1)
    bias_here = lax.dynamic_slice_in_dim(bias_now, rank * hidden_width, hidden_width, 1)

    kept = ()
    sums, attn, chips, arrived = [], [], [], []
    grads, grads_peer = [], []
    for half in range(2):
        kept, (attn_part, back_give, back_keep, sums_part) = middle(
            half, ids, x_full, att_all, out_all, rows_now, weights, bias_here, top_full, kept, held
        )
        arrived_part = tensor_swap(back_give, 1)
        held = ()
        if half == 1:
            grads.append(
                residual_back(
                    0, ids, chips[0], arrived[0], x_full, attn[0], top_full, rows_now, done("middle_1")
                )
            )
            grads_peer.append(tensor_swap(grads[0][0], 1))
            held = done("residual_back_0")
        chip = pair_sum(ids, back_keep, arrived_part, f"back_sum_{half}", held)
        held = done(f"back_sum_{half}")
        chips.append(chip)
        arrived.append(tensor_swap(chip, 2))
        attn.append(attn_part)
        sums.append(sums_part)
    normed_two, activated, grad_hidden, grad_branch = [
        array.reshape(seq, array.shape[2]) for array in kept[:4]
    ]
    branch_give, branch_keep = kept[4:]
    sums = sums[0] + sums[1]
    grad_second = matrices(ids, normed_two, grad_hidden, grad_branch, activated, held)
    grads.append(
        residual_back(
            1, ids, chips[1], arrived[1], x_full, attn[1], top_full, rows_now, done("matrices")
        )
    )
    grads_peer.append(tensor_swap(grads[1][0], 1))
    attn_grads = (grads[0][0], grads_peer[0], grads[1][0], grads_peer[1])
    residual_grads = (grads[0][1], grads[1][1])
    second_sum = lax.psum_scatter(
        behind(grad_second, arrived[1]), "fsdp", scatter_dimension=0, tiled=True
    )

    sends = lambda low: [low[0]] + [fsdp_swap(low[step], 2 * step) for step in range(1, places // 2)]
    out_give, out_keep = out_grad(ids, [each[2] for each in heads], attn_grads, places)
    out_arrived = fsdp_swap(out_give, 1)
    branch_arrived = tensor_swap(behind(branch_give, chips[1]), 1)
    give, branch_stay = split_sum(ids, branch_keep, branch_arrived, "branch_sum", done("out_grad"))
    branch_arrived = tensor_swap(give, 2)
    mixed, head_sums = [], []
    wait = done("branch_sum")
    for pair in range(2):
        weight, qkv, attended, queries = heads[pair]
        mixed_pair, pair_sums = attend_back(
            pair, ids, live_mask, qkv, queries, attended, attn_grads, out_own, wait
        )
        mixed.append(mixed_pair)
        head_sums.append(pair_sums)
        if pair == 0:
            in_give, in_keep = in_grad(0, ids, normed_flat, mixed_pair, places)
            in_arrived = fsdp_swap(in_give, 1)
            block_output, own_sums = own_block(
                ids,
                x_full,
                top_full,
                attn,
                residual_grads,
                branch_stay,
                branch_arrived,
                rows_now,
                done("in_grad_0"),
            )
            out_low = low_sum(ids, out_keep, out_arrived, "out_low", done("own_block"))
            wait = done("out_low")
    in_low = low_sum(ids, in_keep, in_arrived, "in_low_0", done("attend_back_1"))
    in_sums = sends(in_low)
    out_sums = sends(out_low)
    input_give, input_keep, input_sums = input_back(
        ids,
        scaled_one.reshape(4, rows, features),
        [each.reshape(4, rows, each.shape[1]) for each in mixed],
        [each[0] for each in heads],
        done("in_low_0"),
    )

    lay = lambda values, start, total: lax.dynamic_update_slice_in_dim(
        jnp.zeros((total,), F32), values, start, 0
    )
    head_sums = jnp.concatenate(head_sums, axis=1)
    grad_rows = jnp.stack(
        [
            input_sums[0],
            input_sums[1],
            lay(head_sums[0], rank * head_width, features),
            lay(head_sums[1], rank * head_width, features),
            own_sums[0],
            own_sums[1],
            sums[1],
            sums[2],
            own_sums[2],
            own_sums[3],
        ]
    )
    grad_bias = lay(sums[0], rank * hidden_width, expand_bias.shape[0] * places)
    grad_bias = grad_bias.reshape(places, -1, shard).transpose(1, 0, 2).reshape(-1, features)
    small = jnp.concatenate([grad_rows, grad_bias, jnp.zeros((16 - small_rows, features), F32)])
    in_give, in_keep = in_grad(1, ids, normed_flat, mixed[1], places, (), small)
    in_arrived = fsdp_swap(in_give, 1)
    give, stay = split_sum(ids, input_keep, tensor_swap(input_give, 1), "input_sum", done("in_grad_1"))
    input_arrived = tensor_swap(give, 2)
    sum_first = high_sum(ids, in_sums, "in_sum_0", done("input_sum"))
    in_low = low_sum(
        ids, in_keep, behind(in_arrived, input_arrived), "in_low_1", done("in_sum_0")
    )
    in_sums = [sum_first] + sends(in_low)
    input_grad = input_grad_of(
        ids, stay, input_arrived, x_full, residual_grads, rows_now, done("in_low_1")
    )
    new_out = adam(
        out_gradients,
        WEIGHT_DECAY,
        True,
        ids,
        out_sums,
        project_out,
        moment_project_out,
        second_project_out,
        "adam_out",
        done("input_grad"),
    )
    second = (second_sum,)
    new_expand = adam(
        expand_gradients,
        WEIGHT_DECAY,
        False,
        ids,
        second,
        expand,
        moment_expand,
        second_expand,
        "adam_expand",
        done("adam_out"),
    )
    new_contract = adam(
        contract_gradients,
        WEIGHT_DECAY,
        False,
        ids,
        second,
        contract,
        moment_contract,
        second_contract,
        "adam_contract",
        done("adam_expand"),
    )
    new_in = adam(
        in_gradients,
        WEIGHT_DECAY,
        False,
        ids,
        in_sums,
        parts_first(project_in),
        parts_first(moment_project_in),
        parts_first(second_project_in),
        "adam_in",
        done("adam_contract"),
    )
    new_in = [parts_first(array) for array in new_in]
    small = sum(each[shard:, :shard].astype(F32) for each in in_sums[1:])
    small = behind(small, *done("adam_contract"))
    small = sum([tensor_swap(small, bit) for bit in (1, 2, 3)], small)
    grad_vectors = small[:vector_rows]
    grad_bias = small[vector_rows:small_rows].reshape(-1)
    change, first, second = adam_step(vectors, grad_vectors, moment_vectors, second_vectors, 0.0)
    new_vectors = (grad_vectors, change, first, second)
    change, first, second = adam_step(
        expand_bias, grad_bias, moment_expand_bias, second_expand_bias, 0.0
    )
    new_bias = (grad_bias, change, first, second)
    updated = (new_in, new_out, new_expand, new_contract, new_vectors, new_bias)
    return (
        block_output,
        input_grad,
        *[each[0] for each in updated],
        *[each[1] for each in updated],
        *[array for each in updated for array in each[2:]],
        grad_vectors[7],
    )


def solution(mesh):
    tokens = P("tensor", "fsdp", None)
    into = P("fsdp", None, "tensor")
    wide = P("fsdp", "tensor")
    tall = P("tensor", "fsdp")
    row = P(None, "fsdp")
    line = P("fsdp")
    params = (into, tall, wide, tall, row, line)
    moments = (into, into, tall, tall, wide, wide, tall, tall, row, row, line, line)
    return jax.shard_map(
        body,
        mesh=mesh,
        in_specs=(tokens, row, tokens) + params + moments,
        out_specs=(tokens, tokens) + params + params + moments + (line,),
        check_vma=False,
    )
```

```python
import functools

import jax
import jax.numpy as jnp
from jax import lax
from jax.experimental import pallas as pl
from jax.experimental.pallas import tpu as pltpu
from jax.sharding import PartitionSpec as P

HEAD_DIM = 64
STEP = 3
NORM_EPS = 1e-06
BETA_FIRST = 0.9
BETA_SECOND = 0.999
LEARN_RATE = 0.004
WEIGHT_DECAY = 0.04
ADAM_EPS = 1e-08
MASKED_SCORE = -1e30
ROOT_HALF = 0.7071067811865476
DENSITY_NORM = 0.3989422804014327
SCORE_SCALE = HEAD_DIM ** (-0.5)
LANES = 128
TILE = 512
CHUNK = 256
LONG = 4
SMALL = 16
LARGE = 32
ALL = 56
TOKENS = {}
F32 = jnp.float32
BF16 = jnp.bfloat16


def dot_nn(left, right):
    return lax.dot_general(left, right, (((1,), (0,)), ((), ())), preferred_element_type=F32)


def dot_nt(left, right):
    return lax.dot_general(left, right, (((1,), (1,)), ((), ())), preferred_element_type=F32)


def dot_tn(left, right):
    return lax.dot_general(left, right, (((0,), (0,)), ((), ())), preferred_element_type=F32)


def tiles_of(total, tile):
    return [(low, min(tile, total - low)) for low in range(0, total, tile)]


def norm_forward(values):
    center = jnp.mean(values, axis=-1, keepdims=True)
    offset = values - center
    spread = jnp.mean(offset * offset, axis=-1, keepdims=True)
    inverse = lax.rsqrt(spread + NORM_EPS)
    return offset * inverse, inverse


def norm_backward(scaled, inverse, grad_normed, norm_gain):
    grad_scaled = grad_normed * norm_gain
    first_mean = jnp.mean(grad_scaled, axis=-1, keepdims=True)
    second_mean = jnp.mean(grad_scaled * scaled, axis=-1, keepdims=True)
    return inverse * (grad_scaled - first_mean - scaled * second_mean)


def gelu_parts(hidden):
    normal_cdf = 0.5 * (1.0 + lax.erf(hidden * ROOT_HALF))
    density = DENSITY_NORM * jnp.exp(-0.5 * hidden * hidden)
    return (hidden * normal_cdf, normal_cdf + hidden * density)


def call(kernel, ids, args, in_specs, outs, out_specs, name, cost=(0, 0, 0), grid=(1,), scratch=(), aliases=None, after=(), vmem=SMALL):
    count = 1 + len(args)
    waits = len(after)
    token = shape_of((8, LANES), F32)

    def run(*refs):
        place = count + waits + len(outs)
        refs[place][...] = jnp.zeros_like(refs[place])
        kernel(*refs[:count], *refs[count + waits : place], *refs[place + 1 :])

    *results, done = pl.pallas_call(
        run,
        grid_spec=pltpu.PrefetchScalarGridSpec(
            num_scalar_prefetch=1,
            grid=grid,
            in_specs=list(in_specs) + [pl.BlockSpec(memory_space=pl.ANY)] * waits,
            out_specs=list(out_specs) + [whole(token)],
            scratch_shapes=scratch,
        ),
        out_shape=list(outs) + [token],
        input_output_aliases=aliases or {},
        compiler_params=pltpu.CompilerParams(vmem_limit_bytes=vmem * 2**20),
        cost_estimate=pl.CostEstimate(flops=cost[0], bytes_accessed=cost[1], transcendentals=cost[2]),
        name=name,
    )(ids, *args, *after)
    TOKENS[name] = done
    return results


def done(*names):
    return tuple(TOKENS[name] for name in names)


def whole(array):
    zeros = (0,) * len(array.shape)
    return pl.BlockSpec(array.shape, lambda *i: zeros)


def plain(kernel, ids, args, outs, name, **more):
    return call(kernel, ids, args, [whole(a) for a in args], outs, [whole(o) for o in outs], name, **more)


def shape_of(shape, dtype):
    return jax.ShapeDtypeStruct(shape, dtype)


ANYWHERE = pl.BlockSpec(memory_space=pl.ANY)


def low_bit(ids_ref):
    return lax.rem(ids_ref[0], 2)


def pack_kernel(ids_ref, in_ref, out_ref, expand_ref, contract_ref, small_ref, first, second, third):
    for pair, packed in enumerate((first, second)):
        for part in range(3):
            packed[:, part * LANES : (part + 1) * LANES] = in_ref[
                part, :, pair * LANES : (pair + 1) * LANES
            ].astype(BF16)
    first[:, 3 * LANES :] = small_ref[...].T.astype(BF16)
    second[:, 3 * LANES :] = out_ref[...].T.astype(BF16)
    hidden = expand_ref.shape[1]
    third[:, :hidden] = expand_ref[...].astype(BF16)
    third[:, hidden:] = contract_ref[...].T.astype(BF16)


def pack(ids, project_in, project_out, expand, contract, small):
    _, shard, head_width = project_in.shape
    widths = (4 * LANES, 3 * LANES + head_width, 2 * expand.shape[1])
    args = (project_in, project_out, expand, contract, small)
    outs = [shape_of((shard, width), BF16) for width in widths]
    return plain(pack_kernel, ids, args, outs, "pack", vmem=ALL)


def place_rows(ids_ref, near_ref, far_ref, write):
    count, shard = near_ref.shape[0], near_ref.shape[1]
    mine = ids_ref[0]
    for step in range(count):
        for low, ref in enumerate((near_ref, far_ref)):
            owner = lax.bitwise_xor(mine, 2 * step + low)
            write(pl.ds(pl.multiple_of(owner * shard, shard), shard), ref[step])


def flatten_kernel(ids_ref, normed_ref, flat_ref):
    flat_ref[...] = normed_ref[...].T


def flatten(ids, normed, after=()):
    seq, features = normed.shape
    return plain(flatten_kernel, ids, (normed,), [shape_of((features, seq), BF16)], "flatten", after=after)[0]


def unpack_kernel(ids_ref, near_ref, far_ref, out_ref):
    def write(at, values):
        out_ref[at, :] = values[:, 3 * LANES :]

    place_rows(ids_ref, near_ref, far_ref, write)


def unpack(ids, near, far, after=()):
    count, shard, width = near.shape
    outs = [shape_of((2 * count * shard, width - 3 * LANES), BF16)]
    return plain(unpack_kernel, ids, (near, far), outs, "unpack", after=after)[0]


def attend_kernel(pair, ids_ref, live_ref, near_ref, far_ref, normed_ref, *refs):
    if pair == 0:
        x_ref = normed_ref
        rows_ref, normed_ref, scaled_ref, held_ref = refs[0], refs[1], refs[2], refs[-1]
        weight_ref, qkv_ref, attended_ref, query_ref, key_ref, value_ref = refs[3:-1]
    else:
        rows_ref, weight_ref, qkv_ref, attended_ref, query_ref, key_ref, value_ref = refs
    seq = normed_ref.shape[0]
    width = 3 * LANES

    def write(at, values):
        weight_ref[at, :] = values[:, :width]
        if pair == 0:
            held_ref[at, :] = values[:, width:].astype(F32)

    place_rows(ids_ref, near_ref, far_ref, write)
    if pair == 0:
        rows_ref[...] = held_ref[...].T[0 : rows_ref.shape[0]]
    start = pl.multiple_of(ids_ref[1] * (2 * LANES) + pair * LANES, LANES)
    bias_row = jnp.concatenate(
        [rows_ref[2:3, pl.ds(start, LANES)], jnp.zeros((1, LANES), F32), rows_ref[3:4, pl.ds(start, LANES)]],
        axis=1,
    )
    for low, count in tiles_of(seq, TILE):
        at = slice(low, low + count)
        if pair == 0:
            scaled, _ = norm_forward(x_ref[at, :].astype(F32))
            scaled_ref[at, :] = scaled.astype(BF16)
            normed_ref[at, :] = (scaled * rows_ref[0:1, :] + rows_ref[1:2, :]).astype(BF16)
        mixed = dot_nn(normed_ref[at, :], weight_ref[...]) + bias_row
        qkv_ref[at, :] = mixed.astype(BF16)
    lane = lax.broadcasted_iota(jnp.int32, (seq, LANES), 1)
    bias = jnp.where(live_ref[...] > 0, 0.0, MASKED_SCORE).astype(F32)
    key_rows = qkv_ref[:, LANES : 2 * LANES].astype(F32)
    value_rows = qkv_ref[:, 2 * LANES : 3 * LANES].astype(F32)
    for head in range(2):
        own = (lane // HEAD_DIM) == head
        spare = HEAD_DIM * (1 - head)
        extra = jnp.where(lane == spare, bias, 0.0)
        key_ref[head] = jnp.where(own, key_rows, extra).astype(BF16)
        extra = jnp.where(lane == spare, 1.0, 0.0)
        value_ref[head] = jnp.where(own, value_rows, extra).astype(BF16)
    for low, count in tiles_of(seq, TILE):
        at = slice(low, low + count)
        lane = lax.broadcasted_iota(jnp.int32, (count, LANES), 1)
        queries = qkv_ref[at, 0:LANES].astype(F32) * SCORE_SCALE
        both = None
        for head in range(2):
            own = (lane // HEAD_DIM) == head
            spare = HEAD_DIM * (1 - head)
            extra = jnp.where(lane == spare, 1.0, 0.0)
            mine = jnp.where(own, queries, extra).astype(BF16)
            scores = dot_nt(mine, key_ref[head])
            highest = jnp.max(scores, axis=-1, keepdims=True)
            weights = jnp.exp(scores - highest).astype(BF16)
            output = dot_nn(weights, value_ref[head])
            summed = output[:, spare : spare + 1]
            output = output / summed
            both = output if head == 0 else jnp.where(own, output, both)
            rest = -(highest + jnp.log(summed))
            extra = jnp.where(lane == spare + 3, 1.0, 0.0)
            for place in range(3):
                part = rest.astype(BF16).astype(F32)
                extra = jnp.where(lane == spare + place, part, extra)
                rest = rest - part
            query_ref[at, LANES * head : LANES * (head + 1)] = jnp.where(
                own, queries, extra
            ).astype(BF16)
        attended_ref[at, :] = both.astype(BF16)


def attend(pair, ids, live, near, far, normed, rows=None, after=()):
    seq, features = normed.shape
    outs = [
        shape_of((features, 3 * LANES), BF16),
        shape_of((seq, 3 * LANES), BF16),
        shape_of((seq, LANES), BF16),
        shape_of((seq, 2 * LANES), BF16),
    ]
    scratch = [pltpu.VMEM((2, seq, LANES), BF16), pltpu.VMEM((2, seq, LANES), BF16)]
    args = (live, near, far, normed)
    if pair == 0:
        outs = [shape_of((16, features), F32)] + [shape_of((seq, features), BF16)] * 2 + outs
        scratch.append(pltpu.VMEM((features, LANES), F32))
    else:
        args += (rows,)
    return plain(
        functools.partial(attend_kernel, pair),
        ids,
        args,
        outs,
        f"attend_{pair}",
        cost=(LONG * 160 * seq * seq * HEAD_DIM, 0, 0),
        vmem=LARGE,
        scratch=scratch,
        after=after,
    )


def attend_back_kernel(
    ids_ref,
    live_ref,
    qkv_ref,
    query_ref,
    attended_ref,
    mine_a,
    other_a,
    mine_b,
    other_b,
    out_ref,
    mixed_ref,
    sums_ref,
    grad_ref,
    held_ref,
    query_sum_ref,
):
    seq = qkv_ref.shape[0]
    rows = mine_a.shape[0]
    core = ids_ref[2]
    for index, ref in enumerate((mine_a, other_a, mine_b, other_b)):
        block = 2 * (index // 2) + lax.bitwise_xor(core, index % 2)
        grad_ref[pl.ds(pl.multiple_of(block * rows, 8), rows), :] = dot_nn(ref[...], out_ref[...])
    lane = lax.broadcasted_iota(jnp.int32, (seq, LANES), 1)
    grad = grad_ref[...].astype(BF16).astype(F32)
    product = grad * attended_ref[...].astype(F32)
    for head in range(2):
        own = (lane // HEAD_DIM) == head
        spare = HEAD_DIM * (1 - head)
        inner = -jnp.sum(jnp.where(own, product, 0.0), axis=-1, keepdims=True)
        first = inner.astype(BF16).astype(F32)
        extra = jnp.where(lane == spare, first, jnp.where(lane == spare + 1, inner - first, 0.0))
        held_ref[head] = jnp.where(own, grad, extra).astype(BF16)
    value_sum = jnp.zeros((1, LANES), F32)
    for index, (low, count) in enumerate(tiles_of(seq, TILE)):
        at = slice(low, low + count)
        lane = lax.broadcasted_iota(jnp.int32, (count, LANES), 1)
        bias = jnp.where(live_ref[at, :] > 0, 0.0, MASKED_SCORE).astype(F32)
        key_rows = qkv_ref[at, LANES : 2 * LANES].astype(F32)
        value_rows = qkv_ref[at, 2 * LANES : 3 * LANES].astype(F32)
        grad_keys = grad_values = None
        for head in range(2):
            own = (lane // HEAD_DIM) == head
            spare = HEAD_DIM * (1 - head)
            ones = jnp.where((lane >= spare) & (lane < spare + 3), 1.0, 0.0)
            extra = jnp.where(lane == spare + 3, bias, ones)
            keys = jnp.where(own, key_rows, extra).astype(BF16)
            values = jnp.where(own, value_rows, ones).astype(BF16)
            queries = query_ref[:, LANES * head : LANES * (head + 1)]
            above = held_ref[head]
            weights = jnp.exp(dot_nt(keys, queries))
            grad_scores = (weights * dot_nt(values, above)).astype(BF16)
            value_part = dot_nn(weights.astype(BF16), above)
            key_part = dot_nn(grad_scores, queries)
            part = slice(HEAD_DIM * head, HEAD_DIM * (head + 1))
            query_part = dot_tn(keys, grad_scores)[part]
            if index == 0:
                query_sum_ref[part] = query_part
            else:
                query_sum_ref[part] += query_part
            grad_keys = key_part if head == 0 else jnp.where(own, key_part, grad_keys)
            grad_values = value_part if head == 0 else jnp.where(own, value_part, grad_values)
        grad_values = grad_values.astype(BF16)
        mixed_ref[at, LANES : 2 * LANES] = grad_keys.astype(BF16)
        mixed_ref[at, 2 * LANES : 3 * LANES] = grad_values
        value_sum += jnp.sum(grad_values.astype(F32), axis=0, keepdims=True)
    grad_queries = (query_sum_ref[...].T * SCORE_SCALE).astype(BF16)
    mixed_ref[:, 0:LANES] = grad_queries
    sums_ref[0:1, :] = jnp.sum(grad_queries.astype(F32), axis=0, keepdims=True)
    sums_ref[1:2, :] = value_sum


def attend_back(pair, ids, live, qkv, queries, attended, grads, out_own, after=()):
    seq = qkv.shape[0]
    features = out_own.shape[0]
    outs = [shape_of((seq, 3 * LANES), BF16), shape_of((8, LANES), F32)]
    args = (live, qkv, queries, attended, *grads)
    return call(
        attend_back_kernel,
        ids,
        (*args, out_own),
        [whole(a) for a in args] + [pl.BlockSpec((features, LANES), lambda i, _: (0, pair))],
        outs,
        [whole(o) for o in outs],
        f"attend_back_{pair}",
        cost=(80 * seq * seq * HEAD_DIM, 0, 0),
        vmem=LARGE,
        scratch=[
            pltpu.VMEM((seq, LANES), F32),
            pltpu.VMEM((2, seq, LANES), BF16),
            pltpu.VMEM((LANES, seq), F32),
        ],
        after=after,
    )


def middle_kernel(ids_ref, x_ref, *refs):
    att_refs, out_refs = refs[:8], refs[8:12]
    rows_ref, expand_ref, contract_ref, bias_ref, top_ref = refs[12:17]
    outs = refs[-14:-5]
    normed_ref, act_ref, hidden_ref = outs[:3]
    branch_refs, attn_ref, back_refs, sums_ref = outs[3:5], outs[5], outs[6:8], outs[8]
    held_ref, normed_held, act_held, hidden_held, grad_held = refs[-5:]
    step = pl.program_id(0)

    @pl.when(step == 0)
    def _():
        sums_ref[...] = jnp.zeros_like(sums_ref)

    attn_sum = rows_ref[4:5, :]
    for device, out_ref in enumerate(out_refs):
        held_ref[:, :LANES] = att_refs[2 * device][0]
        held_ref[:, LANES:] = att_refs[2 * device + 1][0]
        attn_sum = attn_sum + dot_nt(held_ref[...], out_ref[...])

    @pl.when(lax.rem(step, 2) == 1)
    def _():
        attn_ref[0] = attn_sum.astype(BF16)

    residual = x_ref[0].astype(F32) + rows_ref[5:6, :] * attn_sum
    scaled, _ = norm_forward(residual)
    normed_held[...] = (scaled * rows_ref[6:7, :] + rows_ref[7:8, :]).astype(BF16)
    normed_ref[0] = normed_held[...]
    grad_held[...] = (top_ref[0].astype(F32) * rows_ref[9:10, :]).astype(BF16)
    for low in range(0, act_held.shape[1], CHUNK):
        at = slice(low, low + CHUNK)
        activated, slope = gelu_parts(dot_nn(normed_held[...], expand_ref[:, at]) + bias_ref[:, at])
        act_held[:, at] = activated.astype(BF16)
        grad_hidden = (dot_nn(grad_held[...], contract_ref[:, at]) * slope).astype(BF16)
        hidden_held[:, at] = grad_hidden
        sums_ref[0:1, at] += jnp.sum(grad_hidden.astype(F32), axis=0, keepdims=True)
    act_ref[0] = act_held[...]
    hidden_ref[0] = hidden_held[...]
    back = dot_nt(hidden_held[...], expand_ref[...])
    sums_ref[1:2, :] += jnp.sum(back * scaled, axis=0, keepdims=True)
    sums_ref[2:3, :] += jnp.sum(back, axis=0, keepdims=True)
    branch = dot_nt(act_held[...], contract_ref[...]).astype(BF16)
    for index in range(2):

        @pl.when(lax.rem(step, 2) == index)
        def _():
            back_refs[index][0] = back.astype(BF16)
            branch_refs[index][0] = branch


def middle(ids, x_full, att, out_all, rows, weights, bias, top_full, after=()):
    _, count, features = x_full.shape
    hidden = weights.shape[1] // 2

    def block(i, ids_ref):
        return 2 * lax.div(i, 2) + lax.bitwise_xor(ids_ref[2], 1 - lax.rem(i, 2))

    part = lambda n: pl.BlockSpec((1, count, n), lambda i, ids_ref: (block(i, ids_ref), 0, 0))
    held = pl.BlockSpec((1, count, features), lambda i, _: (lax.div(i, 2), 0, 0))
    column = lambda c: pl.BlockSpec((features, hidden), lambda i, _: (0, c))
    sums = shape_of((8, features), F32)
    outs = [shape_of((4, count, n), BF16) for n in (features, hidden, hidden)]
    outs += [shape_of((2, count, features), BF16)] * 5 + [sums]
    specs = [part(features), part(hidden), part(hidden)] + [held] * 5 + [whole(sums)]
    seq = 4 * count
    return call(
        middle_kernel,
        ids,
        (x_full, *att, *out_all, rows, weights, weights, bias, top_full),
        [part(features)]
        + [part(LANES)] * len(att)
        + [whole(o) for o in out_all]
        + [whole(rows), column(0), column(1), whole(bias), part(features)],
        outs,
        specs,
        "middle",
        cost=(2 * seq * features * (features + 4 * hidden), 0, 0),
        grid=(4,),
        scratch=[pltpu.VMEM((count, 2 * LANES), BF16)] + [pltpu.VMEM((count, features), BF16)] * 4,
        after=after,
        vmem=ALL,
    )


def pair_sum_kernel(ids_ref, keep_ref, arrived_ref, sum_ref):
    sum_ref[...] = (keep_ref[...].astype(F32) + arrived_ref[...].astype(F32)).astype(BF16)


def pair_sum(half, ids, keep, arrived):
    _, count, features = keep.shape
    part = pl.BlockSpec((None, count, features), lambda i, _: (half, 0, 0))
    out = shape_of((count, features), BF16)
    return call(
        pair_sum_kernel, ids, (keep, arrived), [part, part], [out], [whole(out)], f"back_sum_{half}"
    )[0]


def split_sum_kernel(ids_ref, keep_ref, arrived_ref, give_ref, stay_ref):
    half = ids_ref[3]
    total = keep_ref[...].astype(F32) + arrived_ref[...].astype(F32)
    give_ref[...] = jnp.where(half == 0, total[1], total[0]).astype(BF16)
    stay_ref[...] = jnp.where(half == 0, total[0], total[1]).astype(BF16)


def split_sum(ids, keep, arrived, name, after=()):
    outs = [shape_of(keep.shape[1:], BF16)] * 2
    return plain(split_sum_kernel, ids, (keep, arrived), outs, name, after=after)


def residual_kernel(ids_ref, chip_ref, arrived_ref, x_ref, attn_ref, top_ref, rows_ref, grad_ref, residual_ref):
    total = chip_ref[...].astype(F32) + arrived_ref[...].astype(F32)
    attn_sum = attn_ref[...].astype(F32)
    scaled, inverse = norm_forward(x_ref[0].astype(F32) + rows_ref[5:6, :] * attn_sum)
    grad = top_ref[0].astype(F32) + norm_backward(scaled, inverse, total, rows_ref[6:7, :])
    residual_ref[...] = grad.astype(BF16)
    grad_ref[...] = (grad * rows_ref[5:6, :]).astype(BF16)


def residual_back(half, ids, chip, arrived, x_full, attn, top_full, rows, after=()):
    count, features = chip.shape
    part = pl.BlockSpec((1, count, features), lambda i, ids_ref: (2 * half + ids_ref[2], 0, 0))
    held = pl.BlockSpec((None, count, features), lambda i, _: (half, 0, 0))
    outs = [shape_of((count, features), BF16)] * 2
    return call(
        residual_kernel,
        ids,
        (chip, arrived, x_full, attn, top_full, rows),
        [whole(chip), whole(arrived), part, held, part, whole(rows)],
        outs,
        [whole(out) for out in outs],
        f"residual_back_{half}",
        after=after,
        vmem=ALL,
    )


def own_kernel(
    ids_ref, x_ref, top_ref, attn_ref, grad_a, grad_b, stay_ref, branch_ref, rows_ref, output_ref, sums_ref
):
    first = ids_ref[3] == 0
    choose = lambda a, b: jnp.where(first, a[...].astype(F32), b[...].astype(F32))
    attn_sum = attn_ref[...].astype(F32)
    grad = choose(grad_a, grad_b)
    branch = stay_ref[...].astype(F32) + branch_ref[...].astype(F32) + rows_ref[8:9, :]
    output_ref[:, 0, :] = x_ref[0].astype(F32) + rows_ref[5:6, :] * attn_sum + rows_ref[9:10, :] * branch
    top = top_ref[0].astype(F32)
    for row, values in enumerate((grad * rows_ref[5:6, :], grad * attn_sum, top * rows_ref[9:10, :], top * branch)):
        sums_ref[row : row + 1, :] = jnp.sum(values, axis=0, keepdims=True)


def own_block(ids, x_full, top_full, attn, grads, stay, branch, rows, after=()):
    _, count, features = x_full.shape
    part = pl.BlockSpec((1, count, features), lambda i, ids_ref: (ids_ref[1], 0, 0))
    outs = [shape_of((count, 1, features), F32), shape_of((8, features), F32)]
    held = pl.BlockSpec((None, count, features), lambda i, ids_ref: (ids_ref[3], 0, 0))
    rest = (*grads, stay, branch, rows)
    return call(
        own_kernel,
        ids,
        (x_full, top_full, attn, *rest),
        [part, part, held] + [whole(a) for a in rest],
        outs,
        [whole(o) for o in outs],
        "own_block",
        after=after,
        vmem=24,
    )


def matrices_kernel(ids_ref, left_a, top_ref, right_a, right_b, rows_ref, out_ref, flat_ref):
    step = pl.program_id(0)
    per = pl.num_programs(0) // 2

    @pl.when(step == 0)
    def _():
        flat_ref[...] = left_a[...].T

    @pl.when(step == per)
    def _():
        flat_ref[...] = (top_ref[...].astype(F32) * rows_ref[9:10, :]).astype(BF16).T

    right = jnp.where(step < per, right_a[...], right_b[...])
    out_ref[...] = dot_nn(flat_ref[...], right).astype(BF16)


def matrices(ids, normed, hidden, top_full, activated, rows, after=()):
    seq, features = normed.shape
    width = hidden.shape[1]
    block = 512
    per = width // block
    out = shape_of((features, 2 * width), BF16)
    top = top_full.reshape(seq, features)
    return call(
        matrices_kernel,
        ids,
        (normed, top, hidden, activated, rows),
        [
            whole(normed),
            whole(top),
            pl.BlockSpec((seq, block), lambda i, _: (0, jnp.minimum(i, per - 1))),
            pl.BlockSpec((seq, block), lambda i, _: (0, jnp.maximum(i - per, 0))),
            whole(rows),
        ],
        [out],
        [pl.BlockSpec((features, block), lambda i, _: (0, i))],
        "matrices",
        grid=(2 * per,),
        scratch=[pltpu.VMEM((features, seq), BF16)],
        after=after,
        vmem=ALL,
    )[0]


def store_shards(ids_ref, index, values, give_ref, keep_ref):
    @pl.when(low_bit(ids_ref) == index % 2)
    def _():
        keep_ref[index // 2] = values

    @pl.when(low_bit(ids_ref) != index % 2)
    def _():
        give_ref[index // 2] = values


def out_grad_kernel(ids_ref, att_a, att_b, mine_a, other_a, mine_b, other_b, give_ref, keep_ref):
    core = ids_ref[2]
    total = [None, None]
    for index, ref in enumerate((mine_a, other_a, mine_b, other_b)):
        block = 2 * (index // 2) + lax.bitwise_xor(core, index % 2)
        for pair, att_ref in enumerate((att_a, att_b)):
            part = dot_tn(att_ref[block], ref[...])
            total[pair] = part if index == 0 else total[pair] + part
    count, shard, _ = give_ref.shape
    values = jnp.concatenate([t.T for t in total], axis=1).astype(BF16)
    for place in range(2 * count):
        store_shards(ids_ref, place, values[place * shard : (place + 1) * shard], give_ref, keep_ref)


def out_grad(ids, attended, grads, places, after=()):
    count, features = grads[0].shape
    outs = [shape_of((places // 2, features // places, 2 * LANES), BF16)] * 2
    args = [a.reshape(4, count, LANES) for a in attended] + list(grads)
    return plain(out_grad_kernel, ids, args, outs, "out_grad", after=after)


def in_grad_kernel(ids_ref, flat_ref, mixed_ref, *refs):
    if len(refs) > 2:
        base_ref, input_ref, own_ref, first_ref, second_ref, give_ref, keep_ref, small_ref = refs
        small_ref[...] = base_ref[...]
        small_ref[0:2, :] = input_ref[0:2, :]
        small_ref[4:5, :] = own_ref[0:1, :]
        small_ref[5:6, :] = own_ref[1:2, :]
        small_ref[8:9, :] = own_ref[2:3, :]
        small_ref[9:10, :] = own_ref[3:4, :]
        for pair, head_ref in enumerate((first_ref, second_ref)):
            start = pl.multiple_of(ids_ref[1] * (2 * LANES) + pair * LANES, LANES)
            small_ref[2:3, pl.ds(start, LANES)] = head_ref[0:1, :]
            small_ref[3:4, pl.ds(start, LANES)] = head_ref[1:2, :]
    else:
        give_ref, keep_ref = refs
    count, held, width = give_ref.shape
    values = dot_nn(flat_ref[...], mixed_ref[...]).astype(BF16)
    shard = values.shape[0] // (2 * count)
    for place in range(2 * count):
        at = slice(place * shard, (place + 1) * shard)
        part = values[at]
        if held > shard:
            below = small_ref[:, at].astype(BF16)
            below = jnp.concatenate([below, jnp.zeros((held - shard, width - shard), BF16)], axis=1)
            part = jnp.concatenate([part, below])
        store_shards(ids_ref, place, part, give_ref, keep_ref)


def in_grad(pair, ids, flat, mixed, places, after=(), small=()):
    features = flat.shape[0]
    held, scratch = features // places, []
    if small:
        held += small[0].shape[0]
        scratch = [pltpu.VMEM(small[0].shape, F32)]
    outs = [shape_of((places // 2, held, mixed.shape[1]), BF16)] * 2
    args = (flat, mixed, *small)
    return plain(in_grad_kernel, ids, args, outs, f"in_grad_{pair}", after=after, scratch=scratch)


def low_sum_kernel(parts, ids_ref, *refs):
    out_refs = refs[2 * parts :]
    high = lax.div(ids_ref[0], 2)
    for step, out_ref in enumerate(out_refs):
        at = lax.bitwise_xor(high, step)
        low = 0
        for keep_ref, arrived_ref in zip(refs[0 : 2 * parts : 2], refs[1 : 2 * parts : 2]):
            width = keep_ref.shape[2]
            total = keep_ref[at].astype(F32) + arrived_ref[at].astype(F32)
            out_ref[:, low : low + width] = total.astype(BF16)
            low += width


def low_sum(ids, pairs, name, after=()):
    count, held, _ = pairs[0].shape
    outs = [shape_of((held, sum(a.shape[2] for a in pairs[::2])), BF16)] * count
    kernel = functools.partial(low_sum_kernel, len(pairs) // 2)
    return plain(kernel, ids, pairs, outs, name, after=after)


def input_back_kernel(ids_ref, scaled_ref, mixed_a, mixed_b, weight_a, weight_b, give_ref, keep_ref, sums_ref):
    step = pl.program_id(0)

    @pl.when(step == 0)
    def _():
        sums_ref[...] = jnp.zeros_like(sums_ref)

    total = dot_nt(mixed_a[0], weight_a[...]) + dot_nt(mixed_b[0], weight_b[...])
    sums_ref[0:1, :] += jnp.sum(total * scaled_ref[0].astype(F32), axis=0, keepdims=True)
    sums_ref[1:2, :] += jnp.sum(total, axis=0, keepdims=True)

    @pl.when(step < 2)
    def _():
        give_ref[0] = total.astype(BF16)

    @pl.when(step >= 2)
    def _():
        keep_ref[0] = total.astype(BF16)


def input_back(ids, scaled, mixed, weights, after=()):
    _, count, features = scaled.shape
    width = mixed[0].shape[2]
    def part(n):
        return pl.BlockSpec(
            (1, count, n),
            lambda i, ids_ref: (2 * lax.rem(i, 2) + lax.bitwise_xor(ids_ref[2], 1 - lax.div(i, 2)), 0, 0),
        )
    outs = [shape_of((2, count, features), BF16)] * 2 + [shape_of((8, features), F32)]
    return call(
        input_back_kernel,
        ids,
        (scaled, *mixed, *weights),
        [part(features), part(width), part(width)] + [whole(w) for w in weights],
        outs,
        [
            pl.BlockSpec((1, count, features), lambda i, _: (jnp.minimum(i, 1), 0, 0)),
            pl.BlockSpec((1, count, features), lambda i, _: (jnp.maximum(i - 2, 0), 0, 0)),
            whole(outs[2]),
        ],
        "input_back",
        grid=(4,),
        after=after,
    )


def input_kernel(ids_ref, stay_ref, arrived_ref, x_ref, grad_a, grad_b, rows_ref, out_ref):
    total = stay_ref[...].astype(F32) + arrived_ref[...].astype(F32)
    scaled, inverse = norm_forward(x_ref[0].astype(F32))
    grad = jnp.where(ids_ref[3] == 0, grad_a[...].astype(F32), grad_b[...].astype(F32))
    out_ref[:, 0, :] = grad + norm_backward(scaled, inverse, total, rows_ref[0:1, :])


def input_grad_of(ids, stay, arrived, x_full, grads, rows, after=()):
    _, count, features = x_full.shape
    part = pl.BlockSpec((1, count, features), lambda i, ids_ref: (ids_ref[1], 0, 0))
    outs = [shape_of((count, 1, features), F32)]
    return call(
        input_kernel,
        ids,
        (stay, arrived, x_full, *grads, rows),
        [whole(stay), whole(arrived), part, whole(grads[0]), whole(grads[1]), whole(rows)],
        outs,
        [whole(o) for o in outs],
        "input_grad",
        after=after,
        vmem=ALL,
    )[0]


def adam_step(master, gradient, first, second, decay):
    first_new = BETA_FIRST * first + (1.0 - BETA_FIRST) * gradient
    second_new = BETA_SECOND * second + (1.0 - BETA_SECOND) * gradient * gradient
    first_hat = first_new / (1.0 - BETA_FIRST**STEP)
    second_hat = second_new / (1.0 - BETA_SECOND**STEP)
    change = -LEARN_RATE * (first_hat / (jnp.sqrt(second_hat) + ADAM_EPS) + decay * master)
    return (change, first_new, second_new)


def adam_kernel(gradients, decay, keep_change, ids_ref, *refs):
    count = len(refs) - 7
    parts, (master, first, second), outs = refs[:count], refs[count:-4], refs[-4:]
    for at, gradient in gradients(parts):
        change, first_new, second_new = adam_step(master[at], gradient, first[at], second[at], decay)
        outs[0][at] = gradient
        outs[1][at] = change if keep_change else master[at] + change
        outs[2][at] = first_new
        outs[3][at] = second_new


def adam(gradients, decay, keep_change, ids, parts, master, first, second, name, after=()):
    outs = [shape_of(master.shape, F32)] * 4
    return plain(
        functools.partial(adam_kernel, gradients, decay, keep_change),
        ids,
        (*parts, master, first, second),
        outs,
        name,
        after=after,
        vmem=ALL,
    )


def sum_refs(refs):
    total = refs[0][...].astype(F32)
    for ref in refs[1:]:
        total = total + ref[...].astype(F32)
    return total


def high_sum_kernel(ids_ref, *refs):
    refs[-1][...] = sum_refs(refs[:-1])


def high_sum(ids, parts, name, after=()):
    out = shape_of(parts[0].shape, F32)
    return plain(high_sum_kernel, ids, parts, [out], name, after=after)[0]


def in_gradients(parts):
    totals = (parts[0][...], sum_refs(parts[1:]))
    for pair, total in enumerate(totals):
        columns = slice(pair * LANES, (pair + 1) * LANES)
        for part in range(3):
            values = total[: parts[0].shape[0], part * LANES : (part + 1) * LANES]
            yield (part, slice(None), columns), values


def out_gradients(parts):
    yield (slice(None), slice(None)), parts[0][:, 3 * LANES :].T


def expand_gradients(parts):
    yield (slice(None), slice(None)), parts[0][:, : parts[0].shape[1] // 2].astype(F32)


def contract_gradients(parts):
    yield (slice(None), slice(None)), parts[0][:, parts[0].shape[1] // 2 :].astype(F32).T


def tensor_swap(array, bit):
    return lax.ppermute(array, "tensor", [(rank, rank ^ bit) for rank in range(4)])


def fsdp_swap(array, bit):
    size = lax.axis_size("fsdp")
    return lax.ppermute(array, "fsdp", [(rank, rank ^ bit) for rank in range(size)])


def behind(array, *others):
    return lax.optimization_barrier((array,) + others)[0]


def around(array, *first):
    across = tensor_swap(array, 2)
    corner = tensor_swap(behind(across, *first) if first else across, 1)
    return (array, tensor_swap(array, 1), across, corner)


def gather_positions(block, rank, *first):
    full = jnp.zeros((4,) + block.shape, block.dtype)
    for bit, piece in enumerate(around(block, *first)):
        full = lax.dynamic_update_slice_in_dim(full, piece[None], rank ^ bit, 0)
    return full


def gather_shards(piece):
    count = lax.axis_size("fsdp") // 2
    near = jnp.stack([piece] + [fsdp_swap(piece, 2 * step) for step in range(1, count)])
    return near, fsdp_swap(near, 1)


def body(
    block_input,
    live_mask,
    cotangent,
    project_in,
    project_out,
    expand,
    contract,
    vectors,
    expand_bias,
    moment_project_in,
    second_project_in,
    moment_project_out,
    second_project_out,
    moment_expand,
    second_expand,
    moment_contract,
    second_contract,
    moment_vectors,
    second_vectors,
    moment_expand_bias,
    second_expand_bias,
):
    rows, _, features = block_input.shape
    shard, _, head_width = project_in.shape
    hidden_width = expand.shape[1]
    seq = 4 * rows
    places = lax.axis_size("fsdp")
    rank = lax.axis_index("tensor")
    place = lax.axis_index("fsdp")
    ids = jnp.stack([place, rank, rank % 2, rank // 2]).astype(jnp.int32)
    parts_first = lambda array: array.transpose(1, 0, 2)

    bias_shard = expand_bias.reshape(-1, shard)
    vector_rows = vectors.shape[0]
    small_rows = vector_rows + bias_shard.shape[0]
    small_shard = jnp.concatenate(
        [vectors, bias_shard, jnp.zeros((LANES - small_rows, shard), F32)]
    )
    packed = pack(ids, parts_first(project_in), project_out, expand, contract, small_shard)
    first_shards = gather_shards(packed[0])
    second_shards = gather_shards(behind(packed[1], first_shards[0]))
    weights = lax.all_gather(
        behind(packed[2], first_shards[0]), "fsdp", axis=0, tiled=True
    )

    x_own = block_input[:, 0]
    live_own = lax.dynamic_slice_in_dim(live_mask, rank * rows, rows, 0) > 0
    top_own = cotangent[:, 0] * live_own.astype(F32)
    x_full = gather_positions(x_own.astype(BF16), rank)
    top_full = gather_positions(behind(top_own.astype(BF16), x_full), rank)

    rows_now, normed_one, scaled_one, *heads = attend(
        0, ids, live_mask, *first_shards, x_full.reshape(seq, features)
    )
    heads = [heads]
    out_own = unpack(ids, *second_shards, after=done("attend_0"))
    heads.append(attend(1, ids, live_mask, *second_shards, normed_one, rows_now, done("unpack")))
    normed_flat = flatten(ids, normed_one, done("attend_1"))
    held = done("flatten")
    out_all = around(out_own)
    att_sets = [around(each[2]) for each in heads]
    att_all = [
        att_sets[pair][device].reshape(4, rows, LANES) for device in range(4) for pair in range(2)
    ]
    bias_now = rows_now[vector_rows:small_rows]
    bias_now = bias_now.reshape(-1, places, shard).transpose(1, 0, 2).reshape(1, -1)
    bias_here = lax.dynamic_slice_in_dim(bias_now, rank * hidden_width, hidden_width, 1)

    kept = middle(ids, x_full, att_all, out_all, rows_now, weights, bias_here, top_full, held)
    normed_two, activated, grad_hidden = [array.reshape(seq, array.shape[2]) for array in kept[:3]]
    branch_give, branch_keep, attn, back_give, back_keep, sums = kept[3:]
    back_arrived = tensor_swap(back_give, 1)
    chips, arrived, grads, grads_peer = [], [], [], []
    for half in range(2):
        chips.append(pair_sum(half, ids, back_keep, back_arrived))
        arrived.append(tensor_swap(chips[half], 2))
    grad_second = matrices(
        ids, normed_two, grad_hidden, top_full, activated, rows_now, done("back_sum_1")
    )
    for half in range(2):
        wait = done("residual_back_0" if half == 1 else "matrices")
        grads.append(
            residual_back(
                half, ids, chips[half], arrived[half], x_full, attn, top_full, rows_now, wait
            )
        )
        grads_peer.append(tensor_swap(grads[half][0], 1))
    attn_grads = (grads[0][0], grads_peer[0], grads[1][0], grads_peer[1])
    residual_grads = (grads[0][1], grads[1][1])
    second_sum = lax.psum_scatter(
        behind(grad_second, arrived[0]), "fsdp", scatter_dimension=0, tiled=True
    )

    lay = lambda values, start, total: lax.dynamic_update_slice_in_dim(
        jnp.zeros((total,), F32), values, start, 0
    )
    grad_bias = lay(sums[0], rank * hidden_width, expand_bias.shape[0] * places)
    grad_bias = grad_bias.reshape(places, -1, shard).transpose(1, 0, 2).reshape(-1, features)
    none = jnp.zeros((6, features), F32)
    small = jnp.concatenate([none, sums[1:3], none[:2], grad_bias, none[: 16 - small_rows]])

    sends = lambda low: [low[0]] + [fsdp_swap(low[step], 2 * step) for step in range(1, places // 2)]
    branch_arrived = tensor_swap(behind(branch_give, chips[1]), 1)
    give, branch_stay = split_sum(ids, branch_keep, branch_arrived, "branch_sum", done("residual_back_1"))
    branch_arrived = tensor_swap(give, 2)
    mixed, head_sums = [], []
    wait = done("branch_sum")
    for pair in range(2):
        weight, qkv, attended, queries = heads[pair]
        mixed_pair, pair_sums = attend_back(
            pair, ids, live_mask, qkv, queries, attended, attn_grads, out_own, wait
        )
        mixed.append(mixed_pair)
        head_sums.append(pair_sums)
        if pair == 0:
            in_give, in_keep = in_grad(0, ids, normed_flat, mixed_pair, places)
            in_arrived = fsdp_swap(in_give, 1)
            block_output, own_sums = own_block(
                ids,
                x_full,
                top_full,
                attn,
                residual_grads,
                branch_stay,
                branch_arrived,
                rows_now,
                done("in_grad_0"),
            )
            out_give, out_keep = out_grad(
                ids, [each[2] for each in heads], attn_grads, places, done("own_block")
            )
            out_arrived = fsdp_swap(out_give, 1)
            wait = done("out_grad") + (small,)
    first_sums = sends(
        low_sum(ids, (in_keep, in_arrived, out_keep, out_arrived), "in_low_0", done("attend_back_1"))
    )
    input_give, input_keep, input_sums = input_back(
        ids,
        scaled_one.reshape(4, rows, features),
        [each.reshape(4, rows, each.shape[1]) for each in mixed],
        [each[0] for each in heads],
        done("in_low_0"),
    )

    in_give, in_keep = in_grad(
        1, ids, normed_flat, mixed[1], places, (), (small, input_sums, own_sums, *head_sums)
    )
    in_arrived = fsdp_swap(in_give, 1)
    give, stay = split_sum(ids, input_keep, tensor_swap(input_give, 1), "input_sum", done("in_grad_1"))
    input_arrived = tensor_swap(give, 2)
    in_low = low_sum(
        ids, (in_keep, behind(in_arrived, input_arrived)), "in_low_1", done("input_sum")
    )
    second_sums = sends(in_low)
    input_grad = input_grad_of(
        ids, stay, input_arrived, x_full, residual_grads, rows_now, done("in_low_1")
    )
    sum_first = high_sum(ids, first_sums, "in_sum_0", done("input_grad"))
    in_sums = [sum_first] + second_sums
    new_out = adam(
        out_gradients,
        WEIGHT_DECAY,
        True,
        ids,
        (sum_first,),
        project_out,
        moment_project_out,
        second_project_out,
        "adam_out",
        done("in_sum_0"),
    )
    second = (second_sum,)
    new_expand = adam(
        expand_gradients,
        WEIGHT_DECAY,
        False,
        ids,
        second,
        expand,
        moment_expand,
        second_expand,
        "adam_expand",
        done("adam_out"),
    )
    new_contract = adam(
        contract_gradients,
        WEIGHT_DECAY,
        False,
        ids,
        second,
        contract,
        moment_contract,
        second_contract,
        "adam_contract",
        done("adam_expand"),
    )
    new_in = adam(
        in_gradients,
        WEIGHT_DECAY,
        False,
        ids,
        in_sums,
        parts_first(project_in),
        parts_first(moment_project_in),
        parts_first(second_project_in),
        "adam_in",
        done("adam_contract"),
    )
    new_in = [parts_first(array) for array in new_in]
    small = sum(each[shard:, :shard].astype(F32) for each in in_sums[1:])
    small = behind(small, *done("adam_contract"))
    small = sum([tensor_swap(small, bit) for bit in (1, 2, 3)], small)
    grad_vectors = small[:vector_rows]
    grad_bias = small[vector_rows:small_rows].reshape(-1)
    change, first, second = adam_step(vectors, grad_vectors, moment_vectors, second_vectors, 0.0)
    new_vectors = (grad_vectors, change, first, second)
    change, first, second = adam_step(
        expand_bias, grad_bias, moment_expand_bias, second_expand_bias, 0.0
    )
    new_bias = (grad_bias, change, first, second)
    updated = (new_in, new_out, new_expand, new_contract, new_vectors, new_bias)
    return (
        block_output,
        input_grad,
        *[each[0] for each in updated],
        *[each[1] for each in updated],
        *[array for each in updated for array in each[2:]],
        grad_vectors[7],
    )


def solution(mesh):
    tokens = P("tensor", "fsdp", None)
    into = P("fsdp", None, "tensor")
    wide = P("fsdp", "tensor")
    tall = P("tensor", "fsdp")
    row = P(None, "fsdp")
    line = P("fsdp")
    params = (into, tall, wide, tall, row, line)
    moments = (into, into, tall, tall, wide, wide, tall, tall, row, row, line, line)
    return jax.shard_map(
        body,
        mesh=mesh,
        in_specs=(tokens, row, tokens) + params + moments,
        out_specs=(tokens, tokens) + params + params + moments + (line,),
        check_vma=False,
    )
```

```python
import functools

import jax
import jax.numpy as jnp
from jax import lax
from jax.experimental import pallas as pl
from jax.experimental.pallas import tpu as pltpu
from jax.sharding import PartitionSpec as P

HEAD_DIM = 64
STEP = 3
NORM_EPS = 1e-06
BETA_FIRST = 0.9
BETA_SECOND = 0.999
LEARN_RATE = 0.004
WEIGHT_DECAY = 0.04
ADAM_EPS = 1e-08
MASKED_SCORE = -1e30
ROOT_HALF = 0.7071067811865476
DENSITY_NORM = 0.3989422804014327
SCORE_SCALE = HEAD_DIM ** (-0.5)
LANES = 128
TILE = 352
CHUNK = 256
LONG = 4
SMALL = 16
LARGE = 32
ALL = 56
TOKENS = {}
F32 = jnp.float32
BF16 = jnp.bfloat16


def dot_nn(left, right):
    return lax.dot_general(left, right, (((1,), (0,)), ((), ())), preferred_element_type=F32)


def dot_nt(left, right):
    return lax.dot_general(left, right, (((1,), (1,)), ((), ())), preferred_element_type=F32)


def dot_tn(left, right):
    return lax.dot_general(left, right, (((0,), (0,)), ((), ())), preferred_element_type=F32)


def tiles_of(total, tile):
    return [(low, min(tile, total - low)) for low in range(0, total, tile)]


def norm_forward(values):
    center = jnp.mean(values, axis=-1, keepdims=True)
    offset = values - center
    spread = jnp.mean(offset * offset, axis=-1, keepdims=True)
    inverse = lax.rsqrt(spread + NORM_EPS)
    return offset * inverse, inverse


def norm_backward(scaled, inverse, grad_normed, norm_gain):
    grad_scaled = grad_normed * norm_gain
    first_mean = jnp.mean(grad_scaled, axis=-1, keepdims=True)
    second_mean = jnp.mean(grad_scaled * scaled, axis=-1, keepdims=True)
    return inverse * (grad_scaled - first_mean - scaled * second_mean)


def gelu_parts(hidden):
    normal_cdf = 0.5 * (1.0 + lax.erf(hidden * ROOT_HALF))
    density = DENSITY_NORM * jnp.exp(-0.5 * hidden * hidden)
    return (hidden * normal_cdf, normal_cdf + hidden * density)


def call(kernel, ids, args, in_specs, outs, out_specs, name, cost=(0, 0, 0), grid=(1,), scratch=(), aliases=None, after=(), vmem=SMALL):
    count = 1 + len(args)
    waits = len(after)
    token = shape_of((8, LANES), F32)

    def run(*refs):
        place = count + waits + len(outs)
        refs[place][...] = jnp.zeros_like(refs[place])
        kernel(*refs[:count], *refs[count + waits : place], *refs[place + 1 :])

    *results, done = pl.pallas_call(
        run,
        grid_spec=pltpu.PrefetchScalarGridSpec(
            num_scalar_prefetch=1,
            grid=grid,
            in_specs=list(in_specs) + [pl.BlockSpec(memory_space=pl.ANY)] * waits,
            out_specs=list(out_specs) + [whole(token)],
            scratch_shapes=scratch,
        ),
        out_shape=list(outs) + [token],
        input_output_aliases=aliases or {},
        compiler_params=pltpu.CompilerParams(vmem_limit_bytes=vmem * 2**20),
        cost_estimate=pl.CostEstimate(flops=cost[0], bytes_accessed=cost[1], transcendentals=cost[2]),
        name=name,
    )(ids, *args, *after)
    TOKENS[name] = done
    return results


def done(*names):
    return tuple(TOKENS[name] for name in names)


def whole(array):
    zeros = (0,) * len(array.shape)
    return pl.BlockSpec(array.shape, lambda *i: zeros)


def plain(kernel, ids, args, outs, name, **more):
    return call(kernel, ids, args, [whole(a) for a in args], outs, [whole(o) for o in outs], name, **more)


def shape_of(shape, dtype):
    return jax.ShapeDtypeStruct(shape, dtype)


ANYWHERE = pl.BlockSpec(memory_space=pl.ANY)


def low_bit(ids_ref):
    return lax.rem(ids_ref[0], 2)


def pack_kernel(ids_ref, in_ref, out_ref, expand_ref, contract_ref, small_ref, first, second, third):
    for pair, packed in enumerate((first, second)):
        for part in range(3):
            packed[:, part * LANES : (part + 1) * LANES] = in_ref[
                part, :, pair * LANES : (pair + 1) * LANES
            ].astype(BF16)
    first[:, 3 * LANES :] = small_ref[...].T.astype(BF16)
    second[:, 3 * LANES :] = out_ref[...].T.astype(BF16)
    hidden = expand_ref.shape[1]
    third[:, :hidden] = expand_ref[...].astype(BF16)
    third[:, hidden:] = contract_ref[...].T.astype(BF16)


def pack(ids, project_in, project_out, expand, contract, small):
    _, shard, head_width = project_in.shape
    widths = (4 * LANES, 3 * LANES + head_width, 2 * expand.shape[1])
    args = (project_in, project_out, expand, contract, small)
    outs = [shape_of((shard, width), BF16) for width in widths]
    return plain(pack_kernel, ids, args, outs, "pack", vmem=ALL)


def place_rows(ids_ref, near_ref, far_ref, write):
    count, shard = near_ref.shape[0], near_ref.shape[1]
    mine = ids_ref[0]
    for step in range(count):
        for low, ref in enumerate((near_ref, far_ref)):
            owner = lax.bitwise_xor(mine, 2 * step + low)
            write(pl.ds(pl.multiple_of(owner * shard, shard), shard), ref[step])


def flatten_kernel(ids_ref, normed_ref, flat_ref):
    flat_ref[...] = normed_ref[...].T


def flatten(ids, normed, after=()):
    seq, features = normed.shape
    return plain(flatten_kernel, ids, (normed,), [shape_of((features, seq), BF16)], "flatten", after=after)[0]


def unpack_kernel(ids_ref, near_ref, far_ref, out_ref):
    def write(at, values):
        out_ref[at, :] = values[:, 3 * LANES :]

    place_rows(ids_ref, near_ref, far_ref, write)


def unpack(ids, near, far, after=()):
    count, shard, width = near.shape
    outs = [shape_of((2 * count * shard, width - 3 * LANES), BF16)]
    return plain(unpack_kernel, ids, (near, far), outs, "unpack", after=after)[0]


def attend_kernel(pair, ids_ref, live_ref, near_ref, far_ref, normed_ref, *refs):
    if pair == 0:
        x_ref = normed_ref
        rows_ref, normed_ref, scaled_ref, held_ref = refs[0], refs[1], refs[2], refs[-1]
        weight_ref, qkv_ref, attended_ref, query_ref, key_ref, value_ref = refs[3:-1]
    else:
        rows_ref, weight_ref, qkv_ref, attended_ref, query_ref, key_ref, value_ref = refs
    seq = normed_ref.shape[0]
    width = 3 * LANES

    def write(at, values):
        weight_ref[at, :] = values[:, :width]
        if pair == 0:
            held_ref[at, :] = values[:, width:].astype(F32)

    place_rows(ids_ref, near_ref, far_ref, write)
    if pair == 0:
        rows_ref[...] = held_ref[...].T[0 : rows_ref.shape[0]]
    start = pl.multiple_of(ids_ref[1] * (2 * LANES) + pair * LANES, LANES)
    bias_row = jnp.concatenate(
        [rows_ref[2:3, pl.ds(start, LANES)], jnp.zeros((1, LANES), F32), rows_ref[3:4, pl.ds(start, LANES)]],
        axis=1,
    )
    for low, count in tiles_of(seq, TILE):
        at = slice(low, low + count)
        if pair == 0:
            scaled, _ = norm_forward(x_ref[at, :].astype(F32))
            scaled_ref[at, :] = scaled.astype(BF16)
            normed_ref[at, :] = (scaled * rows_ref[0:1, :] + rows_ref[1:2, :]).astype(BF16)
        mixed = dot_nn(normed_ref[at, :], weight_ref[...]) + bias_row
        qkv_ref[at, :] = mixed.astype(BF16)
    lane = lax.broadcasted_iota(jnp.int32, (seq, LANES), 1)
    bias = jnp.where(live_ref[...] > 0, 0.0, MASKED_SCORE).astype(F32)
    key_rows = qkv_ref[:, LANES : 2 * LANES].astype(F32)
    value_rows = qkv_ref[:, 2 * LANES : 3 * LANES].astype(F32)
    for head in range(2):
        own = (lane // HEAD_DIM) == head
        spare = HEAD_DIM * (1 - head)
        extra = jnp.where(lane == spare, bias, 0.0)
        key_ref[head] = jnp.where(own, key_rows, extra).astype(BF16)
        extra = jnp.where(lane == spare, 1.0, 0.0)
        value_ref[head] = jnp.where(own, value_rows, extra).astype(BF16)
    for low, count in tiles_of(seq, TILE):
        at = slice(low, low + count)
        lane = lax.broadcasted_iota(jnp.int32, (count, LANES), 1)
        queries = qkv_ref[at, 0:LANES].astype(F32) * SCORE_SCALE
        both = None
        for head in range(2):
            own = (lane // HEAD_DIM) == head
            spare = HEAD_DIM * (1 - head)
            extra = jnp.where(lane == spare, 1.0, 0.0)
            mine = jnp.where(own, queries, extra).astype(BF16)
            scores = dot_nt(mine, key_ref[head])
            highest = jnp.max(scores, axis=-1, keepdims=True)
            weights = jnp.exp(scores - highest).astype(BF16)
            output = dot_nn(weights, value_ref[head])
            summed = output[:, spare : spare + 1]
            output = output / summed
            both = output if head == 0 else jnp.where(own, output, both)
            rest = -(highest + jnp.log(summed))
            extra = jnp.where(lane == spare + 3, 1.0, 0.0)
            for place in range(3):
                part = rest.astype(BF16).astype(F32)
                extra = jnp.where(lane == spare + place, part, extra)
                rest = rest - part
            query_ref[at, LANES * head : LANES * (head + 1)] = jnp.where(
                own, queries, extra
            ).astype(BF16)
        attended_ref[at, :] = both.astype(BF16)


def attend(pair, ids, live, near, far, normed, rows=None, after=()):
    seq, features = normed.shape
    outs = [
        shape_of((features, 3 * LANES), BF16),
        shape_of((seq, 3 * LANES), BF16),
        shape_of((seq, LANES), BF16),
        shape_of((seq, 2 * LANES), BF16),
    ]
    scratch = [pltpu.VMEM((2, seq, LANES), BF16), pltpu.VMEM((2, seq, LANES), BF16)]
    args = (live, near, far, normed)
    if pair == 0:
        outs = [shape_of((16, features), F32)] + [shape_of((seq, features), BF16)] * 2 + outs
        scratch.append(pltpu.VMEM((features, LANES), F32))
    else:
        args += (rows,)
    return plain(
        functools.partial(attend_kernel, pair),
        ids,
        args,
        outs,
        f"attend_{pair}",
        cost=(LONG * 160 * seq * seq * HEAD_DIM, 0, 0),
        vmem=LARGE,
        scratch=scratch,
        after=after,
    )


def attend_back_kernel(
    ids_ref,
    live_ref,
    qkv_ref,
    query_ref,
    attended_ref,
    mine_a,
    other_a,
    mine_b,
    other_b,
    out_ref,
    mixed_ref,
    sums_ref,
    grad_ref,
    held_ref,
    query_sum_ref,
):
    seq = qkv_ref.shape[0]
    rows = mine_a.shape[0]
    core = ids_ref[2]
    for index, ref in enumerate((mine_a, other_a, mine_b, other_b)):
        block = 2 * (index // 2) + lax.bitwise_xor(core, index % 2)
        grad_ref[pl.ds(pl.multiple_of(block * rows, 8), rows), :] = dot_nn(ref[...], out_ref[...])
    lane = lax.broadcasted_iota(jnp.int32, (seq, LANES), 1)
    grad = grad_ref[...].astype(BF16).astype(F32)
    product = grad * attended_ref[...].astype(F32)
    for head in range(2):
        own = (lane // HEAD_DIM) == head
        spare = HEAD_DIM * (1 - head)
        inner = -jnp.sum(jnp.where(own, product, 0.0), axis=-1, keepdims=True)
        first = inner.astype(BF16).astype(F32)
        extra = jnp.where(lane == spare, first, jnp.where(lane == spare + 1, inner - first, 0.0))
        held_ref[head] = jnp.where(own, grad, extra).astype(BF16)
    value_sum = jnp.zeros((1, LANES), F32)
    for index, (low, count) in enumerate(tiles_of(seq, TILE)):
        at = slice(low, low + count)
        lane = lax.broadcasted_iota(jnp.int32, (count, LANES), 1)
        bias = jnp.where(live_ref[at, :] > 0, 0.0, MASKED_SCORE).astype(F32)
        key_rows = qkv_ref[at, LANES : 2 * LANES].astype(F32)
        value_rows = qkv_ref[at, 2 * LANES : 3 * LANES].astype(F32)
        grad_keys = grad_values = None
        for head in range(2):
            own = (lane // HEAD_DIM) == head
            spare = HEAD_DIM * (1 - head)
            ones = jnp.where((lane >= spare) & (lane < spare + 3), 1.0, 0.0)
            extra = jnp.where(lane == spare + 3, bias, ones)
            keys = jnp.where(own, key_rows, extra).astype(BF16)
            values = jnp.where(own, value_rows, ones).astype(BF16)
            queries = query_ref[:, LANES * head : LANES * (head + 1)]
            above = held_ref[head]
            weights = jnp.exp(dot_nt(keys, queries))
            grad_scores = (weights * dot_nt(values, above)).astype(BF16)
            value_part = dot_nn(weights.astype(BF16), above)
            key_part = dot_nn(grad_scores, queries)
            part = slice(HEAD_DIM * head, HEAD_DIM * (head + 1))
            query_part = dot_tn(keys, grad_scores)[part]
            if index == 0:
                query_sum_ref[part] = query_part
            else:
                query_sum_ref[part] += query_part
            grad_keys = key_part if head == 0 else jnp.where(own, key_part, grad_keys)
            grad_values = value_part if head == 0 else jnp.where(own, value_part, grad_values)
        grad_values = grad_values.astype(BF16)
        mixed_ref[at, LANES : 2 * LANES] = grad_keys.astype(BF16)
        mixed_ref[at, 2 * LANES : 3 * LANES] = grad_values
        value_sum += jnp.sum(grad_values.astype(F32), axis=0, keepdims=True)
    grad_queries = (query_sum_ref[...].T * SCORE_SCALE).astype(BF16)
    mixed_ref[:, 0:LANES] = grad_queries
    sums_ref[0:1, :] = jnp.sum(grad_queries.astype(F32), axis=0, keepdims=True)
    sums_ref[1:2, :] = value_sum


def attend_back(pair, ids, live, qkv, queries, attended, grads, out_own, after=()):
    seq = qkv.shape[0]
    features = out_own.shape[0]
    outs = [shape_of((seq, 3 * LANES), BF16), shape_of((8, LANES), F32)]
    args = (live, qkv, queries, attended, *grads)
    return call(
        attend_back_kernel,
        ids,
        (*args, out_own),
        [whole(a) for a in args] + [pl.BlockSpec((features, LANES), lambda i, _: (0, pair))],
        outs,
        [whole(o) for o in outs],
        f"attend_back_{pair}",
        cost=((1 - pair) * 80 * seq * seq * HEAD_DIM, 0, 0),
        vmem=LARGE,
        scratch=[
            pltpu.VMEM((seq, LANES), F32),
            pltpu.VMEM((2, seq, LANES), BF16),
            pltpu.VMEM((LANES, seq), F32),
        ],
        after=after,
    )


def middle_kernel(ids_ref, x_ref, *refs):
    att_refs, out_refs = refs[:8], refs[8:12]
    rows_ref, expand_ref, contract_ref, bias_ref, top_ref = refs[12:17]
    outs = refs[-14:-5]
    normed_ref, act_ref, hidden_ref = outs[:3]
    branch_refs, attn_ref, back_refs, sums_ref = outs[3:5], outs[5], outs[6:8], outs[8]
    held_ref, normed_held, act_held, hidden_held, grad_held = refs[-5:]
    step = pl.program_id(0)

    @pl.when(step == 0)
    def _():
        sums_ref[...] = jnp.zeros_like(sums_ref)

    attn_sum = rows_ref[4:5, :]
    for device, out_ref in enumerate(out_refs):
        held_ref[:, :LANES] = att_refs[2 * device][0]
        held_ref[:, LANES:] = att_refs[2 * device + 1][0]
        attn_sum = attn_sum + dot_nt(held_ref[...], out_ref[...])

    @pl.when(lax.rem(step, 2) == 1)
    def _():
        attn_ref[0] = attn_sum.astype(BF16)

    residual = x_ref[0].astype(F32) + rows_ref[5:6, :] * attn_sum
    scaled, _ = norm_forward(residual)
    normed_held[...] = (scaled * rows_ref[6:7, :] + rows_ref[7:8, :]).astype(BF16)
    normed_ref[0] = normed_held[...]
    grad_held[...] = (top_ref[0].astype(F32) * rows_ref[9:10, :]).astype(BF16)
    for low in range(0, act_held.shape[1], CHUNK):
        at = slice(low, low + CHUNK)
        activated, slope = gelu_parts(dot_nn(normed_held[...], expand_ref[:, at]) + bias_ref[:, at])
        act_held[:, at] = activated.astype(BF16)
        grad_hidden = (dot_nn(grad_held[...], contract_ref[:, at]) * slope).astype(BF16)
        hidden_held[:, at] = grad_hidden
        sums_ref[0:1, at] += jnp.sum(grad_hidden.astype(F32), axis=0, keepdims=True)
    act_ref[0] = act_held[...]
    hidden_ref[0] = hidden_held[...]
    back = dot_nt(hidden_held[...], expand_ref[...])
    sums_ref[1:2, :] += jnp.sum(back * scaled, axis=0, keepdims=True)
    sums_ref[2:3, :] += jnp.sum(back, axis=0, keepdims=True)
    branch = dot_nt(act_held[...], contract_ref[...]).astype(BF16)
    for index in range(2):

        @pl.when(lax.rem(step, 2) == index)
        def _():
            back_refs[index][0] = back.astype(BF16)
            branch_refs[index][0] = branch


def middle(ids, x_full, att, out_all, rows, weights, bias, top_full, after=()):
    _, count, features = x_full.shape
    hidden = weights.shape[1] // 2

    def block(i, ids_ref):
        return 2 * lax.div(i, 2) + lax.bitwise_xor(ids_ref[2], 1 - lax.rem(i, 2))

    part = lambda n: pl.BlockSpec((1, count, n), lambda i, ids_ref: (block(i, ids_ref), 0, 0))
    held = pl.BlockSpec((1, count, features), lambda i, _: (lax.div(i, 2), 0, 0))
    column = lambda c: pl.BlockSpec((features, hidden), lambda i, _: (0, c))
    sums = shape_of((8, features), F32)
    outs = [shape_of((4, count, n), BF16) for n in (features, hidden, hidden)]
    outs += [shape_of((2, count, features), BF16)] * 5 + [sums]
    specs = [part(features), part(hidden), part(hidden)] + [held] * 5 + [whole(sums)]
    seq = 4 * count
    return call(
        middle_kernel,
        ids,
        (x_full, *att, *out_all, rows, weights, weights, bias, top_full),
        [part(features)]
        + [part(LANES)] * len(att)
        + [whole(o) for o in out_all]
        + [whole(rows), column(0), column(1), whole(bias), part(features)],
        outs,
        specs,
        "middle",
        cost=(2 * seq * features * (features + 4 * hidden), 0, 0),
        grid=(4,),
        scratch=[pltpu.VMEM((count, 2 * LANES), BF16)] + [pltpu.VMEM((count, features), BF16)] * 4,
        after=after,
        vmem=ALL,
    )


def pair_sum_kernel(ids_ref, keep_ref, arrived_ref, sum_ref):
    sum_ref[...] = (keep_ref[...].astype(F32) + arrived_ref[...].astype(F32)).astype(BF16)


def pair_sum(half, ids, keep, arrived):
    _, count, features = keep.shape
    part = pl.BlockSpec((None, count, features), lambda i, _: (half, 0, 0))
    out = shape_of((count, features), BF16)
    return call(
        pair_sum_kernel, ids, (keep, arrived), [part, part], [out], [whole(out)], f"back_sum_{half}"
    )[0]


def split_sum_kernel(ids_ref, keep_ref, arrived_ref, give_ref, stay_ref):
    half = ids_ref[3]
    total = keep_ref[...].astype(F32) + arrived_ref[...].astype(F32)
    give_ref[...] = jnp.where(half == 0, total[1], total[0]).astype(BF16)
    stay_ref[...] = jnp.where(half == 0, total[0], total[1]).astype(BF16)


def split_sum(ids, keep, arrived, name, after=()):
    outs = [shape_of(keep.shape[1:], BF16)] * 2
    return plain(split_sum_kernel, ids, (keep, arrived), outs, name, after=after)


def residual_kernel(ids_ref, chip_ref, arrived_ref, x_ref, attn_ref, top_ref, rows_ref, grad_ref, residual_ref):
    total = chip_ref[...].astype(F32) + arrived_ref[...].astype(F32)
    attn_sum = attn_ref[...].astype(F32)
    scaled, inverse = norm_forward(x_ref[0].astype(F32) + rows_ref[5:6, :] * attn_sum)
    grad = top_ref[0].astype(F32) + norm_backward(scaled, inverse, total, rows_ref[6:7, :])
    residual_ref[...] = grad.astype(BF16)
    grad_ref[...] = (grad * rows_ref[5:6, :]).astype(BF16)


def residual_back(half, ids, chip, arrived, x_full, attn, top_full, rows, after=()):
    count, features = chip.shape
    part = pl.BlockSpec((1, count, features), lambda i, ids_ref: (2 * half + ids_ref[2], 0, 0))
    held = pl.BlockSpec((None, count, features), lambda i, _: (half, 0, 0))
    outs = [shape_of((count, features), BF16)] * 2
    return call(
        residual_kernel,
        ids,
        (chip, arrived, x_full, attn, top_full, rows),
        [whole(chip), whole(arrived), part, held, part, whole(rows)],
        outs,
        [whole(out) for out in outs],
        f"residual_back_{half}",
        after=after,
        vmem=ALL,
    )


def own_kernel(
    ids_ref, x_ref, top_ref, attn_ref, grad_a, grad_b, stay_ref, branch_ref, rows_ref, output_ref, sums_ref
):
    first = ids_ref[3] == 0
    choose = lambda a, b: jnp.where(first, a[...].astype(F32), b[...].astype(F32))
    attn_sum = attn_ref[...].astype(F32)
    grad = choose(grad_a, grad_b)
    branch = stay_ref[...].astype(F32) + branch_ref[...].astype(F32) + rows_ref[8:9, :]
    output_ref[:, 0, :] = x_ref[0].astype(F32) + rows_ref[5:6, :] * attn_sum + rows_ref[9:10, :] * branch
    top = top_ref[0].astype(F32)
    for row, values in enumerate((grad * rows_ref[5:6, :], grad * attn_sum, top * rows_ref[9:10, :], top * branch)):
        sums_ref[row : row + 1, :] = jnp.sum(values, axis=0, keepdims=True)


def own_block(ids, x_full, top_full, attn, grads, stay, branch, rows, after=()):
    _, count, features = x_full.shape
    part = pl.BlockSpec((1, count, features), lambda i, ids_ref: (ids_ref[1], 0, 0))
    outs = [shape_of((count, 1, features), F32), shape_of((8, features), F32)]
    held = pl.BlockSpec((None, count, features), lambda i, ids_ref: (ids_ref[3], 0, 0))
    rest = (*grads, stay, branch, rows)
    return call(
        own_kernel,
        ids,
        (x_full, top_full, attn, *rest),
        [part, part, held] + [whole(a) for a in rest],
        outs,
        [whole(o) for o in outs],
        "own_block",
        after=after,
        vmem=24,
    )


def matrices_kernel(ids_ref, left_a, top_ref, right_a, right_b, rows_ref, out_ref, flat_ref):
    step = pl.program_id(0)
    per = pl.num_programs(0) // 2

    @pl.when(step == 0)
    def _():
        flat_ref[...] = left_a[...].T

    @pl.when(step == per)
    def _():
        flat_ref[...] = (top_ref[...].astype(F32) * rows_ref[9:10, :]).astype(BF16).T

    right = jnp.where(step < per, right_a[...], right_b[...])
    out_ref[...] = dot_nn(flat_ref[...], right).astype(BF16)


def matrices(ids, normed, hidden, top_full, activated, rows, after=()):
    seq, features = normed.shape
    width = hidden.shape[1]
    block = 512
    per = width // block
    out = shape_of((features, 2 * width), BF16)
    top = top_full.reshape(seq, features)
    return call(
        matrices_kernel,
        ids,
        (normed, top, hidden, activated, rows),
        [
            whole(normed),
            whole(top),
            pl.BlockSpec((seq, block), lambda i, _: (0, jnp.minimum(i, per - 1))),
            pl.BlockSpec((seq, block), lambda i, _: (0, jnp.maximum(i - per, 0))),
            whole(rows),
        ],
        [out],
        [pl.BlockSpec((features, block), lambda i, _: (0, i))],
        "matrices",
        grid=(2 * per,),
        scratch=[pltpu.VMEM((features, seq), BF16)],
        after=after,
        vmem=ALL,
    )[0]


def store_shards(ids_ref, index, values, give_ref, keep_ref):
    @pl.when(low_bit(ids_ref) == index % 2)
    def _():
        keep_ref[index // 2] = values

    @pl.when(low_bit(ids_ref) != index % 2)
    def _():
        give_ref[index // 2] = values


def out_grad_kernel(ids_ref, att_a, att_b, mine_a, other_a, mine_b, other_b, give_ref, keep_ref):
    core = ids_ref[2]
    total = [None, None]
    for index, ref in enumerate((mine_a, other_a, mine_b, other_b)):
        block = 2 * (index // 2) + lax.bitwise_xor(core, index % 2)
        for pair, att_ref in enumerate((att_a, att_b)):
            part = dot_tn(att_ref[block], ref[...])
            total[pair] = part if index == 0 else total[pair] + part
    count, shard, _ = give_ref.shape
    values = jnp.concatenate([t.T for t in total], axis=1).astype(BF16)
    for place in range(2 * count):
        store_shards(ids_ref, place, values[place * shard : (place + 1) * shard], give_ref, keep_ref)


def out_grad(ids, attended, grads, places, after=()):
    count, features = grads[0].shape
    outs = [shape_of((places // 2, features // places, 2 * LANES), BF16)] * 2
    args = [a.reshape(4, count, LANES) for a in attended] + list(grads)
    return plain(out_grad_kernel, ids, args, outs, "out_grad", after=after)


def in_grad_kernel(ids_ref, flat_ref, mixed_ref, *refs):
    if len(refs) > 2:
        base_ref, input_ref, own_ref, first_ref, second_ref, give_ref, keep_ref, small_ref = refs
        small_ref[...] = base_ref[...]
        small_ref[0:2, :] = input_ref[0:2, :]
        small_ref[4:5, :] = own_ref[0:1, :]
        small_ref[5:6, :] = own_ref[1:2, :]
        small_ref[8:9, :] = own_ref[2:3, :]
        small_ref[9:10, :] = own_ref[3:4, :]
        for pair, head_ref in enumerate((first_ref, second_ref)):
            start = pl.multiple_of(ids_ref[1] * (2 * LANES) + pair * LANES, LANES)
            small_ref[2:3, pl.ds(start, LANES)] = head_ref[0:1, :]
            small_ref[3:4, pl.ds(start, LANES)] = head_ref[1:2, :]
    else:
        give_ref, keep_ref = refs
    count, held, width = give_ref.shape
    values = dot_nn(flat_ref[...], mixed_ref[...]).astype(BF16)
    shard = values.shape[0] // (2 * count)
    for place in range(2 * count):
        at = slice(place * shard, (place + 1) * shard)
        part = values[at]
        if held > shard:
            below = small_ref[:, at].astype(BF16)
            below = jnp.concatenate([below, jnp.zeros((held - shard, width - shard), BF16)], axis=1)
            part = jnp.concatenate([part, below])
        store_shards(ids_ref, place, part, give_ref, keep_ref)


def in_grad(pair, ids, flat, mixed, places, after=(), small=()):
    features = flat.shape[0]
    held, scratch = features // places, []
    if small:
        held += small[0].shape[0]
        scratch = [pltpu.VMEM(small[0].shape, F32)]
    outs = [shape_of((places // 2, held, mixed.shape[1]), BF16)] * 2
    args = (flat, mixed, *small)
    return plain(in_grad_kernel, ids, args, outs, f"in_grad_{pair}", after=after, scratch=scratch)


def low_sum_kernel(parts, ids_ref, *refs):
    out_refs = refs[2 * parts :]
    high = lax.div(ids_ref[0], 2)
    for step, out_ref in enumerate(out_refs):
        at = lax.bitwise_xor(high, step)
        low = 0
        for keep_ref, arrived_ref in zip(refs[0 : 2 * parts : 2], refs[1 : 2 * parts : 2]):
            width = keep_ref.shape[2]
            total = keep_ref[at].astype(F32) + arrived_ref[at].astype(F32)
            out_ref[:, low : low + width] = total.astype(BF16)
            low += width


def low_sum(ids, pairs, name, after=()):
    count, held, _ = pairs[0].shape
    outs = [shape_of((held, sum(a.shape[2] for a in pairs[::2])), BF16)] * count
    kernel = functools.partial(low_sum_kernel, len(pairs) // 2)
    return plain(kernel, ids, pairs, outs, name, after=after)


def input_back_kernel(ids_ref, scaled_ref, mixed_a, mixed_b, weight_a, weight_b, give_ref, keep_ref, sums_ref):
    step = pl.program_id(0)

    @pl.when(step == 0)
    def _():
        sums_ref[...] = jnp.zeros_like(sums_ref)

    total = dot_nt(mixed_a[0], weight_a[...]) + dot_nt(mixed_b[0], weight_b[...])
    sums_ref[0:1, :] += jnp.sum(total * scaled_ref[0].astype(F32), axis=0, keepdims=True)
    sums_ref[1:2, :] += jnp.sum(total, axis=0, keepdims=True)

    @pl.when(step < 2)
    def _():
        give_ref[0] = total.astype(BF16)

    @pl.when(step >= 2)
    def _():
        keep_ref[0] = total.astype(BF16)


def input_back(ids, scaled, mixed, weights, after=()):
    _, count, features = scaled.shape
    width = mixed[0].shape[2]
    def part(n):
        return pl.BlockSpec(
            (1, count, n),
            lambda i, ids_ref: (2 * lax.rem(i, 2) + lax.bitwise_xor(ids_ref[2], 1 - lax.div(i, 2)), 0, 0),
        )
    outs = [shape_of((2, count, features), BF16)] * 2 + [shape_of((8, features), F32)]
    return call(
        input_back_kernel,
        ids,
        (scaled, *mixed, *weights),
        [part(features), part(width), part(width)] + [whole(w) for w in weights],
        outs,
        [
            pl.BlockSpec((1, count, features), lambda i, _: (jnp.minimum(i, 1), 0, 0)),
            pl.BlockSpec((1, count, features), lambda i, _: (jnp.maximum(i - 2, 0), 0, 0)),
            whole(outs[2]),
        ],
        "input_back",
        grid=(4,),
        after=after,
    )


def input_kernel(ids_ref, stay_ref, arrived_ref, x_ref, grad_a, grad_b, rows_ref, out_ref):
    total = stay_ref[...].astype(F32) + arrived_ref[...].astype(F32)
    scaled, inverse = norm_forward(x_ref[0].astype(F32))
    grad = jnp.where(ids_ref[3] == 0, grad_a[...].astype(F32), grad_b[...].astype(F32))
    out_ref[:, 0, :] = grad + norm_backward(scaled, inverse, total, rows_ref[0:1, :])


def input_grad_of(ids, stay, arrived, x_full, grads, rows, after=()):
    _, count, features = x_full.shape
    part = pl.BlockSpec((1, count, features), lambda i, ids_ref: (ids_ref[1], 0, 0))
    outs = [shape_of((count, 1, features), F32)]
    return call(
        input_kernel,
        ids,
        (stay, arrived, x_full, *grads, rows),
        [whole(stay), whole(arrived), part, whole(grads[0]), whole(grads[1]), whole(rows)],
        outs,
        [whole(o) for o in outs],
        "input_grad",
        after=after,
    )[0]


def adam_step(master, gradient, first, second, decay):
    first_new = BETA_FIRST * first + (1.0 - BETA_FIRST) * gradient
    second_new = BETA_SECOND * second + (1.0 - BETA_SECOND) * gradient * gradient
    first_hat = first_new / (1.0 - BETA_FIRST**STEP)
    second_hat = second_new / (1.0 - BETA_SECOND**STEP)
    change = -LEARN_RATE * (first_hat / (jnp.sqrt(second_hat) + ADAM_EPS) + decay * master)
    return (change, first_new, second_new)


def adam_kernel(gradients, decay, keep_change, ids_ref, *refs):
    count = len(refs) - 7
    parts, (master, first, second), outs = refs[:count], refs[count:-4], refs[-4:]
    for at, gradient in gradients(parts):
        change, first_new, second_new = adam_step(master[at], gradient, first[at], second[at], decay)
        outs[0][at] = gradient
        outs[1][at] = change if keep_change else master[at] + change
        outs[2][at] = first_new
        outs[3][at] = second_new


def adam(gradients, decay, keep_change, ids, parts, master, first, second, name, after=()):
    outs = [shape_of(master.shape, F32)] * 4
    return plain(
        functools.partial(adam_kernel, gradients, decay, keep_change),
        ids,
        (*parts, master, first, second),
        outs,
        name,
        after=after,
    )


def sum_refs(refs):
    total = refs[0][...].astype(F32)
    for ref in refs[1:]:
        total = total + ref[...].astype(F32)
    return total


def high_sum_kernel(ids_ref, *refs):
    refs[-1][...] = sum_refs(refs[:-1])


def high_sum(ids, parts, name, after=()):
    out = shape_of(parts[0].shape, F32)
    return plain(high_sum_kernel, ids, parts, [out], name, after=after)[0]


def in_gradients(parts):
    totals = (parts[0][...], sum_refs(parts[1:]))
    for pair, total in enumerate(totals):
        columns = slice(pair * LANES, (pair + 1) * LANES)
        for part in range(3):
            values = total[: parts[0].shape[0], part * LANES : (part + 1) * LANES]
            yield (part, slice(None), columns), values


def out_gradients(parts):
    yield (slice(None), slice(None)), parts[0][:, 3 * LANES :].T


def expand_gradients(parts):
    yield (slice(None), slice(None)), parts[0][:, : parts[0].shape[1] // 2].astype(F32)


def contract_gradients(parts):
    yield (slice(None), slice(None)), parts[0][:, parts[0].shape[1] // 2 :].astype(F32).T


def tensor_swap(array, bit):
    return lax.ppermute(array, "tensor", [(rank, rank ^ bit) for rank in range(4)])


def fsdp_swap(array, bit):
    size = lax.axis_size("fsdp")
    return lax.ppermute(array, "fsdp", [(rank, rank ^ bit) for rank in range(size)])


def behind(array, *others):
    return lax.optimization_barrier((array,) + others)[0]


def around(array, *first):
    across = tensor_swap(array, 2)
    corner = tensor_swap(behind(across, *first) if first else across, 1)
    return (array, tensor_swap(array, 1), across, corner)


def gather_positions(block, rank, *first):
    full = jnp.zeros((4,) + block.shape, block.dtype)
    for bit, piece in enumerate(around(block, *first)):
        full = lax.dynamic_update_slice_in_dim(full, piece[None], rank ^ bit, 0)
    return full


def gather_shards(piece):
    count = lax.axis_size("fsdp") // 2
    near = jnp.stack([piece] + [fsdp_swap(piece, 2 * step) for step in range(1, count)])
    return near, fsdp_swap(near, 1)


def body(
    block_input,
    live_mask,
    cotangent,
    project_in,
    project_out,
    expand,
    contract,
    vectors,
    expand_bias,
    moment_project_in,
    second_project_in,
    moment_project_out,
    second_project_out,
    moment_expand,
    second_expand,
    moment_contract,
    second_contract,
    moment_vectors,
    second_vectors,
    moment_expand_bias,
    second_expand_bias,
):
    rows, _, features = block_input.shape
    shard, _, head_width = project_in.shape
    hidden_width = expand.shape[1]
    seq = 4 * rows
    places = lax.axis_size("fsdp")
    rank = lax.axis_index("tensor")
    place = lax.axis_index("fsdp")
    ids = jnp.stack([place, rank, rank % 2, rank // 2]).astype(jnp.int32)
    parts_first = lambda array: array.transpose(1, 0, 2)

    bias_shard = expand_bias.reshape(-1, shard)
    vector_rows = vectors.shape[0]
    small_rows = vector_rows + bias_shard.shape[0]
    small_shard = jnp.concatenate(
        [vectors, bias_shard, jnp.zeros((LANES - small_rows, shard), F32)]
    )
    packed = pack(ids, parts_first(project_in), project_out, expand, contract, small_shard)
    first_shards = gather_shards(packed[0])
    second_shards = gather_shards(behind(packed[1], first_shards[0]))
    weights = lax.all_gather(
        behind(packed[2], first_shards[0]), "fsdp", axis=0, tiled=True
    )

    x_own = block_input[:, 0]
    live_own = lax.dynamic_slice_in_dim(live_mask, rank * rows, rows, 0) > 0
    top_own = cotangent[:, 0] * live_own.astype(F32)
    x_full = gather_positions(x_own.astype(BF16), rank)
    top_full = gather_positions(behind(top_own.astype(BF16), x_full), rank)

    rows_now, normed_one, scaled_one, *heads = attend(
        0, ids, live_mask, *first_shards, x_full.reshape(seq, features)
    )
    heads = [heads]
    out_own = unpack(ids, *second_shards, after=done("attend_0"))
    heads.append(attend(1, ids, live_mask, *second_shards, normed_one, rows_now, done("unpack")))
    normed_flat = flatten(ids, normed_one, done("attend_1"))
    held = done("flatten")
    out_all = around(out_own)
    att_sets = [around(each[2]) for each in heads]
    att_all = [
        att_sets[pair][device].reshape(4, rows, LANES) for device in range(4) for pair in range(2)
    ]
    bias_now = rows_now[vector_rows:small_rows]
    bias_now = bias_now.reshape(-1, places, shard).transpose(1, 0, 2).reshape(1, -1)
    bias_here = lax.dynamic_slice_in_dim(bias_now, rank * hidden_width, hidden_width, 1)

    kept = middle(ids, x_full, att_all, out_all, rows_now, weights, bias_here, top_full, held)
    normed_two, activated, grad_hidden = [array.reshape(seq, array.shape[2]) for array in kept[:3]]
    branch_give, branch_keep, attn, back_give, back_keep, sums = kept[3:]
    back_arrived = tensor_swap(back_give, 1)
    chips, arrived, grads, grads_peer = [], [], [], []
    for half in range(2):
        chips.append(pair_sum(half, ids, back_keep, back_arrived))
        arrived.append(tensor_swap(chips[half], 2))
    grad_second = matrices(
        ids, normed_two, grad_hidden, top_full, activated, rows_now, done("back_sum_1")
    )
    lay = lambda values, start, total: lax.dynamic_update_slice_in_dim(
        jnp.zeros((total,), F32), values, start, 0
    )
    grad_bias = lay(sums[0], rank * hidden_width, expand_bias.shape[0] * places)
    grad_bias = grad_bias.reshape(places, -1, shard).transpose(1, 0, 2).reshape(-1, features)
    none = jnp.zeros((6, features), F32)
    small = jnp.concatenate([none, sums[1:3], none[:2], grad_bias, none[: 16 - small_rows]])

    branch_arrived = tensor_swap(behind(branch_give, chips[1]), 1)
    for half in range(2):
        wait = done("matrices")
        if half == 1:
            give, branch_stay = split_sum(
                ids, branch_keep, branch_arrived, "branch_sum", done("residual_back_0")
            )
            branch_arrived = tensor_swap(give, 2)
            wait = done("branch_sum") + (small,)
        grads.append(
            residual_back(
                half, ids, chips[half], arrived[half], x_full, attn, top_full, rows_now, wait
            )
        )
        grads_peer.append(tensor_swap(grads[half][0], 1))
    attn_grads = (grads[0][0], grads_peer[0], grads[1][0], grads_peer[1])
    residual_grads = (grads[0][1], grads[1][1])
    second_sum = lax.psum_scatter(
        behind(grad_second, arrived[0]), "fsdp", scatter_dimension=0, tiled=True
    )

    sends = lambda low: [low[0]] + [fsdp_swap(low[step], 2 * step) for step in range(1, places // 2)]
    mixed, head_sums = [], []
    wait = done("residual_back_1")
    for pair in range(2):
        weight, qkv, attended, queries = heads[pair]
        mixed_pair, pair_sums = attend_back(
            pair, ids, live_mask, qkv, queries, attended, attn_grads, out_own, wait
        )
        mixed.append(mixed_pair)
        head_sums.append(pair_sums)
        if pair == 0:
            in_give, in_keep = in_grad(0, ids, normed_flat, mixed_pair, places)
            in_arrived = fsdp_swap(in_give, 1)
            block_output, own_sums = own_block(
                ids,
                x_full,
                top_full,
                attn,
                residual_grads,
                branch_stay,
                branch_arrived,
                rows_now,
                done("in_grad_0"),
            )
            out_give, out_keep = out_grad(
                ids, [each[2] for each in heads], attn_grads, places, done("own_block")
            )
            out_arrived = fsdp_swap(out_give, 1)
            wait = done("out_grad")
    first_sums = sends(
        low_sum(ids, (in_keep, in_arrived, out_keep, out_arrived), "in_low_0", done("attend_back_1"))
    )
    input_give, input_keep, input_sums = input_back(
        ids,
        scaled_one.reshape(4, rows, features),
        [each.reshape(4, rows, each.shape[1]) for each in mixed],
        [each[0] for each in heads],
        done("in_low_0"),
    )

    in_give, in_keep = in_grad(
        1, ids, normed_flat, mixed[1], places, (), (small, input_sums, own_sums, *head_sums)
    )
    in_arrived = fsdp_swap(in_give, 1)
    give, stay = split_sum(ids, input_keep, tensor_swap(input_give, 1), "input_sum", done("in_grad_1"))
    input_arrived = tensor_swap(give, 2)
    in_low = low_sum(
        ids, (in_keep, behind(in_arrived, input_arrived)), "in_low_1", done("input_sum")
    )
    second_sums = sends(in_low)
    input_grad = input_grad_of(
        ids, stay, input_arrived, x_full, residual_grads, rows_now, done("in_low_1")
    )
    sum_first = high_sum(ids, first_sums, "in_sum_0", done("input_grad"))
    in_sums = [sum_first] + second_sums
    new_out = adam(
        out_gradients,
        WEIGHT_DECAY,
        True,
        ids,
        (sum_first,),
        project_out,
        moment_project_out,
        second_project_out,
        "adam_out",
        done("in_sum_0"),
    )
    second = (second_sum,)
    new_expand = adam(
        expand_gradients,
        WEIGHT_DECAY,
        False,
        ids,
        second,
        expand,
        moment_expand,
        second_expand,
        "adam_expand",
        done("adam_out"),
    )
    new_contract = adam(
        contract_gradients,
        WEIGHT_DECAY,
        False,
        ids,
        second,
        contract,
        moment_contract,
        second_contract,
        "adam_contract",
        done("adam_expand"),
    )
    new_in = adam(
        in_gradients,
        WEIGHT_DECAY,
        False,
        ids,
        in_sums,
        parts_first(project_in),
        parts_first(moment_project_in),
        parts_first(second_project_in),
        "adam_in",
        done("adam_contract"),
    )
    new_in = [parts_first(array) for array in new_in]
    small = sum(each[shard:, :shard].astype(F32) for each in in_sums[1:])
    small = behind(small, *done("adam_contract"))
    small = sum([tensor_swap(small, bit) for bit in (1, 2, 3)], small)
    grad_vectors = small[:vector_rows]
    grad_bias = small[vector_rows:small_rows].reshape(-1)
    change, first, second = adam_step(vectors, grad_vectors, moment_vectors, second_vectors, 0.0)
    new_vectors = (grad_vectors, change, first, second)
    change, first, second = adam_step(
        expand_bias, grad_bias, moment_expand_bias, second_expand_bias, 0.0
    )
    new_bias = (grad_bias, change, first, second)
    updated = (new_in, new_out, new_expand, new_contract, new_vectors, new_bias)
    return (
        block_output,
        input_grad,
        *[each[0] for each in updated],
        *[each[1] for each in updated],
        *[array for each in updated for array in each[2:]],
        grad_vectors[7],
    )


def solution(mesh):
    tokens = P("tensor", "fsdp", None)
    into = P("fsdp", None, "tensor")
    wide = P("fsdp", "tensor")
    tall = P("tensor", "fsdp")
    row = P(None, "fsdp")
    line = P("fsdp")
    params = (into, tall, wide, tall, row, line)
    moments = (into, into, tall, tall, wide, wide, tall, tall, row, row, line, line)
    return jax.shard_map(
        body,
        mesh=mesh,
        in_specs=(tokens, row, tokens) + params + moments,
        out_specs=(tokens, tokens) + params + params + moments + (line,),
        check_vma=False,
    )
```

```python
import functools

import jax
import jax.numpy as jnp
from jax import lax
from jax.experimental import pallas as pl
from jax.experimental.pallas import tpu as pltpu
from jax.sharding import PartitionSpec as P

HEAD_DIM = 64
STEP = 3
NORM_EPS = 1e-06
BETA_FIRST = 0.9
BETA_SECOND = 0.999
LEARN_RATE = 0.004
WEIGHT_DECAY = 0.04
ADAM_EPS = 1e-08
MASKED_SCORE = -1e30
ROOT_HALF = 0.7071067811865476
DENSITY_NORM = 0.3989422804014327
SCORE_SCALE = HEAD_DIM ** (-0.5)
LANES = 128
TILE = 352
CHUNK = 256
LONG = 4
SMALL = 16
LARGE = 32
ALL = 56
TOKENS = {}
F32 = jnp.float32
BF16 = jnp.bfloat16


def dot_nn(left, right):
    return lax.dot_general(left, right, (((1,), (0,)), ((), ())), preferred_element_type=F32)


def dot_nt(left, right):
    return lax.dot_general(left, right, (((1,), (1,)), ((), ())), preferred_element_type=F32)


def dot_tn(left, right):
    return lax.dot_general(left, right, (((0,), (0,)), ((), ())), preferred_element_type=F32)


def tiles_of(total, tile):
    return [(low, min(tile, total - low)) for low in range(0, total, tile)]


def norm_forward(values):
    center = jnp.mean(values, axis=-1, keepdims=True)
    offset = values - center
    spread = jnp.mean(offset * offset, axis=-1, keepdims=True)
    inverse = lax.rsqrt(spread + NORM_EPS)
    return offset * inverse, inverse


def norm_backward(scaled, inverse, grad_normed, norm_gain):
    grad_scaled = grad_normed * norm_gain
    first_mean = jnp.mean(grad_scaled, axis=-1, keepdims=True)
    second_mean = jnp.mean(grad_scaled * scaled, axis=-1, keepdims=True)
    return inverse * (grad_scaled - first_mean - scaled * second_mean)


def gelu_parts(hidden):
    normal_cdf = 0.5 * (1.0 + lax.erf(hidden * ROOT_HALF))
    density = DENSITY_NORM * jnp.exp(-0.5 * hidden * hidden)
    return (hidden * normal_cdf, normal_cdf + hidden * density)


def call(kernel, ids, args, in_specs, outs, out_specs, name, cost=(0, 0, 0), grid=(1,), scratch=(), aliases=None, after=(), vmem=SMALL):
    count = 1 + len(args)
    waits = len(after)
    token = shape_of((8, LANES), F32)

    def run(*refs):
        place = count + waits + len(outs)
        refs[place][...] = jnp.zeros_like(refs[place])
        kernel(*refs[:count], *refs[count + waits : place], *refs[place + 1 :])

    *results, done = pl.pallas_call(
        run,
        grid_spec=pltpu.PrefetchScalarGridSpec(
            num_scalar_prefetch=1,
            grid=grid,
            in_specs=list(in_specs) + [pl.BlockSpec(memory_space=pl.ANY)] * waits,
            out_specs=list(out_specs) + [whole(token)],
            scratch_shapes=scratch,
        ),
        out_shape=list(outs) + [token],
        input_output_aliases=aliases or {},
        compiler_params=pltpu.CompilerParams(vmem_limit_bytes=vmem * 2**20),
        cost_estimate=pl.CostEstimate(flops=cost[0], bytes_accessed=cost[1], transcendentals=cost[2]),
        name=name,
    )(ids, *args, *after)
    TOKENS[name] = done
    return results


def done(*names):
    return tuple(TOKENS[name] for name in names)


def whole(array):
    zeros = (0,) * len(array.shape)
    return pl.BlockSpec(array.shape, lambda *i: zeros)


def plain(kernel, ids, args, outs, name, **more):
    return call(kernel, ids, args, [whole(a) for a in args], outs, [whole(o) for o in outs], name, **more)


def shape_of(shape, dtype):
    return jax.ShapeDtypeStruct(shape, dtype)


ANYWHERE = pl.BlockSpec(memory_space=pl.ANY)


def low_bit(ids_ref):
    return lax.rem(ids_ref[0], 2)


def pack_kernel(ids_ref, in_ref, out_ref, expand_ref, contract_ref, small_ref, first, second, third):
    for pair, packed in enumerate((first, second)):
        for part in range(3):
            packed[:, part * LANES : (part + 1) * LANES] = in_ref[
                part, :, pair * LANES : (pair + 1) * LANES
            ].astype(BF16)
    first[:, 3 * LANES :] = small_ref[...].T.astype(BF16)
    second[:, 3 * LANES :] = out_ref[...].T.astype(BF16)
    hidden = expand_ref.shape[1]
    third[:, :hidden] = expand_ref[...].astype(BF16)
    third[:, hidden:] = contract_ref[...].T.astype(BF16)


def pack(ids, project_in, project_out, expand, contract, small):
    _, shard, head_width = project_in.shape
    widths = (4 * LANES, 3 * LANES + head_width, 2 * expand.shape[1])
    args = (project_in, project_out, expand, contract, small)
    outs = [shape_of((shard, width), BF16) for width in widths]
    return plain(pack_kernel, ids, args, outs, "pack", vmem=ALL)


def place_rows(ids_ref, near_ref, far_ref, write):
    count, shard = near_ref.shape[0], near_ref.shape[1]
    mine = ids_ref[0]
    for step in range(count):
        for low, ref in enumerate((near_ref, far_ref)):
            owner = lax.bitwise_xor(mine, 2 * step + low)
            write(pl.ds(pl.multiple_of(owner * shard, shard), shard), ref[step])


def flatten_kernel(ids_ref, normed_ref, flat_ref):
    flat_ref[...] = normed_ref[...].T


def flatten(ids, normed, after=()):
    seq, features = normed.shape
    return plain(flatten_kernel, ids, (normed,), [shape_of((features, seq), BF16)], "flatten", after=after)[0]


def unpack_kernel(ids_ref, near_ref, far_ref, out_ref):
    def write(at, values):
        out_ref[at, :] = values[:, 3 * LANES :]

    place_rows(ids_ref, near_ref, far_ref, write)


def unpack(ids, near, far, after=()):
    count, shard, width = near.shape
    outs = [shape_of((2 * count * shard, width - 3 * LANES), BF16)]
    return plain(unpack_kernel, ids, (near, far), outs, "unpack", after=after)[0]


def attend_kernel(pair, ids_ref, live_ref, near_ref, far_ref, normed_ref, *refs):
    if pair == 0:
        x_ref = normed_ref
        rows_ref, normed_ref, scaled_ref, held_ref = refs[0], refs[1], refs[2], refs[-1]
        weight_ref, qkv_ref, attended_ref, query_ref, key_ref, value_ref = refs[3:-1]
    else:
        rows_ref, weight_ref, qkv_ref, attended_ref, query_ref, key_ref, value_ref = refs
    seq = normed_ref.shape[0]
    width = 3 * LANES

    def write(at, values):
        weight_ref[at, :] = values[:, :width]
        if pair == 0:
            held_ref[at, :] = values[:, width:].astype(F32)

    place_rows(ids_ref, near_ref, far_ref, write)
    if pair == 0:
        rows_ref[...] = held_ref[...].T[0 : rows_ref.shape[0]]
    start = pl.multiple_of(ids_ref[1] * (2 * LANES) + pair * LANES, LANES)
    bias_row = jnp.concatenate(
        [rows_ref[2:3, pl.ds(start, LANES)], jnp.zeros((1, LANES), F32), rows_ref[3:4, pl.ds(start, LANES)]],
        axis=1,
    )
    for low, count in tiles_of(seq, TILE):
        at = slice(low, low + count)
        if pair == 0:
            scaled, _ = norm_forward(x_ref[at, :].astype(F32))
            scaled_ref[at, :] = scaled.astype(BF16)
            normed_ref[at, :] = (scaled * rows_ref[0:1, :] + rows_ref[1:2, :]).astype(BF16)
        mixed = dot_nn(normed_ref[at, :], weight_ref[...]) + bias_row
        qkv_ref[at, :] = mixed.astype(BF16)
    lane = lax.broadcasted_iota(jnp.int32, (seq, LANES), 1)
    bias = jnp.where(live_ref[...] > 0, 0.0, MASKED_SCORE).astype(F32)
    key_rows = qkv_ref[:, LANES : 2 * LANES].astype(F32)
    value_rows = qkv_ref[:, 2 * LANES : 3 * LANES].astype(F32)
    for head in range(2):
        own = (lane // HEAD_DIM) == head
        spare = HEAD_DIM * (1 - head)
        extra = jnp.where(lane == spare, bias, 0.0)
        key_ref[head] = jnp.where(own, key_rows, extra).astype(BF16)
        extra = jnp.where(lane == spare, 1.0, 0.0)
        value_ref[head] = jnp.where(own, value_rows, extra).astype(BF16)
    for low, count in tiles_of(seq, TILE):
        at = slice(low, low + count)
        lane = lax.broadcasted_iota(jnp.int32, (count, LANES), 1)
        queries = qkv_ref[at, 0:LANES].astype(F32) * SCORE_SCALE
        both = None
        for head in range(2):
            own = (lane // HEAD_DIM) == head
            spare = HEAD_DIM * (1 - head)
            extra = jnp.where(lane == spare, 1.0, 0.0)
            mine = jnp.where(own, queries, extra).astype(BF16)
            scores = dot_nt(mine, key_ref[head])
            highest = jnp.max(scores, axis=-1, keepdims=True)
            weights = jnp.exp(scores - highest).astype(BF16)
            output = dot_nn(weights, value_ref[head])
            summed = output[:, spare : spare + 1]
            output = output / summed
            both = output if head == 0 else jnp.where(own, output, both)
            rest = -(highest + jnp.log(summed))
            extra = jnp.where(lane == spare + 3, 1.0, 0.0)
            for place in range(3):
                part = rest.astype(BF16).astype(F32)
                extra = jnp.where(lane == spare + place, part, extra)
                rest = rest - part
            query_ref[at, LANES * head : LANES * (head + 1)] = jnp.where(
                own, queries, extra
            ).astype(BF16)
        attended_ref[at, :] = both.astype(BF16)


def attend(pair, ids, live, near, far, normed, rows=None, after=()):
    seq, features = normed.shape
    outs = [
        shape_of((features, 3 * LANES), BF16),
        shape_of((seq, 3 * LANES), BF16),
        shape_of((seq, LANES), BF16),
        shape_of((seq, 2 * LANES), BF16),
    ]
    scratch = [pltpu.VMEM((2, seq, LANES), BF16), pltpu.VMEM((2, seq, LANES), BF16)]
    args = (live, near, far, normed)
    if pair == 0:
        outs = [shape_of((16, features), F32)] + [shape_of((seq, features), BF16)] * 2 + outs
        scratch.append(pltpu.VMEM((features, LANES), F32))
    else:
        args += (rows,)
    return plain(
        functools.partial(attend_kernel, pair),
        ids,
        args,
        outs,
        f"attend_{pair}",
        cost=(LONG * 160 * seq * seq * HEAD_DIM, 0, 0),
        vmem=LARGE,
        scratch=scratch,
        after=after,
    )


def attend_back_kernel(
    ids_ref,
    live_ref,
    qkv_ref,
    query_ref,
    attended_ref,
    mine_a,
    other_a,
    mine_b,
    other_b,
    out_ref,
    mixed_ref,
    sums_ref,
    grad_ref,
    held_ref,
    query_sum_ref,
):
    seq = qkv_ref.shape[0]
    rows = mine_a.shape[0]
    core = ids_ref[2]
    for index, ref in enumerate((mine_a, other_a, mine_b, other_b)):
        block = 2 * (index // 2) + lax.bitwise_xor(core, index % 2)
        grad_ref[pl.ds(pl.multiple_of(block * rows, 8), rows), :] = dot_nn(ref[...], out_ref[...])
    lane = lax.broadcasted_iota(jnp.int32, (seq, LANES), 1)
    grad = grad_ref[...].astype(BF16).astype(F32)
    product = grad * attended_ref[...].astype(F32)
    for head in range(2):
        own = (lane // HEAD_DIM) == head
        spare = HEAD_DIM * (1 - head)
        inner = -jnp.sum(jnp.where(own, product, 0.0), axis=-1, keepdims=True)
        first = inner.astype(BF16).astype(F32)
        extra = jnp.where(lane == spare, first, jnp.where(lane == spare + 1, inner - first, 0.0))
        held_ref[head] = jnp.where(own, grad, extra).astype(BF16)
    value_sum = jnp.zeros((1, LANES), F32)
    for index, (low, count) in enumerate(tiles_of(seq, TILE)):
        at = slice(low, low + count)
        lane = lax.broadcasted_iota(jnp.int32, (count, LANES), 1)
        bias = jnp.where(live_ref[at, :] > 0, 0.0, MASKED_SCORE).astype(F32)
        key_rows = qkv_ref[at, LANES : 2 * LANES].astype(F32)
        value_rows = qkv_ref[at, 2 * LANES : 3 * LANES].astype(F32)
        grad_keys = grad_values = None
        for head in range(2):
            own = (lane // HEAD_DIM) == head
            spare = HEAD_DIM * (1 - head)
            ones = jnp.where((lane >= spare) & (lane < spare + 3), 1.0, 0.0)
            extra = jnp.where(lane == spare + 3, bias, ones)
            keys = jnp.where(own, key_rows, extra).astype(BF16)
            values = jnp.where(own, value_rows, ones).astype(BF16)
            queries = query_ref[:, LANES * head : LANES * (head + 1)]
            above = held_ref[head]
            weights = jnp.exp(dot_nt(keys, queries))
            grad_scores = (weights * dot_nt(values, above)).astype(BF16)
            value_part = dot_nn(weights.astype(BF16), above)
            key_part = dot_nn(grad_scores, queries)
            part = slice(HEAD_DIM * head, HEAD_DIM * (head + 1))
            query_part = dot_tn(keys, grad_scores)[part]
            if index == 0:
                query_sum_ref[part] = query_part
            else:
                query_sum_ref[part] += query_part
            grad_keys = key_part if head == 0 else jnp.where(own, key_part, grad_keys)
            grad_values = value_part if head == 0 else jnp.where(own, value_part, grad_values)
        grad_values = grad_values.astype(BF16)
        mixed_ref[at, LANES : 2 * LANES] = grad_keys.astype(BF16)
        mixed_ref[at, 2 * LANES : 3 * LANES] = grad_values
        value_sum += jnp.sum(grad_values.astype(F32), axis=0, keepdims=True)
    grad_queries = (query_sum_ref[...].T * SCORE_SCALE).astype(BF16)
    mixed_ref[:, 0:LANES] = grad_queries
    sums_ref[0:1, :] = jnp.sum(grad_queries.astype(F32), axis=0, keepdims=True)
    sums_ref[1:2, :] = value_sum


def attend_back(pair, ids, live, qkv, queries, attended, grads, out_own, after=()):
    seq = qkv.shape[0]
    features = out_own.shape[0]
    outs = [shape_of((seq, 3 * LANES), BF16), shape_of((8, LANES), F32)]
    args = (live, qkv, queries, attended, *grads)
    return call(
        attend_back_kernel,
        ids,
        (*args, out_own),
        [whole(a) for a in args] + [pl.BlockSpec((features, LANES), lambda i, _: (0, pair))],
        outs,
        [whole(o) for o in outs],
        f"attend_back_{pair}",
        cost=((1 - pair) * 80 * seq * seq * HEAD_DIM, 0, 0),
        vmem=LARGE,
        scratch=[
            pltpu.VMEM((seq, LANES), F32),
            pltpu.VMEM((2, seq, LANES), BF16),
            pltpu.VMEM((LANES, seq), F32),
        ],
        after=after,
    )


def middle_kernel(ids_ref, x_ref, *refs):
    att_refs, out_refs = refs[:8], refs[8:12]
    rows_ref, expand_ref, contract_ref, bias_ref, top_ref = refs[12:17]
    outs = refs[-14:-5]
    normed_ref, act_ref, hidden_ref = outs[:3]
    branch_refs, attn_ref, back_refs, sums_ref = outs[3:5], outs[5], outs[6:8], outs[8]
    held_ref, normed_held, act_held, hidden_held, grad_held = refs[-5:]
    step = pl.program_id(0)

    @pl.when(step == 0)
    def _():
        sums_ref[...] = jnp.zeros_like(sums_ref)

    attn_sum = rows_ref[4:5, :]
    for device, out_ref in enumerate(out_refs):
        held_ref[:, :LANES] = att_refs[2 * device][0]
        held_ref[:, LANES:] = att_refs[2 * device + 1][0]
        attn_sum = attn_sum + dot_nt(held_ref[...], out_ref[...])

    @pl.when(lax.rem(step, 2) == 1)
    def _():
        attn_ref[0] = attn_sum.astype(BF16)

    residual = x_ref[0].astype(F32) + rows_ref[5:6, :] * attn_sum
    scaled, _ = norm_forward(residual)
    normed_held[...] = (scaled * rows_ref[6:7, :] + rows_ref[7:8, :]).astype(BF16)
    normed_ref[0] = normed_held[...]
    grad_held[...] = (top_ref[0].astype(F32) * rows_ref[9:10, :]).astype(BF16)
    for low in range(0, act_held.shape[1], CHUNK):
        at = slice(low, low + CHUNK)
        activated, slope = gelu_parts(dot_nn(normed_held[...], expand_ref[:, at]) + bias_ref[:, at])
        act_held[:, at] = activated.astype(BF16)
        grad_hidden = (dot_nn(grad_held[...], contract_ref[:, at]) * slope).astype(BF16)
        hidden_held[:, at] = grad_hidden
        sums_ref[0:1, at] += jnp.sum(grad_hidden.astype(F32), axis=0, keepdims=True)
    act_ref[0] = act_held[...]
    hidden_ref[0] = hidden_held[...]
    back = dot_nt(hidden_held[...], expand_ref[...])
    sums_ref[1:2, :] += jnp.sum(back * scaled, axis=0, keepdims=True)
    sums_ref[2:3, :] += jnp.sum(back, axis=0, keepdims=True)
    branch = dot_nt(act_held[...], contract_ref[...]).astype(BF16)
    for index in range(2):

        @pl.when(lax.rem(step, 2) == index)
        def _():
            back_refs[index][0] = back.astype(BF16)
            branch_refs[index][0] = branch


def middle(ids, x_full, att, out_all, rows, weights, bias, top_full, after=()):
    _, count, features = x_full.shape
    hidden = weights.shape[1] // 2

    def block(i, ids_ref):
        return 2 * lax.div(i, 2) + lax.bitwise_xor(ids_ref[2], 1 - lax.rem(i, 2))

    part = lambda n: pl.BlockSpec((1, count, n), lambda i, ids_ref: (block(i, ids_ref), 0, 0))
    held = pl.BlockSpec((1, count, features), lambda i, _: (lax.div(i, 2), 0, 0))
    column = lambda c: pl.BlockSpec((features, hidden), lambda i, _: (0, c))
    sums = shape_of((8, features), F32)
    outs = [shape_of((4, count, n), BF16) for n in (features, hidden, hidden)]
    outs += [shape_of((2, count, features), BF16)] * 5 + [sums]
    specs = [part(features), part(hidden), part(hidden)] + [held] * 5 + [whole(sums)]
    seq = 4 * count
    return call(
        middle_kernel,
        ids,
        (x_full, *att, *out_all, rows, weights, weights, bias, top_full),
        [part(features)]
        + [part(LANES)] * len(att)
        + [whole(o) for o in out_all]
        + [whole(rows), column(0), column(1), whole(bias), part(features)],
        outs,
        specs,
        "middle",
        cost=(2 * seq * features * (features + 4 * hidden), 0, 0),
        grid=(4,),
        scratch=[pltpu.VMEM((count, 2 * LANES), BF16)] + [pltpu.VMEM((count, features), BF16)] * 4,
        after=after,
        vmem=ALL,
    )


def pair_sum_kernel(ids_ref, keep_ref, arrived_ref, sum_ref):
    sum_ref[...] = (keep_ref[...].astype(F32) + arrived_ref[...].astype(F32)).astype(BF16)


def pair_sum(half, ids, keep, arrived):
    _, count, features = keep.shape
    part = pl.BlockSpec((None, count, features), lambda i, _: (half, 0, 0))
    out = shape_of((count, features), BF16)
    return call(
        pair_sum_kernel, ids, (keep, arrived), [part, part], [out], [whole(out)], f"back_sum_{half}"
    )[0]


def split_sum_kernel(ids_ref, keep_ref, arrived_ref, give_ref, stay_ref):
    half = ids_ref[3]
    total = keep_ref[...].astype(F32) + arrived_ref[...].astype(F32)
    give_ref[...] = jnp.where(half == 0, total[1], total[0]).astype(BF16)
    stay_ref[...] = jnp.where(half == 0, total[0], total[1]).astype(BF16)


def split_sum(ids, keep, arrived, name, after=()):
    outs = [shape_of(keep.shape[1:], BF16)] * 2
    return plain(split_sum_kernel, ids, (keep, arrived), outs, name, after=after)


def residual_kernel(ids_ref, chip_ref, arrived_ref, x_ref, attn_ref, top_ref, rows_ref, grad_ref, residual_ref):
    total = chip_ref[...].astype(F32) + arrived_ref[...].astype(F32)
    attn_sum = attn_ref[...].astype(F32)
    scaled, inverse = norm_forward(x_ref[0].astype(F32) + rows_ref[5:6, :] * attn_sum)
    grad = top_ref[0].astype(F32) + norm_backward(scaled, inverse, total, rows_ref[6:7, :])
    residual_ref[...] = grad.astype(BF16)
    grad_ref[...] = (grad * rows_ref[5:6, :]).astype(BF16)


def residual_back(half, ids, chip, arrived, x_full, attn, top_full, rows, after=()):
    count, features = chip.shape
    part = pl.BlockSpec((1, count, features), lambda i, ids_ref: (2 * half + ids_ref[2], 0, 0))
    held = pl.BlockSpec((None, count, features), lambda i, _: (half, 0, 0))
    outs = [shape_of((count, features), BF16)] * 2
    return call(
        residual_kernel,
        ids,
        (chip, arrived, x_full, attn, top_full, rows),
        [whole(chip), whole(arrived), part, held, part, whole(rows)],
        outs,
        [whole(out) for out in outs],
        f"residual_back_{half}",
        after=after,
        vmem=ALL,
    )


def own_kernel(
    ids_ref, x_ref, top_ref, attn_ref, grad_a, grad_b, stay_ref, branch_ref, rows_ref, output_ref, sums_ref
):
    first = ids_ref[3] == 0
    choose = lambda a, b: jnp.where(first, a[...].astype(F32), b[...].astype(F32))
    attn_sum = attn_ref[...].astype(F32)
    grad = choose(grad_a, grad_b)
    branch = stay_ref[...].astype(F32) + branch_ref[...].astype(F32) + rows_ref[8:9, :]
    output_ref[:, 0, :] = x_ref[0].astype(F32) + rows_ref[5:6, :] * attn_sum + rows_ref[9:10, :] * branch
    top = top_ref[0].astype(F32)
    for row, values in enumerate((grad * rows_ref[5:6, :], grad * attn_sum, top * rows_ref[9:10, :], top * branch)):
        sums_ref[row : row + 1, :] = jnp.sum(values, axis=0, keepdims=True)


def own_block(ids, x_full, top_full, attn, grads, stay, branch, rows, after=()):
    _, count, features = x_full.shape
    part = pl.BlockSpec((1, count, features), lambda i, ids_ref: (ids_ref[1], 0, 0))
    outs = [shape_of((count, 1, features), F32), shape_of((8, features), F32)]
    held = pl.BlockSpec((None, count, features), lambda i, ids_ref: (ids_ref[3], 0, 0))
    rest = (*grads, stay, branch, rows)
    return call(
        own_kernel,
        ids,
        (x_full, top_full, attn, *rest),
        [part, part, held] + [whole(a) for a in rest],
        outs,
        [whole(o) for o in outs],
        "own_block",
        after=after,
        vmem=24,
    )


def matrices_kernel(ids_ref, left_a, top_ref, right_a, right_b, rows_ref, out_ref, flat_ref):
    step = pl.program_id(0)
    per = pl.num_programs(0) // 2

    @pl.when(step == 0)
    def _():
        flat_ref[...] = left_a[...].T

    @pl.when(step == per)
    def _():
        flat_ref[...] = (top_ref[...].astype(F32) * rows_ref[9:10, :]).astype(BF16).T

    right = jnp.where(step < per, right_a[...], right_b[...])
    out_ref[...] = dot_nn(flat_ref[...], right).astype(BF16)


def matrices(ids, normed, hidden, top_full, activated, rows, after=()):
    seq, features = normed.shape
    width = hidden.shape[1]
    block = 512
    per = width // block
    out = shape_of((features, 2 * width), BF16)
    top = top_full.reshape(seq, features)
    return call(
        matrices_kernel,
        ids,
        (normed, top, hidden, activated, rows),
        [
            whole(normed),
            whole(top),
            pl.BlockSpec((seq, block), lambda i, _: (0, jnp.minimum(i, per - 1))),
            pl.BlockSpec((seq, block), lambda i, _: (0, jnp.maximum(i - per, 0))),
            whole(rows),
        ],
        [out],
        [pl.BlockSpec((features, block), lambda i, _: (0, i))],
        "matrices",
        grid=(2 * per,),
        scratch=[pltpu.VMEM((features, seq), BF16)],
        after=after,
        vmem=ALL,
    )[0]


def store_shards(ids_ref, index, values, give_ref, keep_ref):
    @pl.when(low_bit(ids_ref) == index % 2)
    def _():
        keep_ref[index // 2] = values

    @pl.when(low_bit(ids_ref) != index % 2)
    def _():
        give_ref[index // 2] = values


def out_grad_kernel(ids_ref, att_a, att_b, mine_a, other_a, mine_b, other_b, give_ref, keep_ref):
    core = ids_ref[2]
    total = [None, None]
    for index, ref in enumerate((mine_a, other_a, mine_b, other_b)):
        block = 2 * (index // 2) + lax.bitwise_xor(core, index % 2)
        for pair, att_ref in enumerate((att_a, att_b)):
            part = dot_tn(att_ref[block], ref[...])
            total[pair] = part if index == 0 else total[pair] + part
    count, shard, _ = give_ref.shape
    values = jnp.concatenate([t.T for t in total], axis=1).astype(BF16)
    for place in range(2 * count):
        store_shards(ids_ref, place, values[place * shard : (place + 1) * shard], give_ref, keep_ref)


def out_grad(ids, attended, grads, places, after=()):
    count, features = grads[0].shape
    outs = [shape_of((places // 2, features // places, 2 * LANES), BF16)] * 2
    args = [a.reshape(4, count, LANES) for a in attended] + list(grads)
    return plain(out_grad_kernel, ids, args, outs, "out_grad", after=after)


def in_grad_kernel(ids_ref, flat_ref, mixed_ref, *refs):
    if len(refs) > 2:
        base_ref, input_ref, own_ref, first_ref, second_ref, give_ref, keep_ref, small_ref = refs
        small_ref[...] = base_ref[...]
        small_ref[0:2, :] = input_ref[0:2, :]
        small_ref[4:5, :] = own_ref[0:1, :]
        small_ref[5:6, :] = own_ref[1:2, :]
        small_ref[8:9, :] = own_ref[2:3, :]
        small_ref[9:10, :] = own_ref[3:4, :]
        for pair, head_ref in enumerate((first_ref, second_ref)):
            start = pl.multiple_of(ids_ref[1] * (2 * LANES) + pair * LANES, LANES)
            small_ref[2:3, pl.ds(start, LANES)] = head_ref[0:1, :]
            small_ref[3:4, pl.ds(start, LANES)] = head_ref[1:2, :]
    else:
        give_ref, keep_ref = refs
    count, held, width = give_ref.shape
    values = dot_nn(flat_ref[...], mixed_ref[...]).astype(BF16)
    shard = values.shape[0] // (2 * count)
    for place in range(2 * count):
        at = slice(place * shard, (place + 1) * shard)
        part = values[at]
        if held > shard:
            below = small_ref[:, at].astype(BF16)
            below = jnp.concatenate([below, jnp.zeros((held - shard, width - shard), BF16)], axis=1)
            part = jnp.concatenate([part, below])
        store_shards(ids_ref, place, part, give_ref, keep_ref)


def in_grad(pair, ids, flat, mixed, places, after=(), small=()):
    features = flat.shape[0]
    held, scratch = features // places, []
    if small:
        held += small[0].shape[0]
        scratch = [pltpu.VMEM(small[0].shape, F32)]
    outs = [shape_of((places // 2, held, mixed.shape[1]), BF16)] * 2
    args = (flat, mixed, *small)
    return plain(in_grad_kernel, ids, args, outs, f"in_grad_{pair}", after=after, scratch=scratch)


def low_sum_kernel(parts, ids_ref, *refs):
    out_refs = refs[2 * parts :]
    high = lax.div(ids_ref[0], 2)
    for step, out_ref in enumerate(out_refs):
        at = lax.bitwise_xor(high, step)
        low = 0
        for keep_ref, arrived_ref in zip(refs[0 : 2 * parts : 2], refs[1 : 2 * parts : 2]):
            width = keep_ref.shape[2]
            total = keep_ref[at].astype(F32) + arrived_ref[at].astype(F32)
            out_ref[:, low : low + width] = total.astype(BF16)
            low += width


def low_sum(ids, pairs, name, after=()):
    count, held, _ = pairs[0].shape
    outs = [shape_of((held, sum(a.shape[2] for a in pairs[::2])), BF16)] * count
    kernel = functools.partial(low_sum_kernel, len(pairs) // 2)
    return plain(kernel, ids, pairs, outs, name, after=after)


def input_back_kernel(ids_ref, scaled_ref, mixed_a, mixed_b, weight_a, weight_b, give_ref, keep_ref, sums_ref):
    step = pl.program_id(0)

    @pl.when(step == 0)
    def _():
        sums_ref[...] = jnp.zeros_like(sums_ref)

    total = dot_nt(mixed_a[0], weight_a[...]) + dot_nt(mixed_b[0], weight_b[...])
    sums_ref[0:1, :] += jnp.sum(total * scaled_ref[0].astype(F32), axis=0, keepdims=True)
    sums_ref[1:2, :] += jnp.sum(total, axis=0, keepdims=True)

    @pl.when(step < 2)
    def _():
        give_ref[0] = total.astype(BF16)

    @pl.when(step >= 2)
    def _():
        keep_ref[0] = total.astype(BF16)


def input_back(ids, scaled, mixed, weights, after=()):
    _, count, features = scaled.shape
    width = mixed[0].shape[2]
    def part(n):
        return pl.BlockSpec(
            (1, count, n),
            lambda i, ids_ref: (2 * lax.rem(i, 2) + lax.bitwise_xor(ids_ref[2], 1 - lax.div(i, 2)), 0, 0),
        )
    outs = [shape_of((2, count, features), BF16)] * 2 + [shape_of((8, features), F32)]
    return call(
        input_back_kernel,
        ids,
        (scaled, *mixed, *weights),
        [part(features), part(width), part(width)] + [whole(w) for w in weights],
        outs,
        [
            pl.BlockSpec((1, count, features), lambda i, _: (jnp.minimum(i, 1), 0, 0)),
            pl.BlockSpec((1, count, features), lambda i, _: (jnp.maximum(i - 2, 0), 0, 0)),
            whole(outs[2]),
        ],
        "input_back",
        grid=(4,),
        after=after,
    )


def input_kernel(ids_ref, stay_ref, arrived_ref, x_ref, grad_a, grad_b, rows_ref, out_ref):
    total = stay_ref[...].astype(F32) + arrived_ref[...].astype(F32)
    scaled, inverse = norm_forward(x_ref[0].astype(F32))
    grad = jnp.where(ids_ref[3] == 0, grad_a[...].astype(F32), grad_b[...].astype(F32))
    out_ref[:, 0, :] = grad + norm_backward(scaled, inverse, total, rows_ref[0:1, :])


def input_grad_of(ids, stay, arrived, x_full, grads, rows, after=()):
    _, count, features = x_full.shape
    part = pl.BlockSpec((1, count, features), lambda i, ids_ref: (ids_ref[1], 0, 0))
    outs = [shape_of((count, 1, features), F32)]
    return call(
        input_kernel,
        ids,
        (stay, arrived, x_full, *grads, rows),
        [whole(stay), whole(arrived), part, whole(grads[0]), whole(grads[1]), whole(rows)],
        outs,
        [whole(o) for o in outs],
        "input_grad",
        after=after,
    )[0]


def adam_step(master, gradient, first, second, decay):
    first_new = BETA_FIRST * first + (1.0 - BETA_FIRST) * gradient
    second_new = BETA_SECOND * second + (1.0 - BETA_SECOND) * gradient * gradient
    first_hat = first_new / (1.0 - BETA_FIRST**STEP)
    second_hat = second_new / (1.0 - BETA_SECOND**STEP)
    change = -LEARN_RATE * (first_hat / (jnp.sqrt(second_hat) + ADAM_EPS) + decay * master)
    return (change, first_new, second_new)


def adam_kernel(gradients, decay, keep_change, ids_ref, *refs):
    count = len(refs) - 7
    parts, (master, first, second), outs = refs[:count], refs[count:-4], refs[-4:]
    for at, gradient in gradients(parts):
        change, first_new, second_new = adam_step(master[at], gradient, first[at], second[at], decay)
        outs[0][at] = gradient
        outs[1][at] = change if keep_change else master[at] + change
        outs[2][at] = first_new
        outs[3][at] = second_new


def adam(gradients, decay, keep_change, ids, parts, master, first, second, name, after=()):
    outs = [shape_of(master.shape, F32)] * 4
    return plain(
        functools.partial(adam_kernel, gradients, decay, keep_change),
        ids,
        (*parts, master, first, second),
        outs,
        name,
        after=after,
    )


def sum_refs(refs):
    total = refs[0][...].astype(F32)
    for ref in refs[1:]:
        total = total + ref[...].astype(F32)
    return total


def high_sum_kernel(ids_ref, *refs):
    refs[-1][...] = sum_refs(refs[:-1])


def high_sum(ids, parts, name, after=()):
    out = shape_of(parts[0].shape, F32)
    return plain(high_sum_kernel, ids, parts, [out], name, after=after)[0]


def in_gradients(parts):
    totals = (parts[0][...], sum_refs(parts[1:]))
    for pair, total in enumerate(totals):
        columns = slice(pair * LANES, (pair + 1) * LANES)
        for part in range(3):
            values = total[: parts[0].shape[0], part * LANES : (part + 1) * LANES]
            yield (part, slice(None), columns), values


def out_gradients(parts):
    yield (slice(None), slice(None)), parts[0][:, 3 * LANES :].T


def expand_gradients(parts):
    yield (slice(None), slice(None)), parts[0][:, : parts[0].shape[1] // 2].astype(F32)


def contract_gradients(parts):
    yield (slice(None), slice(None)), parts[0][:, parts[0].shape[1] // 2 :].astype(F32).T


def tensor_swap(array, bit):
    return lax.ppermute(array, "tensor", [(rank, rank ^ bit) for rank in range(4)])


def fsdp_swap(array, bit):
    size = lax.axis_size("fsdp")
    return lax.ppermute(array, "fsdp", [(rank, rank ^ bit) for rank in range(size)])


def behind(array, *others):
    return lax.optimization_barrier((array,) + others)[0]


def around(array, *first):
    across = tensor_swap(array, 2)
    corner = tensor_swap(behind(across, *first) if first else across, 1)
    return (array, tensor_swap(array, 1), across, corner)


def gather_positions(block, rank, *first):
    full = jnp.zeros((4,) + block.shape, block.dtype)
    for bit, piece in enumerate(around(block, *first)):
        full = lax.dynamic_update_slice_in_dim(full, piece[None], rank ^ bit, 0)
    return full


def gather_shards(piece):
    count = lax.axis_size("fsdp") // 2
    near = jnp.stack([piece] + [fsdp_swap(piece, 2 * step) for step in range(1, count)])
    return near, fsdp_swap(near, 1)


def body(
    block_input,
    live_mask,
    cotangent,
    project_in,
    project_out,
    expand,
    contract,
    vectors,
    expand_bias,
    moment_project_in,
    second_project_in,
    moment_project_out,
    second_project_out,
    moment_expand,
    second_expand,
    moment_contract,
    second_contract,
    moment_vectors,
    second_vectors,
    moment_expand_bias,
    second_expand_bias,
):
    rows, _, features = block_input.shape
    shard, _, head_width = project_in.shape
    hidden_width = expand.shape[1]
    seq = 4 * rows
    places = lax.axis_size("fsdp")
    rank = lax.axis_index("tensor")
    place = lax.axis_index("fsdp")
    ids = jnp.stack([place, rank, rank % 2, rank // 2]).astype(jnp.int32)
    parts_first = lambda array: array.transpose(1, 0, 2)

    bias_shard = expand_bias.reshape(-1, shard)
    vector_rows = vectors.shape[0]
    small_rows = vector_rows + bias_shard.shape[0]
    small_shard = jnp.concatenate(
        [vectors, bias_shard, jnp.zeros((LANES - small_rows, shard), F32)]
    )
    packed = pack(ids, parts_first(project_in), project_out, expand, contract, small_shard)
    first_shards = gather_shards(packed[0])
    second_shards = gather_shards(behind(packed[1], first_shards[0]))
    weights = lax.all_gather(
        behind(packed[2], first_shards[0]), "fsdp", axis=0, tiled=True
    )

    x_own = block_input[:, 0]
    live_own = lax.dynamic_slice_in_dim(live_mask, rank * rows, rows, 0) > 0
    top_own = cotangent[:, 0] * live_own.astype(F32)
    x_full = gather_positions(x_own.astype(BF16), rank)
    top_full = gather_positions(behind(top_own.astype(BF16), x_full), rank)

    rows_now, normed_one, scaled_one, *heads = attend(
        0, ids, live_mask, *first_shards, x_full.reshape(seq, features)
    )
    heads = [heads]
    out_own = unpack(ids, *second_shards, after=done("attend_0"))
    heads.append(attend(1, ids, live_mask, *second_shards, normed_one, rows_now, done("unpack")))
    normed_flat = flatten(ids, normed_one, done("attend_1"))
    held = done("flatten")
    out_all = around(out_own)
    att_sets = [around(each[2]) for each in heads]
    att_all = [
        att_sets[pair][device].reshape(4, rows, LANES) for device in range(4) for pair in range(2)
    ]
    bias_now = rows_now[vector_rows:small_rows]
    bias_now = bias_now.reshape(-1, places, shard).transpose(1, 0, 2).reshape(1, -1)
    bias_here = lax.dynamic_slice_in_dim(bias_now, rank * hidden_width, hidden_width, 1)

    kept = middle(ids, x_full, att_all, out_all, rows_now, weights, bias_here, top_full, held)
    normed_two, activated, grad_hidden = [array.reshape(seq, array.shape[2]) for array in kept[:3]]
    branch_give, branch_keep, attn, back_give, back_keep, sums = kept[3:]
    back_arrived = tensor_swap(back_give, 1)
    chips, arrived, grads, grads_peer = [], [], [], []
    for half in range(2):
        chips.append(pair_sum(half, ids, back_keep, back_arrived))
        arrived.append(tensor_swap(chips[half], 2))
    grad_second = matrices(
        ids, normed_two, grad_hidden, top_full, activated, rows_now, done("back_sum_1")
    )
    lay = lambda values, start, total: lax.dynamic_update_slice_in_dim(
        jnp.zeros((total,), F32), values, start, 0
    )
    grad_bias = lay(sums[0], rank * hidden_width, expand_bias.shape[0] * places)
    grad_bias = grad_bias.reshape(places, -1, shard).transpose(1, 0, 2).reshape(-1, features)
    none = jnp.zeros((6, features), F32)
    small = jnp.concatenate([none, sums[1:3], none[:2], grad_bias, none[: 16 - small_rows]])

    branch_arrived = tensor_swap(behind(branch_give, chips[1]), 1)
    for half in range(2):
        wait = done("matrices")
        if half == 1:
            give, branch_stay = split_sum(
                ids, branch_keep, branch_arrived, "branch_sum", done("residual_back_0")
            )
            branch_arrived = tensor_swap(give, 2)
            wait = done("branch_sum") + (small,)
        grads.append(
            residual_back(
                half, ids, chips[half], arrived[half], x_full, attn, top_full, rows_now, wait
            )
        )
        grads_peer.append(tensor_swap(grads[half][0], 1))
    attn_grads = (grads[0][0], grads_peer[0], grads[1][0], grads_peer[1])
    residual_grads = (grads[0][1], grads[1][1])
    second_sum = lax.psum_scatter(
        behind(grad_second, arrived[0]), "fsdp", scatter_dimension=0, tiled=True
    )

    sends = lambda low: [low[0]] + [fsdp_swap(low[step], 2 * step) for step in range(1, places // 2)]
    mixed, head_sums = [], []
    wait = done("residual_back_1")
    for pair in range(2):
        weight, qkv, attended, queries = heads[pair]
        mixed_pair, pair_sums = attend_back(
            pair, ids, live_mask, qkv, queries, attended, attn_grads, out_own, wait
        )
        mixed.append(mixed_pair)
        head_sums.append(pair_sums)
        if pair == 0:
            in_give, in_keep = in_grad(0, ids, normed_flat, mixed_pair, places)
            in_arrived = fsdp_swap(in_give, 1)
            block_output, own_sums = own_block(
                ids,
                x_full,
                top_full,
                attn,
                residual_grads,
                branch_stay,
                branch_arrived,
                rows_now,
                done("in_grad_0"),
            )
            out_give, out_keep = out_grad(
                ids, [each[2] for each in heads], attn_grads, places, done("own_block")
            )
            out_arrived = fsdp_swap(out_give, 1)
            wait = done("out_grad")
    first_sums = sends(
        low_sum(ids, (in_keep, in_arrived, out_keep, out_arrived), "in_low_0", done("attend_back_1"))
    )
    input_give, input_keep, input_sums = input_back(
        ids,
        scaled_one.reshape(4, rows, features),
        [each.reshape(4, rows, each.shape[1]) for each in mixed],
        [each[0] for each in heads],
        done("in_low_0"),
    )

    in_give, in_keep = in_grad(
        1, ids, normed_flat, mixed[1], places, (), (small, input_sums, own_sums, *head_sums)
    )
    in_arrived = fsdp_swap(in_give, 1)
    give, stay = split_sum(ids, input_keep, tensor_swap(input_give, 1), "input_sum", done("in_grad_1"))
    input_arrived = tensor_swap(give, 2)
    in_low = low_sum(
        ids, (in_keep, in_arrived), "in_low_1", done("input_sum")
    )
    second_sums = sends(in_low)
    input_grad = input_grad_of(
        ids, stay, input_arrived, x_full, residual_grads, rows_now, done("in_low_1")
    )
    sum_first = high_sum(ids, first_sums, "in_sum_0", done("input_grad"))
    in_sums = [sum_first] + second_sums
    new_out = adam(
        out_gradients,
        WEIGHT_DECAY,
        True,
        ids,
        (sum_first,),
        project_out,
        moment_project_out,
        second_project_out,
        "adam_out",
        done("in_sum_0"),
    )
    second = (second_sum,)
    new_expand = adam(
        expand_gradients,
        WEIGHT_DECAY,
        False,
        ids,
        second,
        expand,
        moment_expand,
        second_expand,
        "adam_expand",
        done("adam_out"),
    )
    new_contract = adam(
        contract_gradients,
        WEIGHT_DECAY,
        False,
        ids,
        second,
        contract,
        moment_contract,
        second_contract,
        "adam_contract",
        done("adam_expand"),
    )
    new_in = adam(
        in_gradients,
        WEIGHT_DECAY,
        False,
        ids,
        in_sums,
        parts_first(project_in),
        parts_first(moment_project_in),
        parts_first(second_project_in),
        "adam_in",
        done("adam_contract"),
    )
    new_in = [parts_first(array) for array in new_in]
    small = sum(each[shard:, :shard].astype(F32) for each in in_sums[1:])
    small = behind(small, *done("adam_contract"))
    small = sum([tensor_swap(small, bit) for bit in (1, 2, 3)], small)
    grad_vectors = small[:vector_rows]
    grad_bias = small[vector_rows:small_rows].reshape(-1)
    change, first, second = adam_step(vectors, grad_vectors, moment_vectors, second_vectors, 0.0)
    new_vectors = (grad_vectors, change, first, second)
    change, first, second = adam_step(
        expand_bias, grad_bias, moment_expand_bias, second_expand_bias, 0.0
    )
    new_bias = (grad_bias, change, first, second)
    updated = (new_in, new_out, new_expand, new_contract, new_vectors, new_bias)
    return (
        block_output,
        input_grad,
        *[each[0] for each in updated],
        *[each[1] for each in updated],
        *[array for each in updated for array in each[2:]],
        grad_vectors[7],
    )


def solution(mesh):
    tokens = P("tensor", "fsdp", None)
    into = P("fsdp", None, "tensor")
    wide = P("fsdp", "tensor")
    tall = P("tensor", "fsdp")
    row = P(None, "fsdp")
    line = P("fsdp")
    params = (into, tall, wide, tall, row, line)
    moments = (into, into, tall, tall, wide, wide, tall, tall, row, row, line, line)
    return jax.shard_map(
        body,
        mesh=mesh,
        in_specs=(tokens, row, tokens) + params + moments,
        out_specs=(tokens, tokens) + params + params + moments + (line,),
        check_vma=False,
    )
```
